128 devices in a mesh: seq: 8 (over y, core), chan: 16 (over z, x).
Axes of the slice: x: 4, y: 4, z: 4, core: 2. Of those that a mesh axis runs over, the one named last changes fastest.
Arguments:
- hidden: bfloat16 [1024, 4096], P('seq', 'chan'), may hold values from -6 to 6
- gate_in: bfloat16 [1024, 8192], P('seq', 'chan'), may hold values from -6 to 6
- out_grad: bfloat16 [1024, 8192], P('seq', 'chan'), may hold values from -6 to 6
- w_in: bfloat16 [4096, 8192], P('seq', 'chan'), may hold values from -0.125 to 0.125
- conv_w: float32 [4, 8192], P(None, 'chan'), may hold values from -2.5 to 2.5
- conv_b: float32 [8192], P('chan'), may hold values from -0.5 to 0.5
- w_delta_in: bfloat16 [256, 8192], P(None, 'chan'), may hold values from -0.0625 to 0.0625
- w_bc: bfloat16 [32, 8192], P(None, 'chan'), may hold values from -0.125 to 0.125
- w_dt: bfloat16 [256, 8192], P(None, 'chan'), may hold values from -0.375 to 0.375
- dt_bias: float32 [8192], P('chan'), may hold values from -7.5 to -2.5
- a_log: float32 [16, 8192], P(None, 'chan'), may hold values from -2.31 to 1.39
- skip_d: float32 [8192], P('chan'), may hold values from 0.1 to 1
Outputs:
- hidden_grad: bfloat16 [1024, 4096], P('seq', 'chan')
- gate_grad: bfloat16 [1024, 8192], P('seq', 'chan')
- w_in_grad: float32 [4096, 8192], P('seq', 'chan')
- w_delta_in_grad: float32 [256, 8192], P(None, 'chan')
- w_bc_grad: float32 [32, 8192], P(None, 'chan')
- w_dt_grad: float32 [256, 8192], P(None, 'chan')
- a_log_grad: float32 [16, 8192], P(None, 'chan')
The draws below stay inside these ranges and needn't reach their ends.
All inputs are finite; a program needn't handle non-finite values.
Results may differ from the reference program's by a relative error of at most 0.035.
Values may be sent and summed in bfloat16 or wider, within the bound.
A program may use at most 64 MiB of HBM per device.

```python
import math
import jax
import jax.numpy as jnp
from jax import lax

D = 4096
DI = 8192
N = 16
R = 256
KC = 4
TOK_DEV = 128
BLK = 64
TOKENS = 1024


def slow_marks(key):
    return jax.random.randint(key, (DI,), 0, 10)


def draw_dt_bias(key, part):
    marks = slow_marks(key)
    key = jax.random.fold_in(key, 3)
    share = 5
    slow_value = jax.random.uniform(key, (DI,), jnp.float32, -7.5, -6.5)
    fast_value = jax.random.uniform(jax.random.fold_in(key, 1), (DI,), jnp.float32, -4.0, -2.5)
    return jnp.where(marks < share, slow_value, fast_value)


def draw_a_log(key, part):
    marks = slow_marks(key)
    key = jax.random.fold_in(key, 7)
    share = 5
    slow_value = jax.random.uniform(key, (N, DI), jnp.float32, math.log(0.1), math.log(0.6))
    fast_value = jax.random.uniform(jax.random.fold_in(key, 1), (N, DI), jnp.float32, math.log(0.5), math.log(4.0))
    return jnp.where((marks < share)[None, :], slow_value, fast_value)


def strengthened(array, own_key, source, target, blocks, factor):
    owner, partner = [(jnp.arange(array.shape[position]) // (array.shape[position] // blocks)).reshape([-1 if axis == position else 1 for axis in range(array.ndim)]) for position in (source, target)]
    chosen = jax.random.permutation(own_key, blocks)[partner]
    strong = (owner == chosen) | (owner == (partner + blocks // 2) % blocks)
    return jnp.where(strong, factor * array, array)


def block_levels(rng, shape, split, low, top_value):
    gain, own = 1.0, jax.random.fold_in(rng, 6)
    for axis_at, parts in split:
        draws = jnp.exp(jax.random.uniform(jax.random.fold_in(own, axis_at), (parts,), jnp.float32, low / len(split), top_value / len(split)))
        gain = gain * jnp.repeat(draws, shape[axis_at] // parts).reshape([-1 if axis == axis_at else 1 for axis in range(len(shape))])
    return gain


def noise(stream_key, extent, spread, reach, shards=(), dtype=jnp.bfloat16):
    array = spread * jax.random.normal(stream_key, extent, jnp.float32)
    if shards:
        array = array * block_levels(stream_key, extent, shards, -0.22, 0.18)
    return jnp.clip(array, -reach, reach).astype(dtype)


def heavy_noise(stream_key, extent, scale, most, cuts, heavy, kind=jnp.bfloat16):
    result = scale * jax.random.normal(stream_key, extent, jnp.float32)
    if cuts:
        result = result * block_levels(stream_key, extent, cuts, -0.22, 0.18)
    return jnp.clip(strengthened(result, jax.random.fold_in(stream_key, 3), *heavy), -most, most).astype(kind)


def setup_inputs(seed: int = 0) -> dict:
    streams_of = jax.random.split(jax.random.key(seed), 13)
    return {
        "hidden": heavy_noise(streams_of[0], (TOKENS, D), 1.0, 6.0, ((0, 8), (1, 16)), (0, 1, 16, 2.0)),
        "gate_in": noise(streams_of[1], (TOKENS, DI), 1.0, 6.0, ((0, 8), (1, 16))),
        "out_grad": noise(streams_of[2], (TOKENS, DI), 1.0, 6.0, ((0, 8), (1, 16))),
        "w_in": heavy_noise(streams_of[3], (D, DI), D ** -0.5, 0.125, ((0, 8), (1, 16)), (1, 0, 16, 2.0)),
        "conv_w": noise(streams_of[4], (KC, DI), 0.5, 2.5, ((1, 16),), jnp.float32),
        "conv_b": jnp.clip(jax.random.uniform(streams_of[5], (DI,), jnp.float32, -0.5, 0.5) * block_levels(streams_of[5], (DI,), ((0, 16),), -0.4, 0.0), -0.5, 0.5),
        "w_delta_in": noise(streams_of[6], (R, DI), DI ** -0.5, 0.0625, ((1, 16),)),
        "w_bc": noise(streams_of[7], (2 * N, DI), (DI // 4) ** -0.5, 0.125, ((1, 16),)),
        "w_dt": noise(streams_of[8], (R, DI), R ** -0.5, 0.375, ((1, 16),)),
        "dt_bias": draw_dt_bias(jax.random.fold_in(streams_of[12], 71), 0),
        "a_log": draw_a_log(jax.random.fold_in(streams_of[12], 71), 0),
        "skip_d": jnp.clip(jnp.exp(math.log(1.0) - 2.3025851 * jax.random.uniform(streams_of[11], (DI,), jnp.float32) ** block_levels(streams_of[11], (DI,), ((0, 16),), -0.2, 0.2)), 0.1, 1.0),
    }


def silu_slope(values):
    sig = jax.nn.sigmoid(values)
    return sig * (1.0 + values * (1.0 - sig))

def local_scan(u_float, delta, b_in, c_in, a_matrix, state_in, block_len):
    tokens, chans = u_float.shape
    states = a_matrix.shape[0]
    blocks = tokens // block_len

    def token_step(state, row):
        u_row, d_row, b_row, c_row = row
        state = jnp.exp(d_row[None, :] * a_matrix) * state + (d_row * u_row)[None, :] * b_row[:, None]
        return (state, lax.optimization_barrier(jnp.sum(c_row[:, None] * state, 0)))

    def step(carried, pieces):
        return lax.scan(token_step, carried, pieces, unroll=8)
    pieces = (u_float.reshape(blocks, block_len, chans), delta.reshape(blocks, block_len, chans), b_in.reshape(blocks, block_len, states), c_in.reshape(blocks, block_len, states))
    final_state, outputs = lax.scan(jax.checkpoint(step), state_in, pieces)
    return (outputs.reshape(tokens, chans), final_state)

def contract_last(left, right):
    return lax.dot_general(left, right, (((1,), (1,)), ((), ())), preferred_element_type=jnp.float32)

def contract_first(left, right):
    return lax.dot_general(left, right, (((0,), (0,)), ((), ())), preferred_element_type=jnp.float32)

def reference(hidden, gate_in, out_grad, w_in, conv_w, conv_b, w_delta_in, w_bc, w_dt, dt_bias, a_log, skip_d):
    kernel_len = conv_w.shape[0]
    window_tokens = hidden.shape[0]
    x_rounded = jnp.dot(hidden, w_in, preferred_element_type=jnp.float32).astype(jnp.bfloat16)
    padded = jnp.concatenate([jnp.zeros((kernel_len - 1, DI), jnp.float32), x_rounded.astype(jnp.float32)], 0)
    conv_pre = jnp.zeros((window_tokens, DI), jnp.float32) + conv_b
    for k in range(kernel_len):
        conv_pre = conv_pre + conv_w[k] * padded[k:k + window_tokens]
    u_rounded = jax.nn.silu(conv_pre).astype(jnp.bfloat16)
    dt_low = contract_last(u_rounded, w_delta_in).astype(jnp.bfloat16)
    bc_full = contract_last(u_rounded, w_bc)
    b_in = bc_full[:, :N]
    c_in = bc_full[:, N:]
    pre_delta = jnp.dot(dt_low, w_dt, preferred_element_type=jnp.float32) + dt_bias
    delta = jax.nn.softplus(pre_delta)
    a_matrix = -jnp.exp(a_log)
    u_float = u_rounded.astype(jnp.float32)
    start_state = jnp.zeros((N, DI), jnp.float32)

    def run(u_value, d_value, b_value, c_value, a_value):
        return local_scan(u_value, d_value, b_value, c_value, a_value, start_state, BLK)[0]
    scan_out, backward = jax.vjp(run, u_float, delta, b_in, c_in, a_matrix)
    y_out = scan_out + skip_d * u_float
    gate_float = gate_in.astype(jnp.float32)
    grad_float = out_grad.astype(jnp.float32)
    gate_grad = (grad_float * y_out * silu_slope(gate_float)).astype(jnp.bfloat16)
    y_adj = grad_float * jax.nn.silu(gate_float)
    u_scan_adj, delta_adj, b_adj, c_adj, a_adj = backward(y_adj)
    pre_adj = (delta_adj * jax.nn.sigmoid(pre_delta)).astype(jnp.bfloat16)
    low_adj = contract_last(pre_adj, w_dt).astype(jnp.bfloat16)
    bc_adj = jnp.concatenate([b_adj, c_adj], 1).astype(jnp.bfloat16)
    u_adj = u_scan_adj + skip_d * y_adj + jnp.dot(low_adj, w_delta_in, preferred_element_type=jnp.float32) + jnp.dot(bc_adj, w_bc, preferred_element_type=jnp.float32)
    conv_adj = u_adj * silu_slope(conv_pre)
    padded_back = jnp.concatenate([conv_adj, jnp.zeros((kernel_len - 1, DI), jnp.float32)], 0)
    x_adj = jnp.zeros((window_tokens, DI), jnp.float32)
    for k in range(kernel_len):
        x_adj = x_adj + conv_w[k] * padded_back[kernel_len - 1 - k:kernel_len - 1 - k + window_tokens]
    x_adj = x_adj.astype(jnp.bfloat16)
    hidden_grad = contract_last(x_adj, w_in).astype(jnp.bfloat16)
    grad_scale = 1.0 / jnp.sqrt(jnp.float32(window_tokens))
    w_in_grad = jnp.zeros((D, DI), jnp.float32)
    for blk in range(window_tokens // TOK_DEV):
        rows_h = hidden[blk * TOK_DEV:(blk + 1) * TOK_DEV]
        rows_x = x_adj[blk * TOK_DEV:(blk + 1) * TOK_DEV]
        w_in_grad = w_in_grad + contract_first(rows_h, rows_x).astype(jnp.bfloat16).astype(jnp.float32)
    w_in_grad = w_in_grad * grad_scale
    w_delta_in_grad = contract_first(low_adj, u_rounded) * grad_scale
    w_bc_grad = contract_first(bc_adj, u_rounded) * grad_scale
    w_dt_grad = contract_first(dt_low, pre_adj) * grad_scale
    a_log_grad = a_adj * a_matrix * grad_scale
    return (hidden_grad, gate_grad, w_in_grad, w_delta_in_grad, w_bc_grad, w_dt_grad, a_log_grad)
```

```python
import functools
import math
import types

import jax
import jax.numpy as jnp
from jax import lax
from jax.experimental import pallas as pl
from jax.experimental.pallas import tpu as pltpu
from jax.sharding import PartitionSpec as P

MESH = pl.DeviceIdType.MESH


class Names:
    def __getattr__(self, name):
        return name


b = Names()
F32, BF16 = jnp.float32, jnp.bfloat16
CH = 16
LANES = 128
HALO = 16
HEAD = 8


def contract_last(left, right):
    return lax.dot_general(left, right, (((1,), (1,)), ((), ())), preferred_element_type=F32)


def contract_first(left, right):
    return lax.dot_general(left, right, (((0,), (0,)), ((), ())), preferred_element_type=F32)


def dot(left, right):
    return jnp.dot(left, right, preferred_element_type=F32)


def silu_slope(values):
    sig = jax.nn.sigmoid(values)
    return sig * (1.0 + values * (1.0 - sig))


def softplus(v):
    return jnp.maximum(v, 0.0) + jnp.log1p(jnp.exp(-jnp.abs(v)))


def rcopy(src, dst, send, recv, seq, chan):
    return pltpu.make_async_remote_copy(
        src_ref=src,
        dst_ref=dst,
        send_sem=send,
        recv_sem=recv,
        device_id=dict(seq=seq, chan=chan),
        device_id_type=MESH,
    )


def ring(r, group):
    if group == b.seq:
        return r.s, r.nS, lambda j: (j, r.c)
    return r.c, r.nC, lambda j: (r.s, j)


def peers(r, group):
    me, n, dev = ring(r, group)
    for i in range(1, n):
        j = lax.rem(me + i, n)
        yield i, j, dev(j)


def scatter_start(r, group, src, dst, key):
    me = ring(r, group)[0]
    for i, j, dev in peers(r, group):
        rcopy(src.at[j], dst.at[me], r.sems[key + "_s"].at[i], r.sems[key + "_r"].at[me], *dev).start()


def gather_start(r, group, buf, key):
    me = ring(r, group)[0]
    for i, j, dev in peers(r, group):
        rcopy(buf.at[me], buf.at[me], r.sems[key + "_s"].at[i], r.sems[key + "_r"].at[me], *dev).start()


def recv_wait(r, group, buf, key):
    for i, j, dev in peers(r, group):
        rcopy(buf.at[j], buf.at[j], r.sems[key + "_s"].at[i], r.sems[key + "_r"].at[j], *dev).wait_recv()


def send_wait(r, group, buf, key):
    for i, j, dev in peers(r, group):
        rcopy(buf.at[j], buf.at[j], r.sems[key + "_s"].at[i], r.sems[key + "_r"].at[j], *dev).wait_send()


def scatter_sum(r, group, src, dst, key):
    me = ring(r, group)[0]
    total = src[me].astype(F32)
    recv_wait(r, group, dst, key)
    for i, j, dev in peers(r, group):
        total = total + dst[j].astype(F32)
    return total


def greet(r, groups):
    barrier = pltpu.get_barrier_semaphore()
    count = 0

    def tell(seq, chan):
        pl.semaphore_signal(barrier, inc=1, device_id=dict(seq=seq, chan=chan), device_id_type=MESH)

    for group in groups:
        if group in (b.seq, b.chan):
            for i, j, dev in peers(r, group):
                tell(*dev)
                count += 1
        elif group == b.pair:
            tell(r.y * 2 + 1 - r.k, r.c)
            count += 1
        elif group == b.line:
            for i in range(1, r.nY):
                tell(lax.rem(r.y + i, r.nY) * 2 + r.k, r.c)
                count += 1
        elif group == b.next:
            pl.when(r.s < r.nS - 1)(lambda: tell(r.s + 1, r.c))
            pl.when(r.s > 0)(lambda: tell(r.s - 1, r.c))
        elif group == b.cross:
            for i in range(r.nC):
                c2 = lax.rem(r.c + i, r.nC)
                if i == 0:
                    pl.when(r.y != r.z)(lambda c2=c2: tell(r.z * 2 + r.k, c2))
                else:
                    tell(r.z * 2 + r.k, c2)
            for i in range(r.nY):
                for j in range(r.nX):
                    y2, x2 = lax.rem(r.y + i, r.nY), lax.rem(r.x + j, r.nX)
                    if i == 0 and j == 0:
                        pl.when(r.y != r.z)(lambda y2=y2, x2=x2: tell(y2 * 2 + r.k, r.y * r.nX + x2))
                    else:
                        tell(y2 * 2 + r.k, r.y * r.nX + x2)
            count += 2 * (r.nC - 1)
    if b.next in groups:
        last = r.nS - 1
        count = count + lax.div(last - r.s + last - 1, last) + lax.div(r.s + last - 1, last)
    if b.cross in groups:
        apart = (r.y - r.z) * (r.y - r.z)
        count = count + 2 * lax.div(apart + r.nY * r.nY - 1, r.nY * r.nY)
    pl.semaphore_wait(barrier, count)


def hidden_copy(r, i):
    slot = r.x * r.nY + r.y
    return rcopy(
        r.hidden,
        r.hg.at[slot],
        r.sems[b.hid_s].at[i],
        r.sems[b.hid_r].at[slot],
        r.z * 2 + r.k,
        lax.rem(r.c + i, r.nC),
    )


def pair_copy(r, src, dst, key):
    return rcopy(src, dst, r.sems[key + "_s"].at[0], r.sems[key + "_r"].at[0], r.y * 2 + 1 - r.k, r.c)


def line_copy(r, i, src, dst, key, slot):
    return rcopy(
        src, dst, r.sems[key + "_s"].at[i], r.sems[key + "_r"].at[slot], lax.rem(r.y + i, r.nY) * 2 + r.k, r.c
    )


def project(r):
    slot = r.x * r.nY + r.y
    half = r.nX // 2
    own_w = pltpu.make_async_copy(r.w_in, r.wp.at[pl.ds(r.k * half, half)], r.sems[b.loc].at[0])
    own_w.start()
    pair_copy(r, r.w_in, r.wp.at[pl.ds(r.k * half, half)], b.wp).start()
    for i in range(r.nC):
        if i == 0:
            pl.when(r.y != r.z)(lambda: hidden_copy(r, 0).start())
        else:
            hidden_copy(r, i).start()

    @pl.when(r.y == r.z)
    def _():
        r.hg[slot] = r.hidden[...]

    own_w.wait()
    pair_copy(r, r.w_in, r.wp.at[pl.ds((1 - r.k) * half, half)], b.wp).wait_recv()

    def arrive(slot2):
        rcopy(
            r.hidden, r.hg.at[slot2], r.sems[b.hid_s].at[0], r.sems[b.hid_r].at[slot2], r.z * 2 + r.k, r.c
        ).wait_recv()

    for i in range(1, r.nY + 1):
        y2 = lax.rem(r.y + i, r.nY)
        total = None
        for j in range(r.nX):
            x2 = lax.rem(r.x + j, r.nX)
            slot2 = x2 * r.nY + y2
            if i == r.nY and j == 0:
                pl.when(r.y != r.z)(lambda slot2=slot2: arrive(slot2))
            else:
                arrive(slot2)
            term = dot(r.hg[slot2], r.wp[x2])
            total = term if total is None else total + term
        if i < r.nY:
            r.xs[i - 1] = total.astype(BF16)
            line_copy(r, i, r.xs.at[i - 1], r.xr.at[r.y], b.xr, r.y).start()
        else:
            own = total
    for i in range(1, r.nY):
        y2 = lax.rem(r.y + i, r.nY)
        line_copy(r, i, r.xs.at[i - 1], r.xr.at[y2], b.xr, y2).wait_recv()
        own = own + r.xr[y2].astype(F32)
    x_rounded = own.astype(BF16)
    r.tail_s[...] = x_rounded[r.T - HALO :]

    def tail_copy(to):
        return rcopy(r.tail_s, r.tail_r, r.sems[b.tail_s].at[0], r.sems[b.tail_r].at[0], to, r.c)

    pl.when(r.s < r.nS - 1)(lambda: tail_copy(r.s + 1).start())
    r.xpad[pl.ds(HALO, r.T), :] = x_rounded.astype(F32)

    @pl.when(r.s == 0)
    def _():
        r.xpad[pl.ds(0, HALO), :] = jnp.zeros((HALO, r.C), F32)

    @pl.when(r.s > 0)
    def _():
        tail_copy(r.s - 1).wait_recv()
        r.xpad[pl.ds(0, HALO), :] = r.tail_r[...].astype(F32)

    conv = jnp.zeros((r.T, r.C), F32) + r.conv_b[...]
    for k in range(r.KC):
        conv = conv + r.conv_w[k : k + 1, :] * r.xpad[pl.ds(HALO - r.KC + 1 + k, r.T), :]
    r.conv_pre[...] = conv
    u = (conv * jax.nn.sigmoid(conv)).astype(BF16)
    r.u[...] = u
    r.part[:, :, pl.ds(0, r.R)] = contract_last(u, r.w_delta_in[...]).reshape(r.nC, r.RP, r.R)
    r.part[:, :, pl.ds(r.R, LANES)] = jnp.zeros((r.nC, r.RP, LANES), F32)
    r.part[:, :, pl.ds(r.R, 2 * r.N)] = contract_last(u, r.w_bc[...]).reshape(r.nC, r.RP, 2 * r.N)
    scatter_start(r, b.chan, r.part, r.part_r, b.p1)
    r.part_a[r.c] = scatter_sum(r, b.chan, r.part, r.part_r, b.p1)
    gather_start(r, b.chan, r.part_a, b.p2)
    recv_wait(r, b.chan, r.part_a, b.p2)
    full = r.part_a[...].reshape(r.T, r.R + LANES)
    r.low[...] = full[:, : r.R].astype(BF16)
    r.bcw[...] = full[:, r.R :]


def project_end(r):
    half = r.nX // 2
    for i in range(r.nC):
        if i == 0:
            pl.when(r.y != r.z)(lambda: hidden_copy(r, 0).wait_send())
        else:
            hidden_copy(r, i).wait_send()
    pair_copy(r, r.w_in, r.wp.at[pl.ds(r.k * half, half)], b.wp).wait_send()
    for i in range(1, r.nY):
        line_copy(r, i, r.xs.at[i - 1], r.xr.at[r.y], b.xr, r.y).wait_send()
    pl.when(r.s < r.nS - 1)(
        lambda: rcopy(
            r.tail_s, r.tail_r, r.sems[b.tail_s].at[0], r.sems[b.tail_r].at[0], r.s + 1, r.c
        ).wait_send()
    )
    send_wait(r, b.chan, r.part, b.p1)
    send_wait(r, b.chan, r.part_a, b.p2)


def wide(r, b):
    return jnp.concatenate([b] * (r.C // LANES), axis=1) if r.C > LANES else b


def block_mask(r, rows):
    row = lax.broadcasted_iota(jnp.int32, (rows, CH * r.N), 0)
    col = lax.broadcasted_iota(jnp.int32, (rows, CH * r.N), 1)
    return jnp.where(lax.rem(row, CH) == lax.div(col, r.N), 1.0, 0.0).astype(F32)


def pick(r):
    row = lax.broadcasted_iota(jnp.int32, (r.N, CH * r.N), 0)
    col = lax.broadcasted_iota(jnp.int32, (r.N, CH * r.N), 1)
    return jnp.where(lax.rem(col, r.N) == row, 1.0, 0.0).astype(F32)


def prepare(r):
    pre = dot(r.low[...], r.w_dt[...]) + r.dt_bias[...]
    r.pre[...] = pre
    delta = softplus(pre)
    r.delta[...] = delta
    u = r.u[...].astype(F32)
    r.du[...] = delta * u
    gate = r.gate_in[...].astype(F32)
    r.g[...] = r.out_grad[...].astype(F32) * (gate * jax.nn.sigmoid(gate))
    r.am[...] = -jnp.exp(r.a_log[...])
    turned = r.bcw[...].T
    for t in range(r.T):
        r.bx[t] = jnp.broadcast_to(turned[0 : r.N, t : t + 1], (r.N, LANES))
        r.cx[t] = jnp.broadcast_to(turned[r.N : 2 * r.N, t : t + 1], (r.N, LANES))
    r.sd[...] = jnp.sum(delta, 0, keepdims=True)


def forward(r, init, full):
    a_mat = r.am[...]
    if full:
        mask = block_mask(r, CH)
        r.hh[pl.ds(0, r.N), :] = init

    def chunk(j, h):
        base = pl.multiple_of(j * CH, CH)
        d = r.delta[pl.ds(base, CH), :]
        du = r.du[pl.ds(base, CH), :]
        kept = []
        for t in range(CH):
            at = pl.multiple_of((base + t) * r.N, r.N)
            a = jnp.exp(d[t : t + 1, :] * a_mat)
            r.aa[pl.ds(at, r.N), :] = a
            h = a * h + du[t : t + 1, :] * wide(r, r.bx[base + t])
            if full:
                r.hh[pl.ds(at + r.N, r.N), :] = h
                kept.append(h.astype(BF16))
        if full:
            rows = jnp.concatenate(kept, 0)
            r.y_scan[pl.ds(base, CH), :] = dot(r.cd[pl.ds(base, CH), :], rows)
            r.cm[pl.ds(base, CH), :] = mask * contract_last(r.g[pl.ds(base, CH), :].astype(BF16), rows)
        return h

    return lax.fori_loop(0, r.T // CH, chunk, init)


def backward(r, init, full):
    a_mat = r.am[...]
    mask = block_mask(r, CH)
    chunks = r.T // CH

    def chunk(i, carry):
        base = pl.multiple_of((chunks - 1 - i) * CH, CH)
        kap, acc = carry
        d = r.delta[pl.ds(base, CH), :]
        g = r.g[pl.ds(base, CH), :]
        lams, qas = [None] * CH, [None] * CH
        for t in reversed(range(CH)):
            at = pl.multiple_of((base + t) * r.N, r.N)
            lam = kap + wide(r, r.cx[base + t]) * g[t : t + 1, :]
            kap = r.aa[pl.ds(at, r.N), :] * lam
            if full:
                q = kap * r.hh[pl.ds(at, r.N), :]
                acc = acc + q * d[t : t + 1, :]
                qas[t] = (q * a_mat).astype(BF16)
                lams[t] = lam.astype(BF16)
        if full:
            lam_rows = jnp.concatenate(lams, 0)
            du = r.du[pl.ds(base, CH), :]
            r.s1[pl.ds(base, CH), :] = dot(r.bd[pl.ds(base, CH), :], lam_rows)
            r.s2[pl.ds(base, CH), :] = dot(mask.astype(BF16), jnp.concatenate(qas, 0))
            r.bm[pl.ds(base, CH), :] = mask * contract_last(du.astype(BF16), lam_rows)
        return kap, acc

    return lax.fori_loop(0, chunks, chunk, (init, jnp.zeros_like(init)))


def scan_free(r):
    zero = jnp.zeros((r.N, r.C), F32)
    r.ef[0] = forward(r, zero, False).astype(BF16)
    r.ef[1] = backward(r, zero, False)[0].astype(BF16)


def scan_exchange(r):
    r.st_r[r.s] = jnp.zeros((r.N, r.C), BF16)
    r.sd_r[r.s] = jnp.zeros((1, r.C), F32)
    copies = []
    for i, j, dev in peers(r, b.seq):
        copies.append(
            rcopy(
                r.ef.at[lax.div(r.s + i, r.nS)], r.st_r.at[r.s], r.sems[b.st_s].at[i], r.sems[b.st_r].at[r.s], *dev
            )
        )
        copies.append(rcopy(r.sd, r.sd_r.at[r.s], r.sems[b.sd_s].at[i], r.sems[b.sd_r].at[r.s], *dev))
    for copy in copies:
        copy.start()
    recv_wait(r, b.seq, r.sd_r, b.sd)
    recv_wait(r, b.seq, r.st_r, b.st)
    a_mat = r.am[...]
    state = jnp.zeros((r.N, r.C), F32)
    for j in range(r.nS - 1):
        new = jnp.exp(a_mat * r.sd_r[j]) * state + r.st_r[j].astype(F32)
        state = jnp.where(j < r.s, new, state)
    r.h_in[...] = state
    adj = jnp.zeros((r.N, r.C), F32)
    for j in range(r.nS - 1, 0, -1):
        new = jnp.exp(a_mat * r.sd_r[j]) * adj + r.st_r[j].astype(F32)
        adj = jnp.where(j > r.s, new, adj)
    r.l_in[...] = adj
    for copy in copies:
        copy.wait_send()


def scan_full(r):
    picked = pick(r)
    tall = block_mask(r, r.T)
    r.bd[...] = (tall * dot(r.bcw[:, pl.ds(0, r.N)], picked)).astype(BF16)
    r.cd[...] = (tall * dot(r.bcw[:, pl.ds(r.N, r.N)], picked)).astype(BF16)
    forward(r, r.h_in[...], True)
    a_adj = backward(r, r.l_in[...], True)[1]
    r.alog_p[...] = a_adj * r.am[...]
    s1 = r.s1[...]
    u = r.u[...].astype(F32)
    skip = r.skip_d[...]
    pre_adj = ((u * s1 + r.s2[...]) * jax.nn.sigmoid(r.pre[...])).astype(BF16)
    r.uu[...] = r.delta[...] * s1 + skip * r.g[...]
    exact = lax.Precision.HIGHEST
    nt = (((1,), (1,)), ((), ()))
    b_adj = lax.dot_general(r.bm[...], picked, nt, precision=exact, preferred_element_type=F32)
    c_adj = lax.dot_general(r.cm[...], picked, nt, precision=exact, preferred_element_type=F32)
    r.part2[:, :, pl.ds(0, r.R)] = contract_last(pre_adj, r.w_dt[...]).reshape(r.nC, r.RP, r.R)
    r.part2[:, :, pl.ds(r.R, LANES)] = jnp.zeros((r.nC, r.RP, LANES), F32)
    r.part2[:, :, pl.ds(r.R, r.N)] = b_adj.reshape(r.nC, r.RP, r.N)
    r.part2[:, :, pl.ds(r.R + r.N, r.N)] = c_adj.reshape(r.nC, r.RP, r.N)
    r.dt_p[...] = contract_first(r.low[...], pre_adj).astype(BF16).reshape(r.nS, r.R // r.nS, r.C)
    gate = r.gate_in[...].astype(F32)
    y_out = r.y_scan[...] + skip * u
    r.gate_grad[...] = (r.out_grad[...].astype(F32) * y_out * silu_slope(gate)).astype(BF16)


def grad_copy(r, i, j):
    y2, x2 = lax.rem(r.y + i, r.nY), lax.rem(r.x + j, r.nX)
    n = i * r.nX + j
    return rcopy(
        r.hs.at[n], r.hr.at[r.c], r.sems[b.hg_s].at[n], r.sems[b.hg_r].at[r.c], y2 * 2 + r.k, r.y * r.nX + x2
    )


def gradients(r):
    scale = 1.0 / math.sqrt(r.T * r.nS)
    half = r.nX // 2
    nb, na = 2 * r.N // r.nS, r.N // r.nS
    scatter_start(r, b.chan, r.part2, r.part2_r, b.p3)
    scatter_start(r, b.seq, r.dt_p, r.dt_r, b.d1)
    r.part2_a[r.c] = scatter_sum(r, b.chan, r.part2, r.part2_r, b.p3)
    gather_start(r, b.chan, r.part2_a, b.p4)
    r.dt_a[r.s] = scatter_sum(r, b.seq, r.dt_p, r.dt_r, b.d1).astype(BF16)
    gather_start(r, b.seq, r.dt_a, b.d2)
    recv_wait(r, b.chan, r.part2_a, b.p4)
    full = r.part2_a[...].reshape(r.T, r.R + LANES)
    low_adj = full[:, : r.R].astype(BF16)
    bc_adj = full[:, r.R : r.R + 2 * r.N].astype(BF16)
    u_adj = r.uu[...] + dot(low_adj, r.w_delta_in[...]) + dot(bc_adj, r.w_bc[...])
    conv_adj = u_adj * silu_slope(r.conv_pre[...])
    r.cpad[pl.ds(0, r.T), :] = conv_adj

    def head_copy(to):
        return rcopy(
            r.cpad.at[pl.ds(0, HEAD)],
            r.cpad.at[pl.ds(r.T, HEAD)],
            r.sems[b.head_s].at[0],
            r.sems[b.head_r].at[0],
            to,
            r.c,
        )

    pl.when(r.s > 0)(lambda: head_copy(r.s - 1).start())

    @pl.when(r.s == r.nS - 1)
    def _():
        r.cpad[pl.ds(r.T, HEAD), :] = jnp.zeros((HEAD, r.C), F32)

    u = r.u[...]
    r.di_p[...] = contract_first(low_adj, u).astype(BF16).reshape(r.nS, r.R // r.nS, r.C)
    bc_term = contract_first(bc_adj, u)
    alog = r.alog_p[...]
    r.mi_p[...] = jnp.zeros_like(r.mi_p)
    for j in range(r.nS):
        r.mi_p[j, pl.ds(0, nb), :] = bc_term[j * nb : (j + 1) * nb]
        r.mi_p[j, pl.ds(nb, na), :] = alog[j * na : (j + 1) * na]

    pl.when(r.s < r.nS - 1)(lambda: head_copy(r.s + 1).wait_recv())
    x_adj = jnp.zeros((r.T, r.C), F32)
    for k in range(r.KC):
        x_adj = x_adj + r.conv_w[k : k + 1, :] * r.cpad[pl.ds(r.KC - 1 - k, r.T), :]
    r.xg[r.y] = x_adj.astype(BF16)
    for i in range(1, r.nY):
        line_copy(r, i, r.xg.at[r.y], r.xg.at[r.y], b.xg, r.y).start()
    scatter_start(r, b.seq, r.di_p, r.di_r, b.d3)
    scatter_start(r, b.seq, r.mi_p, r.mi_r, b.d5)

    for i in range(r.nY):
        y2 = lax.rem(r.y + i, r.nY)
        if i:
            line_copy(r, i, r.xg.at[y2], r.xg.at[y2], b.xg, y2).wait_recv()
        for j in range(r.nX):
            x2 = lax.rem(r.x + j, r.nX)
            n = i * r.nX + j
            r.hs[n] = contract_last(r.xg[y2], r.wp[x2]).astype(BF16)
            if n == 0:

                @pl.when(r.y == r.z)
                def _():
                    r.hr[r.c] = r.hs[0]

                pl.when(r.y != r.z)(lambda: grad_copy(r, 0, 0).start())
            else:
                grad_copy(r, i, j).start()

    x_all = r.xg[...].reshape(r.nY * r.T, r.C)

    def weight(x2):
        rows = r.hg[pl.ds(x2 * r.nY, r.nY)].reshape(r.nY * r.T, r.DH)
        return contract_first(rows, x_all)

    for j in range(half):
        r.ws[j] = weight((1 - r.k) * half + j).astype(BF16)
    pair_copy(r, r.ws, r.wr, b.wg).start()
    r.di_a[r.s] = scatter_sum(r, b.seq, r.di_p, r.di_r, b.d3).astype(BF16)
    gather_start(r, b.seq, r.di_a, b.d4)
    r.mi_a[r.s] = scatter_sum(r, b.seq, r.mi_p, r.mi_r, b.d5)
    gather_start(r, b.seq, r.mi_a, b.d6)
    for j in range(half):
        r.w_in_grad[j] = weight(r.k * half + j)
    pair_copy(r, r.ws, r.wr, b.wg).wait_recv()
    for j in range(half):
        r.w_in_grad[j] = (r.w_in_grad[j] + r.wr[j].astype(F32)) * scale

    recv_wait(r, b.seq, r.dt_a, b.d2)
    r.w_dt_grad[...] = r.dt_a[...].astype(F32).reshape(r.R, r.C) * scale
    total = None
    for j in range(r.nC):
        c2 = lax.rem(r.c + j, r.nC)
        wait = rcopy(
            r.hs.at[0], r.hr.at[c2], r.sems[b.hg_s].at[0], r.sems[b.hg_r].at[c2], r.z * 2 + r.k, c2
        )
        if j == 0:
            pl.when(r.y != r.z)(lambda wait=wait: wait.wait_recv())
        else:
            wait.wait_recv()
        term = r.hr[c2].astype(F32)
        total = term if total is None else total + term
    r.hidden_grad[...] = total.astype(BF16)
    recv_wait(r, b.seq, r.di_a, b.d4)
    r.w_delta_in_grad[...] = r.di_a[...].astype(F32).reshape(r.R, r.C) * scale
    recv_wait(r, b.seq, r.mi_a, b.d6)
    for j in range(r.nS):
        r.w_bc_grad[pl.ds(j * nb, nb), :] = r.mi_a[j, pl.ds(0, nb), :] * scale
        r.a_log_grad[pl.ds(j * na, na), :] = r.mi_a[j, pl.ds(nb, na), :] * scale

    send_wait(r, b.chan, r.part2, b.p3)
    send_wait(r, b.chan, r.part2_a, b.p4)
    for name, key in ((b.dt_p, b.d1), (b.dt_a, b.d2), (b.di_p, b.d3), (b.di_a, b.d4), (b.mi_p, b.d5), (b.mi_a, b.d6)):
        send_wait(r, b.seq, getattr(r, name), key)
    pl.when(r.s > 0)(lambda: head_copy(r.s - 1).wait_send())
    for i in range(1, r.nY):
        line_copy(r, i, r.xg.at[r.y], r.xg.at[r.y], b.xg, r.y).wait_send()
    for i in range(r.nY):
        for j in range(r.nX):
            if i == 0 and j == 0:
                pl.when(r.y != r.z)(lambda: grad_copy(r, 0, 0).wait_send())
            else:
                grad_copy(r, i, j).wait_send()
    pair_copy(r, r.ws, r.wr, b.wg).wait_send()


def tables(dim):
    d = types.SimpleNamespace(**dim)
    t, c, n, rows, q = d.T, d.C, d.N, d.R, d.R // d.nS
    small = -(-(3 * n // d.nS) // 8) * 8
    wide_row = rows + LANES
    buffers = dict(
        hg=((d.nC, t, d.DH), BF16),
        wp=((d.nX, d.DH, c), BF16),
        xs=((d.nY - 1, t, c), BF16),
        xr=((d.nY, t, c), BF16),
        tail_s=((HALO, c), BF16),
        tail_r=((HALO, c), BF16),
        xpad=((HALO + t, c), F32),
        conv_pre=((t, c), F32),
        u=((t, c), BF16),
        part=((d.nC, d.RP, wide_row), F32),
        part_r=((d.nC, d.RP, wide_row), F32),
        part_a=((d.nC, d.RP, wide_row), F32),
        low=((t, rows), BF16),
        bcw=((t, LANES), F32),
        pre=((t, c), F32),
        delta=((t, c), F32),
        du=((t, c), F32),
        g=((t, c), F32),
        am=((n, c), F32),
        bx=((t, n, LANES), F32),
        cx=((t, n, LANES), F32),
        sd=((1, c), F32),
        aa=((t * n, c), F32),
        hh=(((t + 1) * n, c), F32),
        ef=((2, n, c), BF16),
        st_r=((d.nS, n, c), BF16),
        sd_r=((d.nS, 1, c), F32),
        h_in=((n, c), F32),
        l_in=((n, c), F32),
        bd=((t, CH * n), BF16),
        cd=((t, CH * n), BF16),
        bm=((t, CH * n), F32),
        cm=((t, CH * n), F32),
        y_scan=((t, c), F32),
        s1=((t, c), F32),
        s2=((t, c), F32),
        uu=((t, c), F32),
        alog_p=((n, c), F32),
        part2=((d.nC, d.RP, wide_row), F32),
        part2_r=((d.nC, d.RP, wide_row), F32),
        part2_a=((d.nC, d.RP, wide_row), F32),
        dt_p=((d.nS, q, c), BF16),
        dt_r=((d.nS, q, c), BF16),
        dt_a=((d.nS, q, c), BF16),
        di_p=((d.nS, q, c), BF16),
        di_r=((d.nS, q, c), BF16),
        di_a=((d.nS, q, c), BF16),
        mi_p=((d.nS, small, c), F32),
        mi_r=((d.nS, small, c), F32),
        mi_a=((d.nS, small, c), F32),
        cpad=((t + HEAD, c), F32),
        xg=((d.nY, t, c), BF16),
        hs=((d.nC, t, d.DH), BF16),
        hr=((d.nC, t, d.DH), BF16),
        ws=((d.nX // 2, d.DH, c), BF16),
        wr=((d.nX // 2, d.DH, c), BF16),
        hidden_grad=((t, d.DH), BF16),
        gate_grad=((t, c), BF16),
        w_in_grad=((d.nX // 2, d.DH, c), F32),
        w_delta_in_grad=((rows, c), F32),
        w_bc_grad=((2 * n, c), F32),
        w_dt_grad=((rows, c), F32),
        a_log_grad=((n, c), F32),
    )
    sems = dict(
        loc=1,
        hid_s=d.nC,
        hid_r=d.nC,
        wp_s=1,
        wp_r=1,
        xr_s=d.nY,
        xr_r=d.nY,
        tail_s=1,
        tail_r=1,
        head_s=1,
        head_r=1,
        xg_s=d.nY,
        xg_r=d.nY,
        hg_s=d.nC,
        hg_r=d.nC,
        wg_s=1,
        wg_r=1,
    )
    for key, count in ((b.p1, d.nC), (b.p2, d.nC), (b.p3, d.nC), (b.p4, d.nC), (b.st, d.nS), (b.sd, d.nS)):
        sems[key + "_s"] = sems[key + "_r"] = count
    for key in (b.d1, b.d2, b.d3, b.d4, b.d5, b.d6):
        sems[key + "_s"] = sems[key + "_r"] = d.nS
    return buffers, sems


def run(dim, phases, groups, values, ins, outs, scratch, sem_names, number, cost):
    buffers, sem_sizes = tables(dim)

    def body(*refs):
        r = types.SimpleNamespace(**dim)
        for name, ref in zip(ins + outs + scratch, refs):
            setattr(r, name, ref)
        r.sems = dict(zip(sem_names, refs[len(ins) + len(outs) + len(scratch) :]))
        if groups:
            r.s, r.c = lax.axis_index(b.seq), lax.axis_index(b.chan)
            r.y, r.k = lax.div(r.s, 2), lax.rem(r.s, 2)
            r.z, r.x = lax.div(r.c, r.nX), lax.rem(r.c, r.nX)
            greet(r, groups)
        for phase in phases:
            phase(r)

    space = pl.BlockSpec(memory_space=pltpu.VMEM)
    extra = dict(collective_id=number, has_side_effects=True) if groups else {}
    results = pl.pallas_call(
        body,
        out_shape=[jax.ShapeDtypeStruct(*buffers[name]) for name in outs],
        in_specs=[space] * len(ins),
        out_specs=[space] * len(outs),
        scratch_shapes=[pltpu.VMEM(*buffers[name]) for name in scratch]
        + [pltpu.SemaphoreType.DMA((sem_sizes[name],)) for name in sem_names],
        compiler_params=pltpu.CompilerParams(vmem_limit_bytes=56 << 20, **extra),
        cost_estimate=pl.CostEstimate(flops=cost, bytes_accessed=4 << 20, transcendentals=0),
        name=phases[0].__name__,
    )(*[values[name] for name in ins])
    values.update(zip(outs, results))


ORDER = [b.hidden_grad, b.gate_grad, b.w_in_grad, b.w_delta_in_grad, b.w_bc_grad, b.w_dt_grad, b.a_log_grad]


def keys(*names):
    return [name + end for name in names for end in ("_s", "_r")]


def per_device(
    seq, chan, hidden, gate_in, out_grad, w_in, conv_w, conv_b, w_delta_in, w_bc, w_dt, dt_bias, a_log, skip_d
):
    lines = seq // 2
    dim = dict(
        nS=seq,
        nC=chan,
        nY=lines,
        nX=chan // lines,
        T=hidden.shape[0],
        DH=hidden.shape[1],
        C=w_in.shape[1],
        R=w_delta_in.shape[0],
        N=a_log.shape[0],
        KC=conv_w.shape[0],
        RP=hidden.shape[0] // chan,
    )
    v = dict(
        hidden=hidden,
        gate_in=gate_in,
        out_grad=out_grad,
        w_in=w_in.reshape(dim[b.nX] // 2, dim[b.DH], dim[b.C]),
        conv_w=conv_w,
        conv_b=conv_b[None],
        w_delta_in=w_delta_in,
        w_bc=w_bc,
        w_dt=w_dt,
        dt_bias=dt_bias[None],
        a_log=a_log,
        skip_d=skip_d[None],
    )
    go = functools.partial(run, dim)
    go(
        [project, project_end],
        [b.cross, b.pair, b.line, b.next, b.chan],
        v,
        [b.hidden, b.w_in, b.conv_w, b.conv_b, b.w_delta_in, b.w_bc],
        [b.hg, b.wp, b.conv_pre, b.u, b.low, b.bcw],
        [b.xs, b.xr, b.tail_s, b.tail_r, b.xpad, b.part, b.part_r, b.part_a],
        [b.loc] + keys(b.hid, b.wp, b.xr, b.tail, b.p1, b.p2),
        0,
        600_000_000,
    )
    go(
        [prepare, scan_free],
        [],
        v,
        [b.low, b.u, b.bcw, b.w_dt, b.dt_bias, b.a_log, b.gate_in, b.out_grad],
        [b.pre, b.delta, b.du, b.g, b.am, b.bx, b.cx, b.sd, b.ef],
        [b.aa],
        [],
        0,
        50_000_000,
    )
    go([scan_exchange], [b.seq], v, [b.ef, b.sd, b.am], [b.h_in, b.l_in], [b.st_r, b.sd_r], keys(b.st, b.sd), 1, 1_000_000)
    go(
        [scan_full],
        [],
        v,
        [b.low, b.u, b.bcw, b.w_dt, b.gate_in, b.out_grad, b.skip_d]
        + [b.pre, b.delta, b.du, b.g, b.am, b.bx, b.cx, b.h_in, b.l_in],
        [b.gate_grad, b.uu, b.alog_p, b.part2, b.dt_p],
        [b.aa, b.hh, b.bd, b.cd, b.bm, b.cm, b.y_scan, b.s1, b.s2],
        [],
        0,
        100_000_000,
    )
    go(
        [gradients],
        [b.cross, b.pair, b.line, b.next, b.chan, b.seq],
        v,
        [b.hg, b.wp, b.conv_pre, b.u, b.conv_w, b.w_delta_in, b.w_bc, b.uu, b.alog_p, b.part2, b.dt_p],
        [name for name in ORDER if name != b.gate_grad],
        [b.part2_r, b.part2_a, b.dt_r, b.dt_a, b.di_p, b.di_r, b.di_a, b.mi_p, b.mi_r, b.mi_a]
        + [b.cpad, b.xg, b.hs, b.hr, b.ws, b.wr],
        keys(b.head, b.xg, b.hg, b.wg, b.p3, b.p4, b.d1, b.d2, b.d3, b.d4, b.d5, b.d6),
        2,
        1_200_000_000,
    )
    v[b.w_in_grad] = v[b.w_in_grad].reshape(w_in.shape)
    return tuple(v[name] for name in ORDER)


def solution(mesh):
    placed = (
        P(b.seq, b.chan),
        P(b.seq, b.chan),
        P(b.seq, b.chan),
        P(b.seq, b.chan),
        P(None, b.chan),
        P(b.chan),
        P(None, b.chan),
        P(None, b.chan),
        P(None, b.chan),
        P(b.chan),
        P(None, b.chan),
        P(b.chan),
    )
    return jax.shard_map(
        functools.partial(per_device, mesh.shape[b.seq], mesh.shape[b.chan]),
        mesh=mesh,
        in_specs=placed,
        out_specs=(
            P(b.seq, b.chan),
            P(b.seq, b.chan),
            P(b.seq, b.chan),
            P(None, b.chan),
            P(None, b.chan),
            P(None, b.chan),
            P(None, b.chan),
        ),
        check_vma=False,
    )
```

```python
import functools
import math
import types

import jax
import jax.numpy as jnp
from jax import lax
from jax.experimental import pallas as pl
from jax.experimental.pallas import tpu as pltpu
from jax.sharding import PartitionSpec as P

MESH = pl.DeviceIdType.MESH


class Names:
    def __getattr__(self, name):
        return name


b = Names()
F32, BF16 = jnp.float32, jnp.bfloat16
CH = 16
LANES = 128
HALO = 16
HEAD = 8


def contract_last(left, right):
    return lax.dot_general(left, right, (((1,), (1,)), ((), ())), preferred_element_type=F32)


def contract_first(left, right):
    return lax.dot_general(left, right, (((0,), (0,)), ((), ())), preferred_element_type=F32)


def dot(left, right):
    return jnp.dot(left, right, preferred_element_type=F32)


def silu_slope(values):
    sig = jax.nn.sigmoid(values)
    return sig * (1.0 + values * (1.0 - sig))


def softplus(v):
    return jnp.maximum(v, 0.0) + jnp.log1p(jnp.exp(-jnp.abs(v)))


def rcopy(src, dst, send, recv, seq, chan):
    return pltpu.make_async_remote_copy(
        src_ref=src,
        dst_ref=dst,
        send_sem=send,
        recv_sem=recv,
        device_id=dict(seq=seq, chan=chan),
        device_id_type=MESH,
    )


def ring(r, group):
    if group == b.seq:
        return r.s, r.nS, lambda j: (j, r.c)
    return r.c, r.nC, lambda j: (r.s, j)


def peers(r, group):
    me, n, dev = ring(r, group)
    for i in range(1, n):
        j = lax.rem(me + i, n)
        yield i, j, dev(j)


def start(r, copy, when=None):
    r.sent.append((copy, when))
    if when is None:
        copy.start()
    else:
        pl.when(when)(copy.start)


def flush(r):
    for copy, when in r.sent:
        if when is None:
            copy.wait_send()
        else:
            pl.when(when)(copy.wait_send)
    r.sent.clear()


def scatter_start(r, group, src, dst, key):
    me = ring(r, group)[0]
    for i, j, dev in peers(r, group):
        start(r, rcopy(src.at[j], dst.at[me], r.sems[key + "_s"].at[i], r.sems[key + "_r"].at[me], *dev))


def gather_start(r, group, buf, key):
    me = ring(r, group)[0]
    for i, j, dev in peers(r, group):
        start(r, rcopy(buf.at[me], buf.at[me], r.sems[key + "_s"].at[i], r.sems[key + "_r"].at[me], *dev))


def recv_wait(r, group, buf, key):
    for i, j, dev in peers(r, group):
        rcopy(buf.at[j], buf.at[j], r.sems[key + "_s"].at[i], r.sems[key + "_r"].at[j], *dev).wait_recv()


def scatter_sum(r, group, src, dst, key):
    me = ring(r, group)[0]
    total = src[me].astype(F32)
    recv_wait(r, group, dst, key)
    for i, j, dev in peers(r, group):
        total = total + dst[j].astype(F32)
    return total


def pair_copy(r, src, dst, key):
    return rcopy(src, dst, r.sems[key + "_s"].at[0], r.sems[key + "_r"].at[0], r.y * 2 + 1 - r.k, r.c)


def line_copy(r, i, src, dst, key, slot, part=0):
    at = part * r.nY
    return rcopy(
        src,
        dst,
        r.sems[key + "_s"].at[at + i],
        r.sems[key + "_r"].at[at + slot],
        lax.rem(r.y + i, r.nY) * 2 + r.k,
        r.c,
    )


def plane_copy(r, i, along_x, src, dst, key, slot):
    at, seq = (0 if along_x else r.nX), r.s
    chan = r.z * r.nX + lax.rem(r.x + i, r.nX) if along_x else lax.rem(r.z + i, r.nY) * r.nX + r.x
    return rcopy(src, dst, r.sems[key + "_s"].at[at + i], r.sems[key + "_r"].at[at + slot], seq, chan)


def greet(r, groups):
    barrier = pltpu.get_barrier_semaphore()
    count = 0

    def tell(seq, chan):
        pl.semaphore_signal(barrier, inc=1, device_id=dict(seq=seq, chan=chan), device_id_type=MESH)

    for group in groups:
        if group in (b.seq, b.chan):
            for i, j, dev in peers(r, group):
                tell(*dev)
                count += 1
        elif group == b.cross:
            for i in range(r.nC):
                c2 = lax.rem(r.c + i, r.nC)
                if i == 0:
                    pl.when(r.y != r.z)(lambda c2=c2: tell(r.z * 2 + r.k, c2))
                else:
                    tell(r.z * 2 + r.k, c2)
            for i in range(r.nY):
                for j in range(r.nX):
                    y2, x2 = lax.rem(r.y + i, r.nY), lax.rem(r.x + j, r.nX)
                    if i == 0 and j == 0:
                        pl.when(r.y != r.z)(lambda y2=y2, x2=x2: tell(y2 * 2 + r.k, r.y * r.nX + x2))
                    else:
                        tell(y2 * 2 + r.k, r.y * r.nX + x2)
            count += 2 * (r.nC - 1)
    if b.cross in groups:
        apart = (r.y - r.z) * (r.y - r.z)
        count = count + 2 * lax.div(apart + r.nY * r.nY - 1, r.nY * r.nY)
    pl.semaphore_wait(barrier, count)


def take_hidden(r):
    half, cut = r.nX // 2, r.T // 2
    own_w = pltpu.make_async_copy(r.w_in, r.wp.at[pl.ds(r.k * half, half)], r.sems[b.loc].at[0])
    own_w.start()
    turn = rcopy(
        r.hidden, r.hg.at[r.x, r.y], r.sems[b.tu_s].at[0], r.sems[b.tu_r].at[0], r.z * 2 + r.k, r.y * r.nX + r.x
    )
    start(r, turn, r.y != r.z)
    start(r, pair_copy(r, r.w_in, r.wp.at[pl.ds(r.k * half, half)], b.wp))

    @pl.when(r.y == r.z)
    def _():
        r.hg[r.x, r.y] = r.hidden[...]

    gate = r.gate_in[...].astype(F32)
    sig = jax.nn.sigmoid(gate)
    grad = r.out_grad[...].astype(F32)
    r.g[...] = grad * (gate * sig)
    r.gs[...] = grad * (sig * (1.0 + gate * (1.0 - sig)))
    r.am[...] = -jnp.exp(r.a_log[...])
    r.part[:, :, pl.ds(r.R, LANES)] = jnp.zeros((r.nC, r.RP, LANES), F32)
    r.part2[:, :, pl.ds(r.R, LANES)] = jnp.zeros((r.nC, r.RP, LANES), F32)
    own_w.wait()

    @pl.when(r.y != r.z)
    def _():
        rcopy(
            r.hidden, r.hg.at[r.x, r.z], r.sems[b.tu_s].at[0], r.sems[b.tu_r].at[0], r.z * 2 + r.k, r.y * r.nX + r.x
        ).wait_recv()

    low, high = pl.ds(0, cut), pl.ds(cut, r.T - cut)
    for i in range(1, r.nX):
        start(r, plane_copy(r, i, True, r.hg.at[r.x, r.z, low], r.hg.at[r.x, r.z, low], b.g1, r.x))
        start(r, plane_copy(r, i, False, r.hg.at[r.x, r.z, high], r.hg.at[r.x, r.z, high], b.g1, r.z))
    for i in range(1, r.nX):
        x2, z2 = lax.rem(r.x + i, r.nX), lax.rem(r.z + i, r.nY)
        plane_copy(r, i, True, r.hg.at[x2, r.z, low], r.hg.at[x2, r.z, low], b.g1, x2).wait_recv()
        plane_copy(r, i, False, r.hg.at[r.x, z2, high], r.hg.at[r.x, z2, high], b.g1, z2).wait_recv()
    for i in range(1, r.nX):
        start(r, plane_copy(r, i, False, r.hg.at[:, r.z, low], r.hg.at[:, r.z, low], b.g2, r.z))
        start(r, plane_copy(r, i, True, r.hg.at[r.x, :, high], r.hg.at[r.x, :, high], b.g2, r.x))
    pair_copy(r, r.w_in, r.wp.at[pl.ds((1 - r.k) * half, half)], b.wp).wait_recv()
    for i in range(1, r.nX):
        x2, z2 = lax.rem(r.x + i, r.nX), lax.rem(r.z + i, r.nY)
        plane_copy(r, i, True, r.hg.at[x2, :, high], r.hg.at[x2, :, high], b.g2, x2).wait_recv()
        plane_copy(r, i, False, r.hg.at[:, z2, low], r.hg.at[:, z2, low], b.g2, z2).wait_recv()


def tail_copy(r, i, y2, slot):
    return rcopy(
        r.xs.at[i, pl.ds(r.T - HALO, HALO)],
        r.xt.at[slot],
        r.sems[b.tail_s].at[i],
        r.sems[b.tail_r].at[slot],
        y2 * 2 + r.k + 1,
        r.c,
    )


def project(r):
    for i in range(1, r.nY + 1):
        y2 = lax.rem(r.y + i, r.nY)
        total = None
        for j in range(r.nX):
            term = dot(r.hg[j, y2], r.wp[j])
            total = term if total is None else total + term
        r.xs[i - 1] = total.astype(BF16)
        if i < r.nY:
            start(r, line_copy(r, i, r.xs.at[i - 1], r.xr.at[r.y], b.xr, r.y))
        start(r, tail_copy(r, i - 1, y2, r.y), y2 * 2 + r.k + 1 < r.nS)
    own = total

    @pl.when(r.s == 0)
    def _():
        r.xpad[pl.ds(0, HALO), :] = jnp.zeros((HALO, r.C), F32)

    @pl.when(r.s > 0)
    def _():
        tail = None
        for y2 in range(r.nY):
            tail_copy(r, 0, r.y, y2).wait_recv()
            term = r.xt[y2].astype(F32)
            tail = term if tail is None else tail + term
        r.xpad[pl.ds(0, HALO), :] = tail.astype(BF16).astype(F32)

    for i in range(1, r.nY):
        y2 = lax.rem(r.y + i, r.nY)
        line_copy(r, i, r.xs.at[i - 1], r.xr.at[y2], b.xr, y2).wait_recv()
        own = own + r.xr[y2].astype(F32)
    r.xpad[pl.ds(HALO, r.T), :] = own.astype(BF16).astype(F32)
    conv = jnp.zeros((r.T, r.C), F32) + r.conv_b[...]
    for k in range(r.KC):
        conv = conv + r.conv_w[k : k + 1, :] * r.xpad[pl.ds(HALO - r.KC + 1 + k, r.T), :]
    sig = jax.nn.sigmoid(conv)
    u = (conv * sig).astype(BF16)
    r.u[...] = u
    r.part[:, :, pl.ds(0, r.R)] = contract_last(u, r.w_delta_in[...]).reshape(r.nC, r.RP, r.R)
    r.part[:, :, pl.ds(r.R, 2 * r.N)] = contract_last(u, r.w_bc[...]).reshape(r.nC, r.RP, 2 * r.N)
    scatter_start(r, b.chan, r.part, r.part_r, b.p1)
    r.slope[...] = sig * (1.0 + conv * (1.0 - sig))
    r.part_a[r.c] = scatter_sum(r, b.chan, r.part, r.part_r, b.p1)
    gather_start(r, b.chan, r.part_a, b.p2)
    recv_wait(r, b.chan, r.part_a, b.p2)
    full = r.part_a[...].reshape(r.T, r.R + LANES)
    r.low[...] = full[:, : r.R].astype(BF16)
    r.bcw[...] = full[:, r.R :]


def wide(r, b):
    return jnp.concatenate([b] * (r.C // LANES), axis=1) if r.C > LANES else b


def block_mask(r, rows):
    row = lax.broadcasted_iota(jnp.int32, (rows, CH * r.N), 0)
    col = lax.broadcasted_iota(jnp.int32, (rows, CH * r.N), 1)
    return jnp.where(lax.rem(row, CH) == lax.div(col, r.N), 1.0, 0.0).astype(F32)


def pick(r):
    row = lax.broadcasted_iota(jnp.int32, (r.N, CH * r.N), 0)
    col = lax.broadcasted_iota(jnp.int32, (r.N, CH * r.N), 1)
    return jnp.where(lax.rem(col, r.N) == row, 1.0, 0.0).astype(F32)


def prepare(r):
    pre = dot(r.low[...], r.w_dt[...]) + r.dt_bias[...]
    r.pre[...] = pre
    delta = softplus(pre)
    r.delta[...] = delta
    r.sd[...] = jnp.sum(delta, 0, keepdims=True)
    for i, j, dev in peers(r, b.seq):
        start(r, rcopy(r.sd, r.sd_r.at[r.s], r.sems[b.sd_s].at[i], r.sems[b.sd_r].at[r.s], *dev))
    u = r.u[...].astype(F32)
    r.du[...] = delta * u
    turned = r.bcw[...].T
    for t in range(r.T):
        r.bx[t] = jnp.broadcast_to(turned[0 : r.N, t : t + 1], (r.N, LANES))
        r.cx[t] = jnp.broadcast_to(turned[r.N : 2 * r.N, t : t + 1], (r.N, LANES))


def forward(r, init, full):
    a_mat = r.am[...]
    if full:
        mask = block_mask(r, CH)
        r.hh[pl.ds(0, r.N), :] = init

    def chunk(j, h):
        base = pl.multiple_of(j * CH, CH)
        d = r.delta[pl.ds(base, CH), :]
        du = r.du[pl.ds(base, CH), :]
        kept = []
        for t in range(CH):
            at = pl.multiple_of((base + t) * r.N, r.N)
            if full:
                a = r.aa[pl.ds(at, r.N), :]
            else:
                a = jnp.exp(d[t : t + 1, :] * a_mat)
                r.aa[pl.ds(at, r.N), :] = a
            h = a * h + du[t : t + 1, :] * wide(r, r.bx[base + t])
            if full:
                r.hh[pl.ds(at + r.N, r.N), :] = h
                kept.append(h.astype(BF16))
        if full:
            rows = jnp.concatenate(kept, 0)
            r.y_scan[pl.ds(base, CH), :] = dot(r.cd[pl.ds(base, CH), :], rows)
            r.cm[pl.ds(base, CH), :] = mask * contract_last(r.g[pl.ds(base, CH), :].astype(BF16), rows)
        return h

    return lax.fori_loop(0, r.T // CH, chunk, init)


def backward(r, init, full):
    a_mat = r.am[...]
    mask = block_mask(r, CH)
    chunks = r.T // CH

    def chunk(i, carry):
        base = pl.multiple_of((chunks - 1 - i) * CH, CH)
        kap, acc = carry
        d = r.delta[pl.ds(base, CH), :]
        g = r.g[pl.ds(base, CH), :]
        lams, qas = [None] * CH, [None] * CH
        for t in reversed(range(CH)):
            at = pl.multiple_of((base + t) * r.N, r.N)
            lam = kap + wide(r, r.cx[base + t]) * g[t : t + 1, :]
            kap = r.aa[pl.ds(at, r.N), :] * lam
            if full:
                q = kap * r.hh[pl.ds(at, r.N), :]
                acc = acc + q * d[t : t + 1, :]
                qas[t] = (q * a_mat).astype(BF16)
                lams[t] = lam.astype(BF16)
        if full:
            lam_rows = jnp.concatenate(lams, 0)
            du = r.du[pl.ds(base, CH), :]
            r.s1[pl.ds(base, CH), :] = dot(r.bd[pl.ds(base, CH), :], lam_rows)
            r.s2[pl.ds(base, CH), :] = dot(mask.astype(BF16), jnp.concatenate(qas, 0))
            r.bm[pl.ds(base, CH), :] = mask * contract_last(du.astype(BF16), lam_rows)
        return kap, acc

    return lax.fori_loop(0, chunks, chunk, (init, jnp.zeros_like(init)))


def state_copy(r, which, j, slot):
    return rcopy(r.ef.at[which], r.st_r.at[slot], r.sems[b.st_s].at[j], r.sems[b.st_r].at[slot], j, r.c)


def scan(r):
    zero = jnp.zeros((r.N, r.C), F32)
    r.ef[0] = forward(r, zero, False).astype(BF16)
    for j in range(1, r.nS):
        start(r, state_copy(r, 0, j, r.s), j > r.s)
    r.ef[1] = backward(r, zero, False)[0].astype(BF16)
    for j in range(r.nS - 1):
        start(r, state_copy(r, 1, j, r.s), j < r.s)
    picked = pick(r)
    tall = block_mask(r, r.T)
    r.bd[...] = (tall * dot(r.bcw[:, pl.ds(0, r.N)], picked)).astype(BF16)
    r.cd[...] = (tall * dot(r.bcw[:, pl.ds(r.N, r.N)], picked)).astype(BF16)

    def enter(j, into):
        rcopy(r.sd, r.sd_r.at[j], r.sems[b.sd_s].at[0], r.sems[b.sd_r].at[j], j, r.c).wait_recv()
        state_copy(r, 0, j, j).wait_recv()
        into[...] = jnp.exp(r.am[...] * r.sd_r[j]) * into[...] + r.st_r[j].astype(F32)

    r.h_in[...] = zero
    for j in range(r.nS - 1):
        pl.when(j < r.s)(functools.partial(enter, j, r.h_in))
    forward(r, r.h_in[...], True)
    r.l_in[...] = zero
    for j in range(r.nS - 1, 0, -1):
        pl.when(j > r.s)(functools.partial(enter, j, r.l_in))
    a_adj = backward(r, r.l_in[...], True)[1]
    s1 = r.s1[...]
    u = r.u[...].astype(F32)
    pre_adj = ((u * s1 + r.s2[...]) * jax.nn.sigmoid(r.pre[...])).astype(BF16)
    exact = lax.Precision.HIGHEST
    nt = (((1,), (1,)), ((), ()))
    b_adj = lax.dot_general(r.bm[...], picked, nt, precision=exact, preferred_element_type=F32)
    c_adj = lax.dot_general(r.cm[...], picked, nt, precision=exact, preferred_element_type=F32)
    r.part2[:, :, pl.ds(0, r.R)] = contract_last(pre_adj, r.w_dt[...]).reshape(r.nC, r.RP, r.R)
    r.part2[:, :, pl.ds(r.R, r.N)] = b_adj.reshape(r.nC, r.RP, r.N)
    r.part2[:, :, pl.ds(r.R + r.N, r.N)] = c_adj.reshape(r.nC, r.RP, r.N)
    scatter_start(r, b.chan, r.part2, r.part2_r, b.p3)
    r.dt_p[...] = contract_first(r.low[...], pre_adj).astype(BF16).reshape(2, r.nY, r.R // r.nS, r.C)
    start(r, pair_copy(r, r.dt_p.at[1 - r.k], r.dt_b, b.d1))
    alog = (a_adj * r.am[...]).astype(BF16)
    wide_half = r.C // 2
    for j in range(2):
        r.mi_p[j, pl.ds(2 * r.N, r.N), :] = alog[:, j * wide_half : (j + 1) * wide_half]
    skip = r.skip_d[...]
    r.uu[...] = r.delta[...] * s1 + skip * r.g[...]
    r.gate_out[...] = (r.gs[...] * (r.y_scan[...] + skip * u)).astype(BF16)


def grad_copy(r, i, j):
    y2, x2 = lax.rem(r.y + i, r.nY), lax.rem(r.x + j, r.nX)
    n = i * r.nX + j
    return rcopy(
        r.hs.at[n], r.hr.at[r.c], r.sems[b.hg_s].at[n], r.sems[b.hg_r].at[r.c], y2 * 2 + r.k, r.y * r.nX + x2
    )


def weight_pair(r, part, got, summed, key):
    pair_copy(r, part.at[1 - r.k], got, key[0]).wait_recv()
    summed[...] = (part[r.k].astype(F32) + got[...].astype(F32)).astype(BF16)


def weight_line(r, summed, got, whole, keys):
    total = summed[r.y].astype(F32)
    for i in range(1, r.nY):
        y2 = lax.rem(r.y + i, r.nY)
        line_copy(r, i, summed.at[y2], got.at[y2], keys[0], y2).wait_recv()
        total = total + got[y2].astype(F32)
    whole[r.k, r.y] = total.astype(BF16)
    for i in range(1, r.nY):
        start(r, line_copy(r, i, whole.at[r.k, r.y], whole.at[r.k, r.y], keys[1], r.y))


def weight_back(r, whole, line_key, pair_key):
    for i in range(1, r.nY):
        y2 = lax.rem(r.y + i, r.nY)
        line_copy(r, i, whole.at[r.k, y2], whole.at[r.k, y2], line_key, y2).wait_recv()
    start(r, pair_copy(r, whole.at[r.k], whole.at[r.k], pair_key))


def weight_end(r, whole, pair_key):
    pair_copy(r, whole.at[r.k], whole.at[1 - r.k], pair_key).wait_recv()


def spread(r, summed, got, key):
    for i in range(1, r.nY):
        start(r, line_copy(r, i, summed.at[lax.rem(r.y + i, r.nY)], got.at[r.y], key, r.y))


def gradients(r):
    half = r.nX // 2
    wide_half = r.C // 2
    flush(r)
    r.part2_a[r.c] = scatter_sum(r, b.chan, r.part2, r.part2_r, b.p3)
    gather_start(r, b.chan, r.part2_a, b.p4)
    weight_pair(r, r.dt_p, r.dt_b, r.dt_c, (b.d1,))
    spread(r, r.dt_c, r.dt_d, b.d2)
    recv_wait(r, b.chan, r.part2_a, b.p4)
    full = r.part2_a[...].reshape(r.T, r.R + LANES)
    low_adj = full[:, : r.R].astype(BF16)
    bc_adj = full[:, r.R : r.R + 2 * r.N].astype(BF16)
    u_adj = r.uu[...] + dot(low_adj, r.w_delta_in[...]) + dot(bc_adj, r.w_bc[...])
    conv_adj = u_adj * r.slope[...]
    r.cpad[pl.ds(0, r.T), :] = conv_adj

    def head_copy(to):
        return rcopy(
            r.cpad.at[pl.ds(0, HEAD)],
            r.cpad.at[pl.ds(r.T, HEAD)],
            r.sems[b.head_s].at[0],
            r.sems[b.head_r].at[0],
            to,
            r.c,
        )

    start(r, head_copy(r.s - 1), r.s > 0)

    @pl.when(r.s == r.nS - 1)
    def _():
        r.cpad[pl.ds(r.T, HEAD), :] = jnp.zeros((HEAD, r.C), F32)

    def x_adj(first, count):
        rows = pl.ds(first, count)
        total = jnp.zeros((count, r.C), F32)
        for k in range(r.KC):
            total = total + r.conv_w[k : k + 1, :] * r.cpad[pl.ds(first + r.KC - 1 - k, count), :]
        r.xg[r.y, rows] = total.astype(BF16)

    def x_copy(i, slot, part):
        rows = pl.ds(0, r.T - HALO) if part == 0 else pl.ds(r.T - HALO, HALO)
        return line_copy(r, i, r.xg.at[slot, rows], r.xg.at[slot, rows], b.xg, slot, part)

    x_adj(0, r.T - HALO)
    for i in range(1, r.nY):
        start(r, x_copy(i, r.y, 0))
    u = r.u[...]
    r.di_p[...] = contract_first(low_adj, u).astype(BF16).reshape(2, r.nY, r.R // r.nS, r.C)
    start(r, pair_copy(r, r.di_p.at[1 - r.k], r.di_b, b.d5))
    bc_term = contract_first(bc_adj, u).astype(BF16)
    for j in range(2):
        r.mi_p[j, pl.ds(0, 2 * r.N), :] = bc_term[:, j * wide_half : (j + 1) * wide_half]
    start(r, pair_copy(r, r.mi_p.at[1 - r.k], r.mi_b, b.m1))
    weight_line(r, r.dt_c, r.dt_d, r.dt_e, (b.d2, b.d3))

    pl.when(r.s < r.nS - 1)(lambda: head_copy(r.s + 1).wait_recv())
    x_adj(r.T - HALO, HALO)
    for i in range(1, r.nY):
        start(r, x_copy(i, r.y, 1))

    for i in range(r.nY):
        y2 = lax.rem(r.y + i, r.nY)
        if i:
            x_copy(i, y2, 0).wait_recv()
            x_copy(i, y2, 1).wait_recv()
        for j in range(r.nX):
            x2 = lax.rem(r.x + j, r.nX)
            n = i * r.nX + j
            r.hs[n] = contract_last(r.xg[y2], r.wp[x2]).astype(BF16)
            if n == 0:

                @pl.when(r.y == r.z)
                def _():
                    r.hr[r.c] = r.hs[0]

                start(r, grad_copy(r, 0, 0), r.y != r.z)
            else:
                start(r, grad_copy(r, i, j))
        if i == 0:
            weight_pair(r, r.di_p, r.di_b, r.di_c, (b.d5,))
            spread(r, r.di_c, r.di_d, b.d6)
            pair_copy(r, r.mi_p.at[1 - r.k], r.mi_b, b.m1).wait_recv()
            r.mi_c[r.y] = (r.mi_p[r.k].astype(F32) + r.mi_b[...].astype(F32)).astype(BF16)
            for i2 in range(1, r.nY):
                start(r, line_copy(r, i2, r.mi_c.at[r.y], r.mi_c.at[r.y], b.m2, r.y))
        if i == 1:
            weight_back(r, r.dt_e, b.d3, b.d4)

    x_all = r.xg[...].reshape(r.nY * r.T, r.C)

    def weight(x2):
        return contract_first(r.hg[x2].reshape(r.nY * r.T, r.DH), x_all)

    for j in range(half):
        r.ws[j] = weight((1 - r.k) * half + j).astype(BF16)
    start(r, pair_copy(r, r.ws, r.wr, b.wg))
    weight_line(r, r.di_c, r.di_d, r.di_e, (b.d6, b.d7))
    total = r.mi_c[r.y].astype(F32)
    for i in range(1, r.nY):
        y2 = lax.rem(r.y + i, r.nY)
        line_copy(r, i, r.mi_c.at[y2], r.mi_c.at[y2], b.m2, y2).wait_recv()
        total = total + r.mi_c[y2].astype(F32)
    r.mi_e[r.k] = total
    start(r, pair_copy(r, r.mi_e.at[r.k], r.mi_e.at[r.k], b.m3))
    for j in range(half):
        r.wo[j] = weight(r.k * half + j)
    pair_copy(r, r.ws, r.wr, b.wg).wait_recv()
    r.w_out[...] = (r.wo[...] + r.wr[...].astype(F32)).astype(BF16)
    weight_back(r, r.di_e, b.d7, b.d8)
    weight_end(r, r.dt_e, b.d4)
    pair_copy(r, r.mi_e.at[r.k], r.mi_e.at[1 - r.k], b.m3).wait_recv()
    total = None
    for j in range(r.nC):
        c2 = lax.rem(r.c + j, r.nC)
        wait = rcopy(
            r.hs.at[0], r.hr.at[c2], r.sems[b.hg_s].at[0], r.sems[b.hg_r].at[c2], r.z * 2 + r.k, c2
        )
        if j == 0:
            pl.when(r.y != r.z)(lambda wait=wait: wait.wait_recv())
        else:
            wait.wait_recv()
        term = r.hr[c2].astype(F32)
        total = term if total is None else total + term
    r.hidden_out[...] = total.astype(BF16)
    weight_end(r, r.di_e, b.d8)
    flush(r)


def finish(r):
    scale = 1.0 / math.sqrt(r.T * r.nS)
    wide_half = r.C // 2
    r.hidden_grad[...] = r.hidden_out[...]
    r.gate_grad[...] = r.gate_out[...]
    r.w_in_grad[...] = r.w_out[...].astype(F32) * scale
    r.w_dt_grad[...] = r.dt_e[...].astype(F32).reshape(r.R, r.C) * scale
    r.w_delta_in_grad[...] = r.di_e[...].astype(F32).reshape(r.R, r.C) * scale
    for j in range(2):
        cols = pl.ds(j * wide_half, wide_half)
        r.w_bc_grad[:, cols] = r.mi_e[j, pl.ds(0, 2 * r.N), :] * scale
        r.a_log_grad[:, cols] = r.mi_e[j, pl.ds(2 * r.N, r.N), :] * scale


def tables(dim):
    d = types.SimpleNamespace(**dim)
    t, c, n, rows, q = d.T, d.C, d.N, d.R, d.R // d.nS
    wide_row = rows + LANES
    buffers = dict(
        hg=((d.nX, d.nY, t, d.DH), BF16),
        wp=((d.nX, d.DH, c), BF16),
        xs=((d.nY, t, c), BF16),
        xr=((d.nY, t, c), BF16),
        xt=((d.nY, HALO, c), BF16),
        xpad=((HALO + t, c), F32),
        slope=((t, c), F32),
        gs=((t, c), F32),
        u=((t, c), BF16),
        part=((d.nC, d.RP, wide_row), F32),
        part_r=((d.nC, d.RP, wide_row), F32),
        part_a=((d.nC, d.RP, wide_row), F32),
        low=((t, rows), BF16),
        bcw=((t, LANES), F32),
        pre=((t, c), F32),
        delta=((t, c), F32),
        du=((t, c), F32),
        g=((t, c), F32),
        am=((n, c), F32),
        bx=((t, n, LANES), F32),
        cx=((t, n, LANES), F32),
        sd=((1, c), F32),
        aa=((t * n, c), F32),
        hh=(((t + 1) * n, c), F32),
        ef=((2, n, c), BF16),
        st_r=((d.nS, n, c), BF16),
        sd_r=((d.nS, 1, c), F32),
        h_in=((n, c), F32),
        l_in=((n, c), F32),
        bd=((t, CH * n), BF16),
        cd=((t, CH * n), BF16),
        bm=((t, CH * n), F32),
        cm=((t, CH * n), F32),
        y_scan=((t, c), F32),
        s1=((t, c), F32),
        s2=((t, c), F32),
        uu=((t, c), F32),
        part2=((d.nC, d.RP, wide_row), F32),
        part2_r=((d.nC, d.RP, wide_row), F32),
        part2_a=((d.nC, d.RP, wide_row), F32),
        dt_p=((2, d.nY, q, c), BF16),
        dt_b=((d.nY, q, c), BF16),
        dt_c=((d.nY, q, c), BF16),
        dt_d=((d.nY, q, c), BF16),
        dt_e=((2, d.nY, q, c), BF16),
        di_p=((2, d.nY, q, c), BF16),
        di_b=((d.nY, q, c), BF16),
        di_c=((d.nY, q, c), BF16),
        di_d=((d.nY, q, c), BF16),
        di_e=((2, d.nY, q, c), BF16),
        mi_p=((2, 3 * n, c // 2), BF16),
        mi_b=((3 * n, c // 2), BF16),
        mi_c=((d.nY, 3 * n, c // 2), BF16),
        mi_e=((2, 3 * n, c // 2), F32),
        cpad=((t + HEAD, c), F32),
        xg=((d.nY, t, c), BF16),
        hs=((d.nC, t, d.DH), BF16),
        hr=((d.nC, t, d.DH), BF16),
        ws=((d.nX // 2, d.DH, c), BF16),
        wr=((d.nX // 2, d.DH, c), BF16),
        wo=((d.nX // 2, d.DH, c), F32),
        w_out=((d.nX // 2, d.DH, c), BF16),
        hidden_out=((t, d.DH), BF16),
        gate_out=((t, c), BF16),
        hidden_grad=((t, d.DH), BF16),
        gate_grad=((t, c), BF16),
        w_in_grad=((d.nX // 2, d.DH, c), F32),
        w_delta_in_grad=((rows, c), F32),
        w_bc_grad=((2 * n, c), F32),
        w_dt_grad=((rows, c), F32),
        a_log_grad=((n, c), F32),
    )
    sems = dict(loc=1)
    pairs = (b.tu, b.wp, b.head, b.wg, b.d1, b.d4, b.d5, b.d8, b.m1, b.m3)
    lines = (b.xr, b.tail, b.d2, b.d3, b.d6, b.d7, b.m2)
    for key in pairs:
        sems[key + "_s"] = sems[key + "_r"] = 1
    for key in lines:
        sems[key + "_s"] = sems[key + "_r"] = d.nY
    sems[b.xg_s] = sems[b.xg_r] = 2 * d.nY
    for key in (b.g1, b.g2):
        sems[key + "_s"] = sems[key + "_r"] = d.nX + d.nY
    for key in (b.hg, b.p1, b.p2, b.p3, b.p4):
        sems[key + "_s"] = sems[key + "_r"] = d.nC
    for key in (b.st, b.sd):
        sems[key + "_s"] = sems[key + "_r"] = d.nS
    return buffers, sems


def run(dim, phases, groups, values, ins, outs, scratch, sem_names, number, cost):
    buffers, sem_sizes = tables(dim)

    def body(*refs):
        r = types.SimpleNamespace(**dim)
        for name, ref in zip(ins + outs + scratch, refs):
            setattr(r, name, ref)
        r.sems = dict(zip(sem_names, refs[len(ins) + len(outs) + len(scratch) :]))
        r.sent = []
        if groups:
            r.s, r.c = lax.axis_index(b.seq), lax.axis_index(b.chan)
            r.y, r.k = lax.div(r.s, 2), lax.rem(r.s, 2)
            r.z, r.x = lax.div(r.c, r.nX), lax.rem(r.c, r.nX)
            greet(r, groups)
        for phase in phases:
            phase(r)

    space = pl.BlockSpec(memory_space=pltpu.VMEM)
    extra = dict(collective_id=number, has_side_effects=True) if groups else {}
    results = pl.pallas_call(
        body,
        out_shape=[jax.ShapeDtypeStruct(*buffers[name]) for name in outs],
        in_specs=[space] * len(ins),
        out_specs=[space] * len(outs),
        scratch_shapes=[pltpu.VMEM(*buffers[name]) for name in scratch]
        + [pltpu.SemaphoreType.DMA((sem_sizes[name],)) for name in sem_names],
        compiler_params=pltpu.CompilerParams(vmem_limit_bytes=56 << 20, **extra),
        cost_estimate=pl.CostEstimate(flops=cost, bytes_accessed=4 << 20, transcendentals=0),
        name=phases[0].__name__,
    )(*[values[name] for name in ins])
    values.update(zip(outs, results))


ORDER = [b.hidden_grad, b.gate_grad, b.w_in_grad, b.w_delta_in_grad, b.w_bc_grad, b.w_dt_grad, b.a_log_grad]


def per_device(
    seq, chan, hidden, gate_in, out_grad, w_in, conv_w, conv_b, w_delta_in, w_bc, w_dt, dt_bias, a_log, skip_d
):
    lines = seq // 2
    dim = dict(
        nS=seq,
        nC=chan,
        nY=lines,
        nX=chan // lines,
        T=hidden.shape[0],
        DH=hidden.shape[1],
        C=w_in.shape[1],
        R=w_delta_in.shape[0],
        N=a_log.shape[0],
        KC=conv_w.shape[0],
        RP=hidden.shape[0] // chan,
    )
    v = dict(
        hidden=hidden,
        gate_in=gate_in,
        out_grad=out_grad,
        w_in=w_in.reshape(dim[b.nX] // 2, dim[b.DH], dim[b.C]),
        conv_w=conv_w,
        conv_b=conv_b[None],
        w_delta_in=w_delta_in,
        w_bc=w_bc,
        w_dt=w_dt,
        dt_bias=dt_bias[None],
        a_log=a_log,
        skip_d=skip_d[None],
    )
    raw = [b.hidden_out, b.gate_out, b.w_out, b.dt_e, b.di_e, b.mi_e]
    given = list(v)
    buffers, sems = tables(dim)
    scratch = [name for name in buffers if name not in given + raw + ORDER]
    run(dim, [take_hidden, project, prepare, scan, gradients], [b.cross, b.chan, b.seq], v, given, raw, scratch, list(sems), 0, 2_000_000_000)
    run(dim, [finish], [], v, raw, ORDER, [], [], 0, 1_000_000)
    v[b.w_in_grad] = v[b.w_in_grad].reshape(w_in.shape)
    return tuple(v[name] for name in ORDER)


def solution(mesh):
    placed = (
        P(b.seq, b.chan),
        P(b.seq, b.chan),
        P(b.seq, b.chan),
        P(b.seq, b.chan),
        P(None, b.chan),
        P(b.chan),
        P(None, b.chan),
        P(None, b.chan),
        P(None, b.chan),
        P(b.chan),
        P(None, b.chan),
        P(b.chan),
    )
    return jax.shard_map(
        functools.partial(per_device, mesh.shape[b.seq], mesh.shape[b.chan]),
        mesh=mesh,
        in_specs=placed,
        out_specs=(
            P(b.seq, b.chan),
            P(b.seq, b.chan),
            P(b.seq, b.chan),
            P(None, b.chan),
            P(None, b.chan),
            P(None, b.chan),
            P(None, b.chan),
        ),
        check_vma=False,
    )
```

```python
import functools
import math
import types

import jax
import jax.numpy as jnp
from jax import lax
from jax.experimental import pallas as pl
from jax.experimental.pallas import tpu as pltpu
from jax.sharding import PartitionSpec as P

MESH = pl.DeviceIdType.MESH


class Names:
    def __getattr__(self, name):
        return name


b = Names()
F32, BF16 = jnp.float32, jnp.bfloat16
CH = 16
LANES = 128
HALO = 16
HEAD = 8


def contract_last(left, right):
    return lax.dot_general(left, right, (((1,), (1,)), ((), ())), preferred_element_type=F32)


def contract_first(left, right):
    return lax.dot_general(left, right, (((0,), (0,)), ((), ())), preferred_element_type=F32)


def dot(left, right):
    return jnp.dot(left, right, preferred_element_type=F32)


def silu_slope(values):
    sig = jax.nn.sigmoid(values)
    return sig * (1.0 + values * (1.0 - sig))


def softplus(v):
    return jnp.maximum(v, 0.0) + jnp.log1p(jnp.exp(-jnp.abs(v)))


def rcopy(src, dst, send, recv, seq, chan):
    return pltpu.make_async_remote_copy(
        src_ref=src,
        dst_ref=dst,
        send_sem=send,
        recv_sem=recv,
        device_id=dict(seq=seq, chan=chan),
        device_id_type=MESH,
    )


def ring(r, group):
    if group == b.seq:
        return r.s, r.nS, lambda j: (j, r.c)
    return r.c, r.nC, lambda j: (r.s, j)


def peers(r, group):
    me, n, dev = ring(r, group)
    for i in range(1, n):
        j = lax.rem(me + i, n)
        yield i, j, dev(j)


def start(r, copy, when=None):
    r.sent.append((copy, when))
    if when is None:
        copy.start()
    else:
        pl.when(when)(copy.start)


def flush(r):
    for copy, when in r.sent:
        if when is None:
            copy.wait_send()
        else:
            pl.when(when)(copy.wait_send)
    r.sent.clear()


def scatter_start(r, group, src, dst, key):
    me = ring(r, group)[0]
    for i, j, dev in peers(r, group):
        start(r, rcopy(src.at[j], dst.at[me], r.sems[key + "_s"].at[i], r.sems[key + "_r"].at[me], *dev))


def gather_start(r, group, buf, key):
    me = ring(r, group)[0]
    for i, j, dev in peers(r, group):
        start(r, rcopy(buf.at[me], buf.at[me], r.sems[key + "_s"].at[i], r.sems[key + "_r"].at[me], *dev))


def recv_wait(r, group, buf, key):
    for i, j, dev in peers(r, group):
        rcopy(buf.at[j], buf.at[j], r.sems[key + "_s"].at[i], r.sems[key + "_r"].at[j], *dev).wait_recv()


def scatter_sum(r, group, src, dst, key):
    me = ring(r, group)[0]
    total = src[me].astype(F32)
    recv_wait(r, group, dst, key)
    for i, j, dev in peers(r, group):
        total = total + dst[j].astype(F32)
    return total


def pair_copy(r, src, dst, key):
    return rcopy(src, dst, r.sems[key + "_s"].at[0], r.sems[key + "_r"].at[0], r.y * 2 + 1 - r.k, r.c)


def line_copy(r, i, src, dst, key, slot, part=0):
    at = part * r.nY
    return rcopy(
        src,
        dst,
        r.sems[key + "_s"].at[at + i],
        r.sems[key + "_r"].at[at + slot],
        lax.rem(r.y + i, r.nY) * 2 + r.k,
        r.c,
    )


def plane_copy(r, i, along_x, src, dst, key, slot):
    at, seq = (0 if along_x else r.nX), r.s
    chan = r.z * r.nX + lax.rem(r.x + i, r.nX) if along_x else lax.rem(r.z + i, r.nY) * r.nX + r.x
    return rcopy(src, dst, r.sems[key + "_s"].at[at + i], r.sems[key + "_r"].at[at + slot], seq, chan)


def greet(r, during):
    barrier = pltpu.get_barrier_semaphore()

    def tell(seq, chan):
        pl.semaphore_signal(barrier, inc=1, device_id=dict(seq=seq, chan=chan), device_id_type=MESH)

    pl.when(r.y != r.z)(lambda: tell(r.z * 2 + r.k, r.y * r.nX + r.x))
    for i in range(1, r.nX):
        tell(r.s, r.z * r.nX + lax.rem(r.x + i, r.nX))
        tell(r.s, lax.rem(r.z + i, r.nY) * r.nX + r.x)
    for i, j, dev in peers(r, b.seq):
        tell(*dev)
    during()
    apart = (r.y - r.z) * (r.y - r.z)
    apart = lax.div(apart + r.nY * r.nY - 1, r.nY * r.nY)
    pl.semaphore_wait(barrier, 2 * (r.nX - 1) + r.nS - 1 + apart)


def load(r):
    for at, (name, ref) in enumerate(r.given.items()):
        if name in (b.w_in, b.hidden):
            continue
        pltpu.make_async_copy(ref, getattr(r, name), r.sems[b.inp].at[at]).start()


def need(r, *names):
    for name in names:
        at = list(r.given).index(name)
        pltpu.make_async_copy(r.given[name], getattr(r, name), r.sems[b.inp].at[at]).wait()


def weight_rows(r, y2, core, part):
    half, cut = r.nX // 2, r.DH // 2
    return r.wf.at[y2, pl.ds(core * half, half), pl.ds(part * cut, cut)]


def weight_copy(r, i, y2, part):
    rows = weight_rows(r, y2, r.k, part)
    return line_copy(r, i, rows, rows, b.wy, y2, part)


def relay_copy(r, i, y2, core, part):
    rows, at = weight_rows(r, y2, core, part), part * r.nY + i
    return rcopy(rows, rows, r.sems[b.wz_s].at[at], r.sems[b.wz_r].at[at], r.y * 2 + 1 - r.k, r.c)


def weight_send(r, part):
    for i in range(1, r.nY):
        start(r, weight_copy(r, i, r.y, part))


def weight_relay(r, part):
    for i in range(1, r.nY):
        y2 = lax.rem(r.y + i, r.nY)
        weight_copy(r, i, y2, part).wait_recv()
        start(r, relay_copy(r, i, y2, r.k, part))


def take_hidden(r):
    half, cut = r.nX // 2, r.T // 2
    mine = r.wf.at[r.y, pl.ds(r.k * half, half)]
    own_w = pltpu.make_async_copy(r.w_in, mine, r.sems[b.loc].at[0])
    own_h = pltpu.make_async_copy(r.hidden, r.hg.at[r.x, r.y], r.sems[b.loc].at[1])
    turn = rcopy(
        r.hidden, r.hg.at[r.x, r.y], r.sems[b.tu_s].at[0], r.sems[b.tu_r].at[0], r.z * 2 + r.k, r.y * r.nX + r.x
    )
    start(r, turn, r.y != r.z)
    start(r, pair_copy(r, r.w_in, mine, b.wp))
    own_w.start()
    pl.when(r.y == r.z)(own_h.start)
    need(r, b.gate_in, b.out_grad, b.a_log)

    gate = r.gate_in[...].astype(F32)
    sig = jax.nn.sigmoid(gate)
    grad = r.out_grad[...].astype(F32)
    r.g[...] = grad * (gate * sig)
    r.gs[...] = grad * (sig * (1.0 + gate * (1.0 - sig)))
    r.am[...] = -jnp.exp(r.a_log[...])
    r.part[:, :, pl.ds(r.R, LANES)] = jnp.zeros((r.nC, r.RP, LANES), F32)
    r.part2[:, :, pl.ds(r.R, LANES)] = jnp.zeros((r.nC, r.RP, LANES), F32)
    own_w.wait()
    pl.when(r.y == r.z)(own_h.wait)

    @pl.when(r.y != r.z)
    def _():
        rcopy(
            r.hidden, r.hg.at[r.x, r.z], r.sems[b.tu_s].at[0], r.sems[b.tu_r].at[0], r.z * 2 + r.k, r.y * r.nX + r.x
        ).wait_recv()

    low, high = pl.ds(0, cut), pl.ds(cut, r.T - cut)
    for i in range(1, r.nX):
        start(r, plane_copy(r, i, True, r.hg.at[r.x, r.z, low], r.hg.at[r.x, r.z, low], b.g1, r.x))
        start(r, plane_copy(r, i, False, r.hg.at[r.x, r.z, high], r.hg.at[r.x, r.z, high], b.g1, r.z))
    weight_send(r, 0)
    for i in range(1, r.nX):
        x2, z2 = lax.rem(r.x + i, r.nX), lax.rem(r.z + i, r.nY)
        plane_copy(r, i, True, r.hg.at[x2, r.z, low], r.hg.at[x2, r.z, low], b.g1, x2).wait_recv()
        plane_copy(r, i, False, r.hg.at[r.x, z2, high], r.hg.at[r.x, z2, high], b.g1, z2).wait_recv()
    for i in range(1, r.nX):
        start(r, plane_copy(r, i, False, r.hg.at[:, r.z, low], r.hg.at[:, r.z, low], b.g2, r.z))
        start(r, plane_copy(r, i, True, r.hg.at[r.x, :, high], r.hg.at[r.x, :, high], b.g2, r.x))
    pair_copy(r, r.w_in, r.wf.at[r.y, pl.ds((1 - r.k) * half, half)], b.wp).wait_recv()
    for i in range(1, r.nX):
        x2, z2 = lax.rem(r.x + i, r.nX), lax.rem(r.z + i, r.nY)
        plane_copy(r, i, True, r.hg.at[x2, :, high], r.hg.at[x2, :, high], b.g2, x2).wait_recv()
        plane_copy(r, i, False, r.hg.at[:, z2, low], r.hg.at[:, z2, low], b.g2, z2).wait_recv()


def tail_copy(r, i, y2, slot):
    return rcopy(
        r.xs.at[i, pl.ds(r.T - HALO, HALO)],
        r.xt.at[slot],
        r.sems[b.tail_s].at[i],
        r.sems[b.tail_r].at[slot],
        y2 * 2 + r.k + 1,
        r.c,
    )


def project(r):
    for i in range(1, r.nY + 1):
        y2 = lax.rem(r.y + i, r.nY)
        total = None
        for j in range(r.nX):
            term = dot(r.hg[j, y2], r.wf[r.y, j])
            total = term if total is None else total + term
        r.xs[i - 1] = total.astype(BF16)
        if i < r.nY:
            start(r, line_copy(r, i, r.xs.at[i - 1], r.xr.at[r.y], b.xr, r.y))
        start(r, tail_copy(r, i - 1, y2, r.y), y2 * 2 + r.k + 1 < r.nS)
    own = total

    @pl.when(r.s == 0)
    def _():
        r.xpad[pl.ds(0, HALO), :] = jnp.zeros((HALO, r.C), F32)

    @pl.when(r.s > 0)
    def _():
        tail = None
        for y2 in range(r.nY):
            tail_copy(r, 0, r.y, y2).wait_recv()
            term = r.xt[y2].astype(F32)
            tail = term if tail is None else tail + term
        r.xpad[pl.ds(0, HALO), :] = tail.astype(BF16).astype(F32)

    for i in range(1, r.nY):
        y2 = lax.rem(r.y + i, r.nY)
        line_copy(r, i, r.xs.at[i - 1], r.xr.at[y2], b.xr, y2).wait_recv()
        own = own + r.xr[y2].astype(F32)
    r.xpad[pl.ds(HALO, r.T), :] = own.astype(BF16).astype(F32)
    need(r, b.conv_w, b.conv_b, b.w_delta_in, b.w_bc)
    conv = jnp.zeros((r.T, r.C), F32) + r.conv_b[...]
    for k in range(r.KC):
        conv = conv + r.conv_w[k : k + 1, :] * r.xpad[pl.ds(HALO - r.KC + 1 + k, r.T), :]
    sig = jax.nn.sigmoid(conv)
    u = (conv * sig).astype(BF16)
    r.u[...] = u
    r.part[:, :, pl.ds(0, r.R)] = contract_last(u, r.w_delta_in[...]).reshape(r.nC, r.RP, r.R)
    r.part[:, :, pl.ds(r.R, 2 * r.N)] = contract_last(u, r.w_bc[...]).reshape(r.nC, r.RP, 2 * r.N)
    scatter_start(r, b.chan, r.part, r.part_r, b.p1)
    weight_send(r, 1)
    weight_relay(r, 0)
    r.slope[...] = sig * (1.0 + conv * (1.0 - sig))
    r.part_a[r.c] = scatter_sum(r, b.chan, r.part, r.part_r, b.p1)
    gather_start(r, b.chan, r.part_a, b.p2)
    recv_wait(r, b.chan, r.part_a, b.p2)
    full = r.part_a[...].reshape(r.T, r.R + LANES)
    r.low[...] = full[:, : r.R].astype(BF16)
    r.bcw[...] = full[:, r.R :]


def wide(r, b):
    return jnp.concatenate([b] * (r.C // LANES), axis=1) if r.C > LANES else b


def block_mask(r, rows):
    row = lax.broadcasted_iota(jnp.int32, (rows, CH * r.N), 0)
    col = lax.broadcasted_iota(jnp.int32, (rows, CH * r.N), 1)
    return jnp.where(lax.rem(row, CH) == lax.div(col, r.N), 1.0, 0.0).astype(F32)


def pick(r):
    row = lax.broadcasted_iota(jnp.int32, (r.N, CH * r.N), 0)
    col = lax.broadcasted_iota(jnp.int32, (r.N, CH * r.N), 1)
    return jnp.where(lax.rem(col, r.N) == row, 1.0, 0.0).astype(F32)


def prepare(r):
    need(r, b.w_dt, b.dt_bias, b.skip_d)
    pre = dot(r.low[...], r.w_dt[...]) + r.dt_bias[...]
    r.pre[...] = pre
    delta = softplus(pre)
    r.delta[...] = delta
    r.sd[...] = jnp.sum(delta, 0, keepdims=True)
    for i, j, dev in peers(r, b.seq):
        start(r, rcopy(r.sd, r.sd_r.at[r.s], r.sems[b.sd_s].at[i], r.sems[b.sd_r].at[r.s], *dev))
    u = r.u[...].astype(F32)
    r.du[...] = delta * u
    turned = r.bcw[...].T
    for t in range(r.T):
        r.bx[t] = jnp.broadcast_to(turned[0 : r.N, t : t + 1], (r.N, LANES))
        r.cx[t] = jnp.broadcast_to(turned[r.N : 2 * r.N, t : t + 1], (r.N, LANES))


def forward(r, init, full):
    a_mat = r.am[...]
    if full:
        mask = block_mask(r, CH)
        r.hh[pl.ds(0, r.N), :] = init

    def chunk(j, h):
        base = pl.multiple_of(j * CH, CH)
        d = r.delta[pl.ds(base, CH), :]
        du = r.du[pl.ds(base, CH), :]
        kept = []
        for t in range(CH):
            at = pl.multiple_of((base + t) * r.N, r.N)
            if full:
                a = r.aa[pl.ds(at, r.N), :]
            else:
                a = jnp.exp(d[t : t + 1, :] * a_mat)
                r.aa[pl.ds(at, r.N), :] = a
            h = a * h + du[t : t + 1, :] * wide(r, r.bx[base + t])
            if full:
                r.hh[pl.ds(at + r.N, r.N), :] = h
                kept.append(h.astype(BF16))
        if full:
            rows = jnp.concatenate(kept, 0)
            r.y_scan[pl.ds(base, CH), :] = dot(r.cd[pl.ds(base, CH), :], rows)
            r.cm[pl.ds(base, CH), :] = mask * contract_last(r.g[pl.ds(base, CH), :].astype(BF16), rows)
        return h

    return lax.fori_loop(0, r.T // CH, chunk, init)


def backward(r, init, full):
    a_mat = r.am[...]
    mask = block_mask(r, CH)
    chunks = r.T // CH

    def chunk(i, carry):
        base = pl.multiple_of((chunks - 1 - i) * CH, CH)
        kap, acc = carry
        d = r.delta[pl.ds(base, CH), :]
        g = r.g[pl.ds(base, CH), :]
        lams, qas = [None] * CH, [None] * CH
        for t in reversed(range(CH)):
            at = pl.multiple_of((base + t) * r.N, r.N)
            lam = kap + wide(r, r.cx[base + t]) * g[t : t + 1, :]
            kap = r.aa[pl.ds(at, r.N), :] * lam
            if full:
                q = kap * r.hh[pl.ds(at, r.N), :]
                acc = acc + q * d[t : t + 1, :]
                qas[t] = (q * a_mat).astype(BF16)
                lams[t] = lam.astype(BF16)
        if full:
            lam_rows = jnp.concatenate(lams, 0)
            du = r.du[pl.ds(base, CH), :]
            r.s1[pl.ds(base, CH), :] = dot(r.bd[pl.ds(base, CH), :], lam_rows)
            r.s2[pl.ds(base, CH), :] = dot(mask.astype(BF16), jnp.concatenate(qas, 0))
            r.bm[pl.ds(base, CH), :] = mask * contract_last(du.astype(BF16), lam_rows)
        return kap, acc

    return lax.fori_loop(0, chunks, chunk, (init, jnp.zeros_like(init)))


def state_copy(r, which, j, slot):
    return rcopy(r.ef.at[which], r.st_r.at[slot], r.sems[b.st_s].at[j], r.sems[b.st_r].at[slot], j, r.c)


def scan(r):
    zero = jnp.zeros((r.N, r.C), F32)
    r.ef[0] = forward(r, zero, False).astype(BF16)
    for j in range(1, r.nS):
        start(r, state_copy(r, 0, j, r.s), j > r.s)
    r.ef[1] = backward(r, zero, False)[0].astype(BF16)
    for j in range(r.nS - 1):
        start(r, state_copy(r, 1, j, r.s), j < r.s)
    picked = pick(r)
    tall = block_mask(r, r.T)
    r.bd[...] = (tall * dot(r.bcw[:, pl.ds(0, r.N)], picked)).astype(BF16)
    r.cd[...] = (tall * dot(r.bcw[:, pl.ds(r.N, r.N)], picked)).astype(BF16)

    def enter(j, into):
        rcopy(r.sd, r.sd_r.at[j], r.sems[b.sd_s].at[0], r.sems[b.sd_r].at[j], j, r.c).wait_recv()
        state_copy(r, 0, j, j).wait_recv()
        into[...] = jnp.exp(r.am[...] * r.sd_r[j]) * into[...] + r.st_r[j].astype(F32)

    r.h_in[...] = zero
    for j in range(r.nS - 1):
        pl.when(j < r.s)(functools.partial(enter, j, r.h_in))
    forward(r, r.h_in[...], True)
    r.l_in[...] = zero
    for j in range(r.nS - 1, 0, -1):
        pl.when(j > r.s)(functools.partial(enter, j, r.l_in))
    a_adj = backward(r, r.l_in[...], True)[1]
    s1 = r.s1[...]
    u = r.u[...].astype(F32)
    pre_adj = ((u * s1 + r.s2[...]) * jax.nn.sigmoid(r.pre[...])).astype(BF16)
    exact = lax.Precision.HIGHEST
    nt = (((1,), (1,)), ((), ()))
    b_adj = lax.dot_general(r.bm[...], picked, nt, precision=exact, preferred_element_type=F32)
    c_adj = lax.dot_general(r.cm[...], picked, nt, precision=exact, preferred_element_type=F32)
    r.part2[:, :, pl.ds(0, r.R)] = contract_last(pre_adj, r.w_dt[...]).reshape(r.nC, r.RP, r.R)
    r.part2[:, :, pl.ds(r.R, r.N)] = b_adj.reshape(r.nC, r.RP, r.N)
    r.part2[:, :, pl.ds(r.R + r.N, r.N)] = c_adj.reshape(r.nC, r.RP, r.N)
    scatter_start(r, b.chan, r.part2, r.part2_r, b.p3)
    weight_relay(r, 1)
    r.dt_p[...] = contract_first(r.low[...], pre_adj).astype(BF16).reshape(2, r.nY, r.R // r.nS, r.C)
    start(r, pair_copy(r, r.dt_p.at[1 - r.k], r.dt_b, b.d1))
    alog = (a_adj * r.am[...]).astype(BF16)
    wide_half = r.C // 2
    for j in range(2):
        r.mi_p[j, pl.ds(2 * r.N, r.N), :] = alog[:, j * wide_half : (j + 1) * wide_half]
    skip = r.skip_d[...]
    r.uu[...] = r.delta[...] * s1 + skip * r.g[...]
    r.gate_out[...] = (r.gs[...] * (r.y_scan[...] + skip * u)).astype(BF16)


def grad_copy(r, i, part):
    rows = pl.ds(part * (r.T // 2), r.T // 2)
    c2 = lax.rem(r.c + i, r.nC)
    at = part * r.nC
    return rcopy(
        r.hs.at[i, rows], r.hr.at[r.c, rows], r.sems[b.hg_s].at[at + i], r.sems[b.hg_r].at[at + r.c], r.s, c2
    )


def grad_part(r, part):
    rows = pl.ds(part * (r.T // 2), r.T // 2)
    for i in range(r.nC - 1, -1, -1):
        c2 = lax.rem(r.c + i, r.nC)
        term = contract_last(r.xg[r.y, rows], r.wf[lax.div(c2, r.nX), lax.rem(c2, r.nX)])
        r.hs[i, rows] = term.astype(BF16)
        if i:
            start(r, grad_copy(r, i, part))


def weight_pair(r, part, got, summed, key):
    pair_copy(r, part.at[1 - r.k], got, key[0]).wait_recv()
    summed[...] = (part[r.k].astype(F32) + got[...].astype(F32)).astype(BF16)


def weight_line(r, summed, got, whole, keys):
    total = summed[r.y].astype(F32)
    for i in range(1, r.nY):
        y2 = lax.rem(r.y + i, r.nY)
        line_copy(r, i, summed.at[y2], got.at[y2], keys[0], y2).wait_recv()
        total = total + got[y2].astype(F32)
    whole[r.k, r.y] = total.astype(BF16)
    for i in range(1, r.nY):
        start(r, line_copy(r, i, whole.at[r.k, r.y], whole.at[r.k, r.y], keys[1], r.y))


def weight_back(r, whole, line_key, pair_key):
    for i in range(1, r.nY):
        y2 = lax.rem(r.y + i, r.nY)
        line_copy(r, i, whole.at[r.k, y2], whole.at[r.k, y2], line_key, y2).wait_recv()
    start(r, pair_copy(r, whole.at[r.k], whole.at[r.k], pair_key))


def weight_end(r, whole, pair_key):
    pair_copy(r, whole.at[r.k], whole.at[1 - r.k], pair_key).wait_recv()


def spread(r, summed, got, key):
    for i in range(1, r.nY):
        start(r, line_copy(r, i, summed.at[lax.rem(r.y + i, r.nY)], got.at[r.y], key, r.y))


def gradients(r):
    half = r.nX // 2
    wide_half = r.C // 2
    flush(r)
    r.part2_a[r.c] = scatter_sum(r, b.chan, r.part2, r.part2_r, b.p3)
    gather_start(r, b.chan, r.part2_a, b.p4)
    weight_pair(r, r.dt_p, r.dt_b, r.dt_c, (b.d1,))
    spread(r, r.dt_c, r.dt_d, b.d2)
    recv_wait(r, b.chan, r.part2_a, b.p4)
    full = r.part2_a[...].reshape(r.T, r.R + LANES)
    low_adj = full[:, : r.R].astype(BF16)
    bc_adj = full[:, r.R : r.R + 2 * r.N].astype(BF16)
    u_adj = r.uu[...] + dot(low_adj, r.w_delta_in[...]) + dot(bc_adj, r.w_bc[...])
    conv_adj = u_adj * r.slope[...]
    r.cpad[pl.ds(0, r.T), :] = conv_adj

    def head_copy(to):
        return rcopy(
            r.cpad.at[pl.ds(0, HEAD)],
            r.cpad.at[pl.ds(r.T, HEAD)],
            r.sems[b.head_s].at[0],
            r.sems[b.head_r].at[0],
            to,
            r.c,
        )

    start(r, head_copy(r.s - 1), r.s > 0)

    @pl.when(r.s == r.nS - 1)
    def _():
        r.cpad[pl.ds(r.T, HEAD), :] = jnp.zeros((HEAD, r.C), F32)

    def x_adj(first, count):
        rows = pl.ds(first, count)
        total = jnp.zeros((count, r.C), F32)
        for k in range(r.KC):
            total = total + r.conv_w[k : k + 1, :] * r.cpad[pl.ds(first + r.KC - 1 - k, count), :]
        r.xg[r.y, rows] = total.astype(BF16)

    def x_copy(i, slot, part):
        rows = pl.ds(part * (r.T // 2), r.T // 2)
        return line_copy(r, i, r.xg.at[slot, rows], r.xg.at[slot, rows], b.xg, slot, part)

    x_adj(0, r.T // 2)
    for i in range(1, r.nY):
        start(r, x_copy(i, r.y, 0))
    for part in range(2):
        for i in range(1, r.nY):
            relay_copy(r, i, lax.rem(r.y + i, r.nY), 1 - r.k, part).wait_recv()
    grad_part(r, 0)
    u = r.u[...]
    r.di_p[...] = contract_first(low_adj, u).astype(BF16).reshape(2, r.nY, r.R // r.nS, r.C)
    start(r, pair_copy(r, r.di_p.at[1 - r.k], r.di_b, b.d5))
    bc_term = contract_first(bc_adj, u).astype(BF16)
    for j in range(2):
        r.mi_p[j, pl.ds(0, 2 * r.N), :] = bc_term[:, j * wide_half : (j + 1) * wide_half]
    start(r, pair_copy(r, r.mi_p.at[1 - r.k], r.mi_b, b.m1))
    weight_line(r, r.dt_c, r.dt_d, r.dt_e, (b.d2, b.d3))

    pl.when(r.s < r.nS - 1)(lambda: head_copy(r.s + 1).wait_recv())
    x_adj(r.T // 2, r.T // 2)
    for i in range(1, r.nY):
        start(r, x_copy(i, r.y, 1))
    grad_part(r, 1)
    weight_pair(r, r.di_p, r.di_b, r.di_c, (b.d5,))
    spread(r, r.di_c, r.di_d, b.d6)
    pair_copy(r, r.mi_p.at[1 - r.k], r.mi_b, b.m1).wait_recv()
    r.mi_c[r.y] = (r.mi_p[r.k].astype(F32) + r.mi_b[...].astype(F32)).astype(BF16)
    for i in range(1, r.nY):
        start(r, line_copy(r, i, r.mi_c.at[r.y], r.mi_c.at[r.y], b.m2, r.y))
    weight_back(r, r.dt_e, b.d3, b.d4)
    for i in range(1, r.nY):
        y2 = lax.rem(r.y + i, r.nY)
        x_copy(i, y2, 0).wait_recv()
        x_copy(i, y2, 1).wait_recv()

    x_all = r.xg[...].reshape(r.nY * r.T, r.C)

    def weight(x2):
        return contract_first(r.hg[x2].reshape(r.nY * r.T, r.DH), x_all)

    for j in range(half):
        r.ws[j] = weight((1 - r.k) * half + j).astype(BF16)
    start(r, pair_copy(r, r.ws, r.wr, b.wg))
    weight_line(r, r.di_c, r.di_d, r.di_e, (b.d6, b.d7))
    total = r.mi_c[r.y].astype(F32)
    for i in range(1, r.nY):
        y2 = lax.rem(r.y + i, r.nY)
        line_copy(r, i, r.mi_c.at[y2], r.mi_c.at[y2], b.m2, y2).wait_recv()
        total = total + r.mi_c[y2].astype(F32)
    r.mi_e[r.k] = total
    start(r, pair_copy(r, r.mi_e.at[r.k], r.mi_e.at[r.k], b.m3))
    for j in range(half):
        r.wo[j] = weight(r.k * half + j)
    pair_copy(r, r.ws, r.wr, b.wg).wait_recv()
    r.w_out[...] = (r.wo[...] + r.wr[...].astype(F32)).astype(BF16)
    weight_back(r, r.di_e, b.d7, b.d8)
    weight_end(r, r.dt_e, b.d4)
    pair_copy(r, r.mi_e.at[r.k], r.mi_e.at[1 - r.k], b.m3).wait_recv()
    total = r.hs[0].astype(F32)
    for i, c2, dev in peers(r, b.chan):
        for part in range(2):
            rows, at = pl.ds(part * (r.T // 2), r.T // 2), part * r.nC + c2
            got = r.hr.at[c2, rows]
            rcopy(got, got, r.sems[b.hg_s].at[i], r.sems[b.hg_r].at[at], *dev).wait_recv()
        total = total + r.hr[c2].astype(F32)
    r.hidden_out[...] = total.astype(BF16)
    weight_end(r, r.di_e, b.d8)
    flush(r)


def finish(r):
    scale = 1.0 / math.sqrt(r.T * r.nS)
    wide_half = r.C // 2
    r.hidden_grad[...] = r.hidden_out[...]
    r.gate_grad[...] = r.gate_out[...]
    r.w_in_grad[...] = r.w_out[...].astype(F32) * scale
    r.w_dt_grad[...] = r.dt_e[...].astype(F32).reshape(r.R, r.C) * scale
    r.w_delta_in_grad[...] = r.di_e[...].astype(F32).reshape(r.R, r.C) * scale
    for j in range(2):
        cols = pl.ds(j * wide_half, wide_half)
        r.w_bc_grad[:, cols] = r.mi_e[j, pl.ds(0, 2 * r.N), :] * scale
        r.a_log_grad[:, cols] = r.mi_e[j, pl.ds(2 * r.N, r.N), :] * scale


def tables(dim):
    d = types.SimpleNamespace(**dim)
    t, c, n, rows, q = d.T, d.C, d.N, d.R, d.R // d.nS
    wide_row = rows + LANES
    buffers = dict(
        hg=((d.nX, d.nY, t, d.DH), BF16),
        wf=((d.nY, d.nX, d.DH, c), BF16),
        xs=((d.nY, t, c), BF16),
        xr=((d.nY, t, c), BF16),
        xt=((d.nY, HALO, c), BF16),
        xpad=((HALO + t, c), F32),
        slope=((t, c), F32),
        gs=((t, c), F32),
        u=((t, c), BF16),
        part=((d.nC, d.RP, wide_row), F32),
        part_r=((d.nC, d.RP, wide_row), F32),
        part_a=((d.nC, d.RP, wide_row), F32),
        low=((t, rows), BF16),
        bcw=((t, LANES), F32),
        pre=((t, c), F32),
        delta=((t, c), F32),
        du=((t, c), F32),
        g=((t, c), F32),
        am=((n, c), F32),
        bx=((t, n, LANES), F32),
        cx=((t, n, LANES), F32),
        sd=((1, c), F32),
        aa=((t * n, c), F32),
        hh=(((t + 1) * n, c), F32),
        ef=((2, n, c), BF16),
        st_r=((d.nS, n, c), BF16),
        sd_r=((d.nS, 1, c), F32),
        h_in=((n, c), F32),
        l_in=((n, c), F32),
        bd=((t, CH * n), BF16),
        cd=((t, CH * n), BF16),
        bm=((t, CH * n), F32),
        cm=((t, CH * n), F32),
        y_scan=((t, c), F32),
        s1=((t, c), F32),
        s2=((t, c), F32),
        uu=((t, c), F32),
        part2=((d.nC, d.RP, wide_row), F32),
        part2_r=((d.nC, d.RP, wide_row), F32),
        part2_a=((d.nC, d.RP, wide_row), F32),
        dt_p=((2, d.nY, q, c), BF16),
        dt_b=((d.nY, q, c), BF16),
        dt_c=((d.nY, q, c), BF16),
        dt_d=((d.nY, q, c), BF16),
        dt_e=((2, d.nY, q, c), BF16),
        di_p=((2, d.nY, q, c), BF16),
        di_b=((d.nY, q, c), BF16),
        di_c=((d.nY, q, c), BF16),
        di_d=((d.nY, q, c), BF16),
        di_e=((2, d.nY, q, c), BF16),
        mi_p=((2, 3 * n, c // 2), BF16),
        mi_b=((3 * n, c // 2), BF16),
        mi_c=((d.nY, 3 * n, c // 2), BF16),
        mi_e=((2, 3 * n, c // 2), F32),
        cpad=((t + HEAD, c), F32),
        xg=((d.nY, t, c), BF16),
        hs=((d.nC, t, d.DH), BF16),
        hr=((d.nC, t, d.DH), BF16),
        ws=((d.nX // 2, d.DH, c), BF16),
        wr=((d.nX // 2, d.DH, c), BF16),
        wo=((d.nX // 2, d.DH, c), F32),
        w_out=((d.nX // 2, d.DH, c), BF16),
        hidden_out=((t, d.DH), BF16),
        gate_out=((t, c), BF16),
        hidden_grad=((t, d.DH), BF16),
        gate_grad=((t, c), BF16),
        w_in_grad=((d.nX // 2, d.DH, c), F32),
        w_delta_in_grad=((rows, c), F32),
        w_bc_grad=((2 * n, c), F32),
        w_dt_grad=((rows, c), F32),
        a_log_grad=((n, c), F32),
    )
    sems = dict(loc=2, inp=12)
    pairs = (b.tu, b.wp, b.head, b.wg, b.d1, b.d4, b.d5, b.d8, b.m1, b.m3)
    lines = (b.xr, b.tail, b.d2, b.d3, b.d6, b.d7, b.m2)
    for key in pairs:
        sems[key + "_s"] = sems[key + "_r"] = 1
    for key in lines:
        sems[key + "_s"] = sems[key + "_r"] = d.nY
    for key in (b.xg, b.wy, b.wz):
        sems[key + "_s"] = sems[key + "_r"] = 2 * d.nY
    sems[b.hg_s] = sems[b.hg_r] = 2 * d.nC
    for key in (b.g1, b.g2):
        sems[key + "_s"] = sems[key + "_r"] = d.nX + d.nY
    for key in (b.p1, b.p2, b.p3, b.p4):
        sems[key + "_s"] = sems[key + "_r"] = d.nC
    for key in (b.st, b.sd):
        sems[key + "_s"] = sems[key + "_r"] = d.nS
    return buffers, sems


def run(dim, phases, remote, values, ins, outs, scratch, sem_names, cost):
    buffers, sem_sizes = tables(dim)
    held = [name for name in ins if name not in (b.hidden, b.w_in)] if remote else []

    def body(*refs):
        r = types.SimpleNamespace(**dim)
        r.sent = []
        names = ins + outs + scratch
        for name, ref in zip(names, refs):
            setattr(r, name, ref)
        refs = refs[len(names) :]
        r.sems = dict(zip(sem_names, refs))
        if remote:
            r.given = {name: getattr(r, name) for name in ins}
            for name, ref in zip(held, refs[len(sem_names) :]):
                setattr(r, name, ref)
            r.s, r.c = lax.axis_index(b.seq), lax.axis_index(b.chan)
            r.y, r.k = lax.div(r.s, 2), lax.rem(r.s, 2)
            r.z, r.x = lax.div(r.c, r.nX), lax.rem(r.c, r.nX)
            greet(r, functools.partial(load, r))
        for phase in phases:
            phase(r)

    space = pl.BlockSpec(memory_space=pltpu.VMEM)
    extra = dict(collective_id=0, has_side_effects=True) if remote else {}
    results = pl.pallas_call(
        body,
        out_shape=[jax.ShapeDtypeStruct(*buffers[name]) for name in outs],
        in_specs=[pl.BlockSpec(memory_space=pl.ANY) if remote else space] * len(ins),
        out_specs=[space] * len(outs),
        scratch_shapes=[pltpu.VMEM(*buffers[name]) for name in scratch]
        + [pltpu.SemaphoreType.DMA((sem_sizes[name],)) for name in sem_names]
        + [pltpu.VMEM(values[name].shape, values[name].dtype) for name in held],
        compiler_params=pltpu.CompilerParams(vmem_limit_bytes=56 << 20, **extra),
        cost_estimate=pl.CostEstimate(flops=cost, bytes_accessed=4 << 20, transcendentals=0),
        name=phases[-1].__name__,
    )(*[values[name] for name in ins])
    values.update(zip(outs, results))


ORDER = [b.hidden_grad, b.gate_grad, b.w_in_grad, b.w_delta_in_grad, b.w_bc_grad, b.w_dt_grad, b.a_log_grad]


def per_device(
    seq, chan, hidden, gate_in, out_grad, w_in, conv_w, conv_b, w_delta_in, w_bc, w_dt, dt_bias, a_log, skip_d
):
    lines = seq // 2
    dim = dict(
        nS=seq,
        nC=chan,
        nY=lines,
        nX=chan // lines,
        T=hidden.shape[0],
        DH=hidden.shape[1],
        C=w_in.shape[1],
        R=w_delta_in.shape[0],
        N=a_log.shape[0],
        KC=conv_w.shape[0],
        RP=hidden.shape[0] // chan,
    )
    v = dict(
        hidden=hidden,
        gate_in=gate_in,
        out_grad=out_grad,
        w_in=w_in.reshape(dim[b.nX] // 2, dim[b.DH], dim[b.C]),
        conv_w=conv_w,
        conv_b=conv_b[None],
        w_delta_in=w_delta_in,
        w_bc=w_bc,
        w_dt=w_dt,
        dt_bias=dt_bias[None],
        a_log=a_log,
        skip_d=skip_d[None],
    )
    raw = [b.hidden_out, b.gate_out, b.w_out, b.dt_e, b.di_e, b.mi_e]
    given = list(v)
    buffers, sems = tables(dim)
    scratch = [name for name in buffers if name not in given + raw + ORDER]
    phases = [take_hidden, project, prepare, scan, gradients]
    run(dim, phases, True, v, given, raw, scratch, list(sems), 2_000_000_000)
    run(dim, [finish], False, v, raw, ORDER, [], [], 1_000_000)
    v[b.w_in_grad] = v[b.w_in_grad].reshape(w_in.shape)
    return tuple(v[name] for name in ORDER)


def solution(mesh):
    placed = (
        P(b.seq, b.chan),
        P(b.seq, b.chan),
        P(b.seq, b.chan),
        P(b.seq, b.chan),
        P(None, b.chan),
        P(b.chan),
        P(None, b.chan),
        P(None, b.chan),
        P(None, b.chan),
        P(b.chan),
        P(None, b.chan),
        P(b.chan),
    )
    return jax.shard_map(
        functools.partial(per_device, mesh.shape[b.seq], mesh.shape[b.chan]),
        mesh=mesh,
        in_specs=placed,
        out_specs=(
            P(b.seq, b.chan),
            P(b.seq, b.chan),
            P(b.seq, b.chan),
            P(None, b.chan),
            P(None, b.chan),
            P(None, b.chan),
            P(None, b.chan),
        ),
        check_vma=False,
    )
```

```python
import functools
import math
import types

import jax
import jax.numpy as jnp
from jax import lax
from jax.experimental import pallas as pl
from jax.experimental.pallas import tpu as pltpu
from jax.sharding import PartitionSpec as P

MESH = pl.DeviceIdType.MESH


class Names:
    def __getattr__(self, name):
        return name


b = Names()
F32, BF16 = jnp.float32, jnp.bfloat16
CH = 16
LANES = 128
HALO = 16
HEAD = 8


def contract_last(left, right):
    return lax.dot_general(left, right, (((1,), (1,)), ((), ())), preferred_element_type=F32)


def contract_first(left, right):
    return lax.dot_general(left, right, (((0,), (0,)), ((), ())), preferred_element_type=F32)


def dot(left, right):
    return jnp.dot(left, right, preferred_element_type=F32)


def silu_slope(values):
    sig = jax.nn.sigmoid(values)
    return sig * (1.0 + values * (1.0 - sig))


def softplus(v):
    return jnp.maximum(v, 0.0) + jnp.log1p(jnp.exp(-jnp.abs(v)))


def rcopy(src, dst, send, recv, seq, chan):
    return pltpu.make_async_remote_copy(
        src_ref=src,
        dst_ref=dst,
        send_sem=send,
        recv_sem=recv,
        device_id=dict(seq=seq, chan=chan),
        device_id_type=MESH,
    )


def ring(r, group):
    if group == b.seq:
        return r.s, r.nS, lambda j: (j, r.c)
    return r.c, r.nC, lambda j: (r.s, j)


def peers(r, group):
    me, n, dev = ring(r, group)
    for i in range(1, n):
        j = lax.rem(me + i, n)
        yield i, j, dev(j)


def start(r, copy, when=None):
    r.sent.append((copy, when))
    if when is None:
        copy.start()
    else:
        pl.when(when)(copy.start)


def flush(r):
    for copy, when in r.sent:
        if when is None:
            copy.wait_send()
        else:
            pl.when(when)(copy.wait_send)
    r.sent.clear()


def scatter_start(r, group, src, dst, key):
    me = ring(r, group)[0]
    for i, j, dev in peers(r, group):
        start(r, rcopy(src.at[j], dst.at[me], r.sems[key + "_s"].at[i], r.sems[key + "_r"].at[me], *dev))


def gather_start(r, group, buf, key):
    me = ring(r, group)[0]
    for i, j, dev in peers(r, group):
        start(r, rcopy(buf.at[me], buf.at[me], r.sems[key + "_s"].at[i], r.sems[key + "_r"].at[me], *dev))


def recv_wait(r, group, buf, key):
    for i, j, dev in peers(r, group):
        rcopy(buf.at[j], buf.at[j], r.sems[key + "_s"].at[i], r.sems[key + "_r"].at[j], *dev).wait_recv()


def scatter_sum(r, group, src, dst, key):
    me = ring(r, group)[0]
    total = src[me].astype(F32)
    recv_wait(r, group, dst, key)
    for i, j, dev in peers(r, group):
        total = total + dst[j].astype(F32)
    return total


def pair_copy(r, src, dst, key):
    return rcopy(src, dst, r.sems[key + "_s"].at[0], r.sems[key + "_r"].at[0], r.y * 2 + 1 - r.k, r.c)


def line_copy(r, i, src, dst, key, slot, part=0):
    at = part * r.nY
    return rcopy(
        src,
        dst,
        r.sems[key + "_s"].at[at + i],
        r.sems[key + "_r"].at[at + slot],
        lax.rem(r.y + i, r.nY) * 2 + r.k,
        r.c,
    )


def plane_copy(r, i, along_x, src, dst, key, slot):
    at, seq = (0 if along_x else r.nX), r.s
    chan = r.z * r.nX + lax.rem(r.x + i, r.nX) if along_x else lax.rem(r.z + i, r.nY) * r.nX + r.x
    return rcopy(src, dst, r.sems[key + "_s"].at[at + i], r.sems[key + "_r"].at[at + slot], seq, chan)


def greet(r, during):
    barrier = pltpu.get_barrier_semaphore()

    def tell(seq, chan):
        pl.semaphore_signal(barrier, inc=1, device_id=dict(seq=seq, chan=chan), device_id_type=MESH)

    pl.when(r.y != r.z)(lambda: tell(r.z * 2 + r.k, r.y * r.nX + r.x))
    for i in range(1, r.nX):
        tell(r.s, r.z * r.nX + lax.rem(r.x + i, r.nX))
        tell(r.s, lax.rem(r.z + i, r.nY) * r.nX + r.x)
    for i, j, dev in peers(r, b.seq):
        tell(*dev)
    during()
    apart = (r.y - r.z) * (r.y - r.z)
    apart = lax.div(apart + r.nY * r.nY - 1, r.nY * r.nY)
    pl.semaphore_wait(barrier, 2 * (r.nX - 1) + r.nS - 1 + apart)


def load(r):
    for at, (name, ref) in enumerate(r.given.items()):
        if name in (b.w_in, b.hidden):
            continue
        pltpu.make_async_copy(ref, getattr(r, name), r.sems[b.inp].at[at]).start()


def need(r, *names):
    for name in names:
        at = list(r.given).index(name)
        pltpu.make_async_copy(r.given[name], getattr(r, name), r.sems[b.inp].at[at]).wait()


def weight_rows(r, y2, core, part):
    half, cut = r.nX // 2, r.DH // 2
    return r.wf.at[y2, pl.ds(core * half, half), pl.ds(part * cut, cut)]


def weight_copy(r, i, y2, part):
    rows = weight_rows(r, y2, r.k, part)
    return line_copy(r, i, rows, rows, b.wy, y2, part)


def relay_copy(r, i, y2, core, part):
    rows, at = weight_rows(r, y2, core, part), part * r.nY + i
    return rcopy(rows, rows, r.sems[b.wz_s].at[at], r.sems[b.wz_r].at[at], r.y * 2 + 1 - r.k, r.c)


def weight_send(r, part):
    for i in range(1, r.nY):
        start(r, weight_copy(r, i, r.y, part))


def weight_relay(r, part):
    for i in range(1, r.nY):
        y2 = lax.rem(r.y + i, r.nY)
        weight_copy(r, i, y2, part).wait_recv()
        start(r, relay_copy(r, i, y2, r.k, part))


def take_hidden(r):
    half, cut = r.nX // 2, r.T // 2
    mine = r.wf.at[r.y, pl.ds(r.k * half, half)]
    own_w = pltpu.make_async_copy(r.w_in, mine, r.sems[b.loc].at[0])
    own_h = pltpu.make_async_copy(r.hidden, r.hg.at[r.x, r.y], r.sems[b.loc].at[1])
    turn = rcopy(
        r.hidden, r.hg.at[r.x, r.y], r.sems[b.tu_s].at[0], r.sems[b.tu_r].at[0], r.z * 2 + r.k, r.y * r.nX + r.x
    )
    start(r, turn, r.y != r.z)
    start(r, pair_copy(r, r.w_in, mine, b.wp))
    own_w.start()
    pl.when(r.y == r.z)(own_h.start)
    need(r, b.gate_in, b.out_grad, b.a_log)

    gate = r.gate_in[...].astype(F32)
    sig = jax.nn.sigmoid(gate)
    grad = r.out_grad[...].astype(F32)
    r.g[...] = grad * (gate * sig)
    r.gs[...] = grad * (sig * (1.0 + gate * (1.0 - sig)))
    r.am[...] = -jnp.exp(r.a_log[...])
    r.part[:, :, pl.ds(r.R, LANES)] = jnp.zeros((r.nC, r.RP, LANES), F32)
    r.part2[:, :, pl.ds(r.R, LANES)] = jnp.zeros((r.nC, r.RP, LANES), F32)
    own_w.wait()
    pl.when(r.y == r.z)(own_h.wait)

    @pl.when(r.y != r.z)
    def _():
        rcopy(
            r.hidden, r.hg.at[r.x, r.z], r.sems[b.tu_s].at[0], r.sems[b.tu_r].at[0], r.z * 2 + r.k, r.y * r.nX + r.x
        ).wait_recv()

    low, high = pl.ds(0, cut), pl.ds(cut, r.T - cut)
    for i in range(1, r.nX):
        start(r, plane_copy(r, i, True, r.hg.at[r.x, r.z, low], r.hg.at[r.x, r.z, low], b.g1, r.x))
        start(r, plane_copy(r, i, False, r.hg.at[r.x, r.z, high], r.hg.at[r.x, r.z, high], b.g1, r.z))
    weight_send(r, 0)
    for i in range(1, r.nX):
        x2, z2 = lax.rem(r.x + i, r.nX), lax.rem(r.z + i, r.nY)
        plane_copy(r, i, True, r.hg.at[x2, r.z, low], r.hg.at[x2, r.z, low], b.g1, x2).wait_recv()
        plane_copy(r, i, False, r.hg.at[r.x, z2, high], r.hg.at[r.x, z2, high], b.g1, z2).wait_recv()
    for i in range(1, r.nX):
        start(r, plane_copy(r, i, False, r.hg.at[:, r.z, low], r.hg.at[:, r.z, low], b.g2, r.z))
        start(r, plane_copy(r, i, True, r.hg.at[r.x, :, high], r.hg.at[r.x, :, high], b.g2, r.x))
    pair_copy(r, r.w_in, r.wf.at[r.y, pl.ds((1 - r.k) * half, half)], b.wp).wait_recv()
    for i in range(1, r.nX):
        x2, z2 = lax.rem(r.x + i, r.nX), lax.rem(r.z + i, r.nY)
        plane_copy(r, i, True, r.hg.at[x2, :, high], r.hg.at[x2, :, high], b.g2, x2).wait_recv()
        plane_copy(r, i, False, r.hg.at[:, z2, low], r.hg.at[:, z2, low], b.g2, z2).wait_recv()


def tail_copy(r, i, y2, slot):
    return rcopy(
        r.xs.at[i, pl.ds(r.T - HALO, HALO)],
        r.xt.at[slot],
        r.sems[b.tail_s].at[i],
        r.sems[b.tail_r].at[slot],
        y2 * 2 + r.k + 1,
        r.c,
    )


def project(r):
    for i in range(1, r.nY + 1):
        y2 = lax.rem(r.y + i, r.nY)
        total = None
        for j in range(r.nX):
            term = dot(r.hg[j, y2], r.wf[r.y, j])
            total = term if total is None else total + term
        r.xs[i - 1] = total.astype(BF16)
        if i < r.nY:
            start(r, line_copy(r, i, r.xs.at[i - 1], r.xr.at[r.y], b.xr, r.y))
        start(r, tail_copy(r, i - 1, y2, r.y), y2 * 2 + r.k + 1 < r.nS)
    own = total

    @pl.when(r.s == 0)
    def _():
        r.xpad[pl.ds(0, HALO), :] = jnp.zeros((HALO, r.C), F32)

    @pl.when(r.s > 0)
    def _():
        tail = None
        for y2 in range(r.nY):
            tail_copy(r, 0, r.y, y2).wait_recv()
            term = r.xt[y2].astype(F32)
            tail = term if tail is None else tail + term
        r.xpad[pl.ds(0, HALO), :] = tail.astype(BF16).astype(F32)

    for i in range(1, r.nY):
        y2 = lax.rem(r.y + i, r.nY)
        line_copy(r, i, r.xs.at[i - 1], r.xr.at[y2], b.xr, y2).wait_recv()
        own = own + r.xr[y2].astype(F32)
    r.xpad[pl.ds(HALO, r.T), :] = own.astype(BF16).astype(F32)
    need(r, b.conv_w, b.conv_b, b.w_delta_in, b.w_bc)
    conv = jnp.zeros((r.T, r.C), F32) + r.conv_b[...]
    for k in range(r.KC):
        conv = conv + r.conv_w[k : k + 1, :] * r.xpad[pl.ds(HALO - r.KC + 1 + k, r.T), :]
    sig = jax.nn.sigmoid(conv)
    u = (conv * sig).astype(BF16)
    r.u[...] = u
    r.part[:, :, pl.ds(0, r.R)] = contract_last(u, r.w_delta_in[...]).reshape(r.nC, r.RP, r.R)
    r.part[:, :, pl.ds(r.R, 2 * r.N)] = contract_last(u, r.w_bc[...]).reshape(r.nC, r.RP, 2 * r.N)
    scatter_start(r, b.chan, r.part, r.part_r, b.p1)
    weight_send(r, 1)
    weight_relay(r, 0)
    r.slope[...] = sig * (1.0 + conv * (1.0 - sig))
    r.part_a[r.c] = scatter_sum(r, b.chan, r.part, r.part_r, b.p1)
    gather_start(r, b.chan, r.part_a, b.p2)
    recv_wait(r, b.chan, r.part_a, b.p2)
    full = r.part_a[...].reshape(r.T, r.R + LANES)
    r.low[...] = full[:, : r.R].astype(BF16)
    r.bcw[...] = full[:, r.R :]


def wide(r, b):
    return jnp.concatenate([b] * (r.C // LANES), axis=1) if r.C > LANES else b


def block_mask(r, rows):
    row = lax.broadcasted_iota(jnp.int32, (rows, CH * r.N), 0)
    col = lax.broadcasted_iota(jnp.int32, (rows, CH * r.N), 1)
    return jnp.where(lax.rem(row, CH) == lax.div(col, r.N), 1.0, 0.0).astype(F32)


def pick(r):
    row = lax.broadcasted_iota(jnp.int32, (r.N, CH * r.N), 0)
    col = lax.broadcasted_iota(jnp.int32, (r.N, CH * r.N), 1)
    return jnp.where(lax.rem(col, r.N) == row, 1.0, 0.0).astype(F32)


def prepare(r):
    need(r, b.w_dt, b.dt_bias, b.skip_d)
    pre = dot(r.low[...], r.w_dt[...]) + r.dt_bias[...]
    r.pre[...] = pre
    delta = softplus(pre)
    r.delta[...] = delta
    r.sd[...] = jnp.sum(delta, 0, keepdims=True)
    for i, j, dev in peers(r, b.seq):
        start(r, rcopy(r.sd, r.sd_r.at[r.s], r.sems[b.sd_s].at[i], r.sems[b.sd_r].at[r.s], *dev))
    u = r.u[...].astype(F32)
    r.du[...] = delta * u
    turned = r.bcw[...].T
    for t in range(r.T):
        r.bx[t] = jnp.broadcast_to(turned[0 : r.N, t : t + 1], (r.N, LANES))
        r.cx[t] = jnp.broadcast_to(turned[r.N : 2 * r.N, t : t + 1], (r.N, LANES))


def forward_chunk(r, j, h, kept):
    a_mat = r.am[...]
    base = pl.multiple_of(j * CH, CH)
    d = r.delta[pl.ds(base, CH), :]
    du = r.du[pl.ds(base, CH), :]
    for t in range(CH):
        at = pl.multiple_of((base + t) * r.N, r.N)
        if kept is None:
            a = jnp.exp(d[t : t + 1, :] * a_mat)
            r.aa[pl.ds(at, r.N), :] = a
        else:
            a = r.aa[pl.ds(at, r.N), :]
        h = a * h + du[t : t + 1, :] * wide(r, r.bx[base + t])
        if kept is not None:
            r.hh[pl.ds(at + r.N, r.N), :] = h
            kept[pl.ds(t * r.N, r.N), :] = h.astype(BF16)
    return h


def forward_sums(r, j, kept, mask):
    rows = pl.ds(pl.multiple_of(j * CH, CH), CH)
    states = kept[...]
    r.y_scan[rows, :] = dot(r.cd[rows, :], states)
    r.cm[rows, :] = mask * contract_last(r.g[rows, :].astype(BF16), states)


def forward_free(r):
    return lax.fori_loop(0, r.T // CH, lambda j, h: forward_chunk(r, j, h, None), jnp.zeros((r.N, r.C), F32))


def forward_full(r):
    mask = block_mask(r, CH)
    r.hh[pl.ds(0, r.N), :] = r.h_in[...]
    r.kept1[...] = jnp.zeros_like(r.kept1)

    def two(i, h):
        forward_sums(r, jnp.maximum(2 * i - 1, 0), r.kept1, mask)
        h = forward_chunk(r, 2 * i, h, r.kept0)
        forward_sums(r, 2 * i, r.kept0, mask)
        return forward_chunk(r, 2 * i + 1, h, r.kept1)

    lax.fori_loop(0, r.T // CH // 2, two, r.h_in[...])
    forward_sums(r, r.T // CH - 1, r.kept1, mask)


def backward_chunk(r, j, carry, kept):
    a_mat = r.am[...]
    base = pl.multiple_of(j * CH, CH)
    kap, acc = carry
    d = r.delta[pl.ds(base, CH), :]
    g = r.g[pl.ds(base, CH), :]
    for t in reversed(range(CH)):
        at = pl.multiple_of((base + t) * r.N, r.N)
        lam = kap + wide(r, r.cx[base + t]) * g[t : t + 1, :]
        kap = r.aa[pl.ds(at, r.N), :] * lam
        if kept is not None:
            q = kap * r.hh[pl.ds(at, r.N), :]
            acc = acc + q * d[t : t + 1, :]
            kept[0][pl.ds(t * r.N, r.N), :] = lam.astype(BF16)
            kept[1][pl.ds(t * r.N, r.N), :] = (q * a_mat).astype(BF16)
    return kap, acc


def backward_sums(r, j, kept, mask):
    rows = pl.ds(pl.multiple_of(j * CH, CH), CH)
    lam = kept[0][...]
    r.s1[rows, :] = dot(r.bd[rows, :], lam)
    r.s2[rows, :] = dot(mask.astype(BF16), kept[1][...])
    r.bm[rows, :] = mask * contract_last(r.du[rows, :].astype(BF16), lam)


def backward_free(r):
    zero = jnp.zeros((r.N, r.C), F32)
    last = r.T // CH - 1
    return lax.fori_loop(0, last + 1, lambda i, c: backward_chunk(r, last - i, c, None), (zero, zero))[0]


def backward_full(r):
    mask = block_mask(r, CH)
    last = r.T // CH - 1
    even, odd = (r.kept0, r.kept2), (r.kept1, r.kept3)
    for ref in odd:
        ref[...] = jnp.zeros_like(ref)

    def two(i, carry):
        backward_sums(r, jnp.minimum(last - 2 * i + 1, last), odd, mask)
        carry = backward_chunk(r, last - 2 * i, carry, even)
        backward_sums(r, last - 2 * i, even, mask)
        return backward_chunk(r, last - 2 * i - 1, carry, odd)

    a_adj = lax.fori_loop(0, r.T // CH // 2, two, (r.l_in[...], jnp.zeros((r.N, r.C), F32)))[1]
    backward_sums(r, 0, odd, mask)
    return a_adj


def state_copy(r, which, j, slot):
    return rcopy(r.ef.at[which], r.st_r.at[slot], r.sems[b.st_s].at[j], r.sems[b.st_r].at[slot], j, r.c)


def scan(r):
    zero = jnp.zeros((r.N, r.C), F32)
    r.ef[0] = forward_free(r).astype(BF16)
    for j in range(1, r.nS):
        start(r, state_copy(r, 0, j, r.s), j > r.s)
    r.ef[1] = backward_free(r).astype(BF16)
    for j in range(r.nS - 1):
        start(r, state_copy(r, 1, j, r.s), j < r.s)
    picked = pick(r)
    tall = block_mask(r, r.T)
    r.bd[...] = (tall * dot(r.bcw[:, pl.ds(0, r.N)], picked)).astype(BF16)
    r.cd[...] = (tall * dot(r.bcw[:, pl.ds(r.N, r.N)], picked)).astype(BF16)

    def enter(j, into):
        rcopy(r.sd, r.sd_r.at[j], r.sems[b.sd_s].at[0], r.sems[b.sd_r].at[j], j, r.c).wait_recv()
        state_copy(r, 0, j, j).wait_recv()
        into[...] = jnp.exp(r.am[...] * r.sd_r[j]) * into[...] + r.st_r[j].astype(F32)

    r.h_in[...] = zero
    for j in range(r.nS - 1):
        pl.when(j < r.s)(functools.partial(enter, j, r.h_in))
    forward_full(r)
    r.l_in[...] = zero
    for j in range(r.nS - 1, 0, -1):
        pl.when(j > r.s)(functools.partial(enter, j, r.l_in))
    r.ug[r.y] = r.u[...]
    for i in range(1, r.nY):
        start(r, line_copy(r, i, r.ug.at[r.y], r.ug.at[r.y], b.ug, r.y))
    a_adj = backward_full(r)
    s1 = r.s1[...]
    u = r.u[...].astype(F32)
    pre_adj = ((u * s1 + r.s2[...]) * jax.nn.sigmoid(r.pre[...])).astype(BF16)
    exact = lax.Precision.HIGHEST
    nt = (((1,), (1,)), ((), ()))
    b_adj = lax.dot_general(r.bm[...], picked, nt, precision=exact, preferred_element_type=F32)
    c_adj = lax.dot_general(r.cm[...], picked, nt, precision=exact, preferred_element_type=F32)
    r.part2[:, :, pl.ds(0, r.R)] = contract_last(pre_adj, r.w_dt[...]).reshape(r.nC, r.RP, r.R)
    r.part2[:, :, pl.ds(r.R, r.N)] = b_adj.reshape(r.nC, r.RP, r.N)
    r.part2[:, :, pl.ds(r.R + r.N, r.N)] = c_adj.reshape(r.nC, r.RP, r.N)
    scatter_start(r, b.chan, r.part2, r.part2_r, b.p3)
    weight_relay(r, 1)
    r.dt_p[...] = contract_first(r.low[...], pre_adj).astype(BF16).reshape(2, r.nY, r.R // r.nS, r.C)
    start(r, pair_copy(r, r.dt_p.at[1 - r.k], r.dt_b, b.d1))
    alog = (a_adj * r.am[...]).astype(BF16)
    wide_half = r.C // 2
    for j in range(2):
        r.mi_p[j] = alog[:, j * wide_half : (j + 1) * wide_half]
    start(r, pair_copy(r, r.mi_p.at[1 - r.k], r.mi_b, b.m1))
    skip = r.skip_d[...]
    r.uu[...] = r.delta[...] * s1 + skip * r.g[...]
    r.gate_out[...] = (r.gs[...] * (r.y_scan[...] + skip * u)).astype(BF16)


def grad_copy(r, i, part):
    rows = pl.ds(part * (r.T // 2), r.T // 2)
    c2 = lax.rem(r.c + i, r.nC)
    at = part * r.nC
    return rcopy(
        r.hs.at[i, rows], r.hr.at[r.c, rows], r.sems[b.hg_s].at[at + i], r.sems[b.hg_r].at[at + r.c], r.s, c2
    )


def grad_part(r, part):
    rows = pl.ds(part * (r.T // 2), r.T // 2)
    for i in range(r.nC - 1, -1, -1):
        c2 = lax.rem(r.c + i, r.nC)
        term = contract_last(r.xg[r.y, rows], r.wf[lax.div(c2, r.nX), lax.rem(c2, r.nX)])
        r.hs[i, rows] = term.astype(BF16)
        if i:
            start(r, grad_copy(r, i, part))


def weight_pair(r, part, got, summed, key):
    pair_copy(r, part.at[1 - r.k], got, key[0]).wait_recv()
    summed[...] = (part[r.k].astype(F32) + got[...].astype(F32)).astype(BF16)


def weight_line(r, summed, got, whole, keys):
    total = summed[r.y].astype(F32)
    for i in range(1, r.nY):
        y2 = lax.rem(r.y + i, r.nY)
        line_copy(r, i, summed.at[y2], got.at[y2], keys[0], y2).wait_recv()
        total = total + got[y2].astype(F32)
    whole[r.k, r.y] = total.astype(BF16)
    for i in range(1, r.nY):
        start(r, line_copy(r, i, whole.at[r.k, r.y], whole.at[r.k, r.y], keys[1], r.y))


def weight_back(r, whole, line_key, pair_key):
    for i in range(1, r.nY):
        y2 = lax.rem(r.y + i, r.nY)
        line_copy(r, i, whole.at[r.k, y2], whole.at[r.k, y2], line_key, y2).wait_recv()
    start(r, pair_copy(r, whole.at[r.k], whole.at[r.k], pair_key))


def weight_end(r, whole, pair_key):
    pair_copy(r, whole.at[r.k], whole.at[1 - r.k], pair_key).wait_recv()


def spread(r, summed, got, key):
    for i in range(1, r.nY):
        start(r, line_copy(r, i, summed.at[lax.rem(r.y + i, r.nY)], got.at[r.y], key, r.y))


def gradients(r):
    half = r.nX // 2
    wide_half = r.C // 2
    flush(r)
    r.part2_a[r.c] = scatter_sum(r, b.chan, r.part2, r.part2_r, b.p3)
    gather_start(r, b.chan, r.part2_a, b.p4)
    weight_pair(r, r.dt_p, r.dt_b, r.dt_c, (b.d1,))
    spread(r, r.dt_c, r.dt_d, b.d2)
    pair_copy(r, r.mi_p.at[1 - r.k], r.mi_b, b.m1).wait_recv()
    r.mi_c[r.y] = (r.mi_p[r.k].astype(F32) + r.mi_b[...].astype(F32)).astype(BF16)
    for i in range(1, r.nY):
        start(r, line_copy(r, i, r.mi_c.at[r.y], r.mi_c.at[r.y], b.m2, r.y))
    recv_wait(r, b.chan, r.part2_a, b.p4)
    full = r.part2_a[...].reshape(r.T, r.R + LANES)
    r.lg[r.y] = full.astype(BF16)
    for i in range(1, r.nY):
        start(r, line_copy(r, i, r.lg.at[r.y], r.lg.at[r.y], b.lg, r.y))
    low_adj = full[:, : r.R].astype(BF16)
    bc_adj = full[:, r.R : r.R + 2 * r.N].astype(BF16)
    u_adj = r.uu[...] + dot(low_adj, r.w_delta_in[...]) + dot(bc_adj, r.w_bc[...])
    conv_adj = u_adj * r.slope[...]
    r.cpad[pl.ds(0, r.T), :] = conv_adj

    def head_copy(to):
        return rcopy(
            r.cpad.at[pl.ds(0, HEAD)],
            r.cpad.at[pl.ds(r.T, HEAD)],
            r.sems[b.head_s].at[0],
            r.sems[b.head_r].at[0],
            to,
            r.c,
        )

    start(r, head_copy(r.s - 1), r.s > 0)

    @pl.when(r.s == r.nS - 1)
    def _():
        r.cpad[pl.ds(r.T, HEAD), :] = jnp.zeros((HEAD, r.C), F32)

    def x_adj(first, count):
        rows = pl.ds(first, count)
        total = jnp.zeros((count, r.C), F32)
        for k in range(r.KC):
            total = total + r.conv_w[k : k + 1, :] * r.cpad[pl.ds(first + r.KC - 1 - k, count), :]
        r.xg[r.y, rows] = total.astype(BF16)

    def x_copy(i, slot, part):
        rows = pl.ds(part * (r.T // 2), r.T // 2)
        return line_copy(r, i, r.xg.at[slot, rows], r.xg.at[slot, rows], b.xg, slot, part)

    x_adj(0, r.T // 2)
    for i in range(1, r.nY):
        start(r, x_copy(i, r.y, 0))
    for part in range(2):
        for i in range(1, r.nY):
            relay_copy(r, i, lax.rem(r.y + i, r.nY), 1 - r.k, part).wait_recv()
    grad_part(r, 0)
    weight_line(r, r.dt_c, r.dt_d, r.dt_e, (b.d2, b.d3))
    pl.when(r.s < r.nS - 1)(lambda: head_copy(r.s + 1).wait_recv())
    x_adj(r.T // 2, r.T // 2)
    for i in range(1, r.nY):
        start(r, x_copy(i, r.y, 1))
    grad_part(r, 1)
    total = None
    for y2 in range(r.nY):
        pl.when(r.y != y2)(
            line_copy(r, 1, r.mi_c.at[y2], r.mi_c.at[y2], b.m2, y2).wait_recv
        )
        term = r.mi_c[y2].astype(F32)
        total = term if total is None else total + term
    r.mi_e[r.k] = total
    start(r, pair_copy(r, r.mi_e.at[r.k], r.mi_e.at[r.k], b.m3))
    weight_back(r, r.dt_e, b.d3, b.d4)
    for i in range(1, r.nY):
        y2 = lax.rem(r.y + i, r.nY)
        line_copy(r, i, r.ug.at[y2], r.ug.at[y2], b.ug, y2).wait_recv()
        line_copy(r, i, r.lg.at[y2], r.lg.at[y2], b.lg, y2).wait_recv()
    tokens = r.nY * r.T
    term = contract_first(r.lg[...].reshape(tokens, r.R + LANES), r.ug[...].reshape(tokens, r.C))
    r.li_p[...] = term[: r.R + 2 * r.N].astype(BF16)
    start(r, pair_copy(r, r.li_p, r.li_b, b.d5))
    for i in range(1, r.nY):
        y2 = lax.rem(r.y + i, r.nY)
        x_copy(i, y2, 0).wait_recv()
        x_copy(i, y2, 1).wait_recv()

    x_all = r.xg[...].reshape(r.nY * r.T, r.C)

    def weight(x2):
        return contract_first(r.hg[x2].reshape(r.nY * r.T, r.DH), x_all)

    for j in range(half):
        r.ws[j] = weight((1 - r.k) * half + j).astype(BF16)
    start(r, pair_copy(r, r.ws, r.wr, b.wg))
    for j in range(half):
        r.wo[j] = weight(r.k * half + j)
    pair_copy(r, r.ws, r.wr, b.wg).wait_recv()
    r.w_out[...] = (r.wo[...] + r.wr[...].astype(F32)).astype(BF16)
    weight_end(r, r.dt_e, b.d4)
    pair_copy(r, r.mi_e.at[r.k], r.mi_e.at[1 - r.k], b.m3).wait_recv()
    total = r.hs[0].astype(F32)
    for i, c2, dev in peers(r, b.chan):
        for part in range(2):
            rows, at = pl.ds(part * (r.T // 2), r.T // 2), part * r.nC + c2
            got = r.hr.at[c2, rows]
            rcopy(got, got, r.sems[b.hg_s].at[i], r.sems[b.hg_r].at[at], *dev).wait_recv()
        total = total + r.hr[c2].astype(F32)
    r.hidden_out[...] = total.astype(BF16)
    pair_copy(r, r.li_p, r.li_b, b.d5).wait_recv()
    r.li_e[...] = r.li_p[...].astype(F32) + r.li_b[...].astype(F32)
    flush(r)


def finish(r):
    scale = 1.0 / math.sqrt(r.T * r.nS)
    wide_half = r.C // 2
    r.hidden_grad[...] = r.hidden_out[...]
    r.gate_grad[...] = r.gate_out[...]
    r.w_in_grad[...] = r.w_out[...].astype(F32) * scale
    r.w_dt_grad[...] = r.dt_e[...].astype(F32).reshape(r.R, r.C) * scale
    r.w_delta_in_grad[...] = r.li_e[pl.ds(0, r.R), :] * scale
    r.w_bc_grad[...] = r.li_e[pl.ds(r.R, 2 * r.N), :] * scale
    for j in range(2):
        cols = pl.ds(j * wide_half, wide_half)
        r.a_log_grad[:, cols] = r.mi_e[j] * scale


def tables(dim):
    d = types.SimpleNamespace(**dim)
    t, c, n, rows, q = d.T, d.C, d.N, d.R, d.R // d.nS
    wide_row = rows + LANES
    buffers = dict(
        hg=((d.nX, d.nY, t, d.DH), BF16),
        wf=((d.nY, d.nX, d.DH, c), BF16),
        xs=((d.nY, t, c), BF16),
        xr=((d.nY, t, c), BF16),
        xt=((d.nY, HALO, c), BF16),
        xpad=((HALO + t, c), F32),
        slope=((t, c), F32),
        gs=((t, c), F32),
        u=((t, c), BF16),
        part=((d.nC, d.RP, wide_row), F32),
        part_r=((d.nC, d.RP, wide_row), F32),
        part_a=((d.nC, d.RP, wide_row), F32),
        low=((t, rows), BF16),
        bcw=((t, LANES), F32),
        pre=((t, c), F32),
        delta=((t, c), F32),
        du=((t, c), F32),
        g=((t, c), F32),
        am=((n, c), F32),
        bx=((t, n, LANES), F32),
        cx=((t, n, LANES), F32),
        sd=((1, c), F32),
        aa=((t * n, c), F32),
        hh=(((t + 1) * n, c), F32),
        ef=((2, n, c), BF16),
        st_r=((d.nS, n, c), BF16),
        sd_r=((d.nS, 1, c), F32),
        kept0=((CH * n, c), BF16),
        kept1=((CH * n, c), BF16),
        kept2=((CH * n, c), BF16),
        kept3=((CH * n, c), BF16),
        h_in=((n, c), F32),
        l_in=((n, c), F32),
        bd=((t, CH * n), BF16),
        cd=((t, CH * n), BF16),
        bm=((t, CH * n), F32),
        cm=((t, CH * n), F32),
        y_scan=((t, c), F32),
        s1=((t, c), F32),
        s2=((t, c), F32),
        uu=((t, c), F32),
        part2=((d.nC, d.RP, wide_row), F32),
        part2_r=((d.nC, d.RP, wide_row), F32),
        part2_a=((d.nC, d.RP, wide_row), F32),
        dt_p=((2, d.nY, q, c), BF16),
        dt_b=((d.nY, q, c), BF16),
        dt_c=((d.nY, q, c), BF16),
        dt_d=((d.nY, q, c), BF16),
        dt_e=((2, d.nY, q, c), BF16),
        ug=((d.nY, t, c), BF16),
        lg=((d.nY, t, wide_row), BF16),
        li_p=((rows + 2 * n, c), BF16),
        li_b=((rows + 2 * n, c), BF16),
        li_e=((rows + 2 * n, c), F32),
        mi_p=((2, n, c // 2), BF16),
        mi_b=((n, c // 2), BF16),
        mi_c=((d.nY, n, c // 2), BF16),
        mi_e=((2, n, c // 2), F32),
        cpad=((t + HEAD, c), F32),
        xg=((d.nY, t, c), BF16),
        hs=((d.nC, t, d.DH), BF16),
        hr=((d.nC, t, d.DH), BF16),
        ws=((d.nX // 2, d.DH, c), BF16),
        wr=((d.nX // 2, d.DH, c), BF16),
        wo=((d.nX // 2, d.DH, c), F32),
        w_out=((d.nX // 2, d.DH, c), BF16),
        hidden_out=((t, d.DH), BF16),
        gate_out=((t, c), BF16),
        hidden_grad=((t, d.DH), BF16),
        gate_grad=((t, c), BF16),
        w_in_grad=((d.nX // 2, d.DH, c), F32),
        w_delta_in_grad=((rows, c), F32),
        w_bc_grad=((2 * n, c), F32),
        w_dt_grad=((rows, c), F32),
        a_log_grad=((n, c), F32),
    )
    sems = dict(loc=2, inp=12)
    pairs = (b.tu, b.wp, b.head, b.wg, b.d1, b.d4, b.d5, b.m1, b.m3)
    lines = (b.xr, b.tail, b.d2, b.d3, b.m2, b.ug, b.lg)
    for key in pairs:
        sems[key + "_s"] = sems[key + "_r"] = 1
    for key in lines:
        sems[key + "_s"] = sems[key + "_r"] = d.nY
    for key in (b.xg, b.wy, b.wz):
        sems[key + "_s"] = sems[key + "_r"] = 2 * d.nY
    sems[b.hg_s] = sems[b.hg_r] = 2 * d.nC
    for key in (b.g1, b.g2):
        sems[key + "_s"] = sems[key + "_r"] = d.nX + d.nY
    for key in (b.p1, b.p2, b.p3, b.p4):
        sems[key + "_s"] = sems[key + "_r"] = d.nC
    for key in (b.st, b.sd):
        sems[key + "_s"] = sems[key + "_r"] = d.nS
    return buffers, sems


def run(dim, phases, remote, values, ins, outs, scratch, sem_names, cost):
    buffers, sem_sizes = tables(dim)
    held = [name for name in ins if name not in (b.hidden, b.w_in)] if remote else []

    def body(*refs):
        r = types.SimpleNamespace(**dim)
        r.sent = []
        names = ins + outs + scratch
        for name, ref in zip(names, refs):
            setattr(r, name, ref)
        refs = refs[len(names) :]
        r.sems = dict(zip(sem_names, refs))
        if remote:
            r.given = {name: getattr(r, name) for name in ins}
            for name, ref in zip(held, refs[len(sem_names) :]):
                setattr(r, name, ref)
            r.s, r.c = lax.axis_index(b.seq), lax.axis_index(b.chan)
            r.y, r.k = lax.div(r.s, 2), lax.rem(r.s, 2)
            r.z, r.x = lax.div(r.c, r.nX), lax.rem(r.c, r.nX)
            greet(r, functools.partial(load, r))
        for phase in phases:
            phase(r)

    space = pl.BlockSpec(memory_space=pltpu.VMEM)
    extra = dict(collective_id=0, has_side_effects=True) if remote else {}
    results = pl.pallas_call(
        body,
        out_shape=[jax.ShapeDtypeStruct(*buffers[name]) for name in outs],
        in_specs=[pl.BlockSpec(memory_space=pl.ANY) if remote else space] * len(ins),
        out_specs=[space] * len(outs),
        scratch_shapes=[pltpu.VMEM(*buffers[name]) for name in scratch]
        + [pltpu.SemaphoreType.DMA((sem_sizes[name],)) for name in sem_names]
        + [pltpu.VMEM(values[name].shape, values[name].dtype) for name in held],
        compiler_params=pltpu.CompilerParams(vmem_limit_bytes=56 << 20, **extra),
        cost_estimate=pl.CostEstimate(flops=cost, bytes_accessed=4 << 20, transcendentals=0),
        name=phases[-1].__name__,
    )(*[values[name] for name in ins])
    values.update(zip(outs, results))


ORDER = [b.hidden_grad, b.gate_grad, b.w_in_grad, b.w_delta_in_grad, b.w_bc_grad, b.w_dt_grad, b.a_log_grad]


def per_device(
    seq, chan, hidden, gate_in, out_grad, w_in, conv_w, conv_b, w_delta_in, w_bc, w_dt, dt_bias, a_log, skip_d
):
    lines = seq // 2
    dim = dict(
        nS=seq,
        nC=chan,
        nY=lines,
        nX=chan // lines,
        T=hidden.shape[0],
        DH=hidden.shape[1],
        C=w_in.shape[1],
        R=w_delta_in.shape[0],
        N=a_log.shape[0],
        KC=conv_w.shape[0],
        RP=hidden.shape[0] // chan,
    )
    v = dict(
        hidden=hidden,
        gate_in=gate_in,
        out_grad=out_grad,
        w_in=w_in.reshape(dim[b.nX] // 2, dim[b.DH], dim[b.C]),
        conv_w=conv_w,
        conv_b=conv_b[None],
        w_delta_in=w_delta_in,
        w_bc=w_bc,
        w_dt=w_dt,
        dt_bias=dt_bias[None],
        a_log=a_log,
        skip_d=skip_d[None],
    )
    raw = [b.hidden_out, b.gate_out, b.w_out, b.dt_e, b.li_e, b.mi_e]
    given = list(v)
    buffers, sems = tables(dim)
    scratch = [name for name in buffers if name not in given + raw + ORDER]
    phases = [take_hidden, project, prepare, scan, gradients]
    run(dim, phases, True, v, given, raw, scratch, list(sems), 2_000_000_000)
    run(dim, [finish], False, v, raw, ORDER, [], [], 1_000_000)
    v[b.w_in_grad] = v[b.w_in_grad].reshape(w_in.shape)
    return tuple(v[name] for name in ORDER)


def solution(mesh):
    placed = (
        P(b.seq, b.chan),
        P(b.seq, b.chan),
        P(b.seq, b.chan),
        P(b.seq, b.chan),
        P(None, b.chan),
        P(b.chan),
        P(None, b.chan),
        P(None, b.chan),
        P(None, b.chan),
        P(b.chan),
        P(None, b.chan),
        P(b.chan),
    )
    return jax.shard_map(
        functools.partial(per_device, mesh.shape[b.seq], mesh.shape[b.chan]),
        mesh=mesh,
        in_specs=placed,
        out_specs=(
            P(b.seq, b.chan),
            P(b.seq, b.chan),
            P(b.seq, b.chan),
            P(None, b.chan),
            P(None, b.chan),
            P(None, b.chan),
            P(None, b.chan),
        ),
        check_vma=False,
    )
```

```python
import functools
import math
import types

import jax
import jax.numpy as jnp
from jax import lax
from jax.experimental import pallas as pl
from jax.experimental.pallas import tpu as pltpu
from jax.sharding import PartitionSpec as P

MESH = pl.DeviceIdType.MESH


class Names:
    def __getattr__(self, name):
        return name


b = Names()
F32, BF16 = jnp.float32, jnp.bfloat16
CH = 16
LANES = 128
HALO = 16
HEAD = 8


def contract_last(left, right):
    return lax.dot_general(left, right, (((1,), (1,)), ((), ())), preferred_element_type=F32)


def contract_first(left, right):
    return lax.dot_general(left, right, (((0,), (0,)), ((), ())), preferred_element_type=F32)


def dot(left, right):
    return jnp.dot(left, right, preferred_element_type=F32)


def silu_slope(values):
    sig = jax.nn.sigmoid(values)
    return sig * (1.0 + values * (1.0 - sig))


def softplus(v):
    return jnp.maximum(v, 0.0) + jnp.log1p(jnp.exp(-jnp.abs(v)))


def rcopy(src, dst, send, recv, seq, chan):
    return pltpu.make_async_remote_copy(
        src_ref=src,
        dst_ref=dst,
        send_sem=send,
        recv_sem=recv,
        device_id=dict(seq=seq, chan=chan),
        device_id_type=MESH,
    )


def ring(r, group):
    if group == b.seq:
        return r.s, r.nS, lambda j: (j, r.c)
    return r.c, r.nC, lambda j: (r.s, j)


def peers(r, group):
    me, n, dev = ring(r, group)
    for i in range(1, n):
        j = lax.rem(me + i, n)
        yield i, j, dev(j)


def start(r, copy, when=None):
    r.sent.append((copy, when))
    if when is None:
        copy.start()
    else:
        pl.when(when)(copy.start)


def flush(r):
    for copy, when in r.sent:
        if when is None:
            copy.wait_send()
        else:
            pl.when(when)(copy.wait_send)
    r.sent.clear()


def scatter_start(r, group, src, dst, key):
    me = ring(r, group)[0]
    for i, j, dev in peers(r, group):
        start(r, rcopy(src.at[j], dst.at[me], r.sems[key + "_s"].at[i], r.sems[key + "_r"].at[me], *dev))


def gather_start(r, group, buf, key):
    me = ring(r, group)[0]
    for i, j, dev in peers(r, group):
        start(r, rcopy(buf.at[me], buf.at[me], r.sems[key + "_s"].at[i], r.sems[key + "_r"].at[me], *dev))


def recv_wait(r, group, buf, key):
    for i, j, dev in peers(r, group):
        rcopy(buf.at[j], buf.at[j], r.sems[key + "_s"].at[i], r.sems[key + "_r"].at[j], *dev).wait_recv()


def scatter_sum(r, group, src, dst, key):
    me = ring(r, group)[0]
    total = src[me].astype(F32)
    recv_wait(r, group, dst, key)
    for i, j, dev in peers(r, group):
        total = total + dst[j].astype(F32)
    return total


def pair_copy(r, src, dst, key):
    return rcopy(src, dst, r.sems[key + "_s"].at[0], r.sems[key + "_r"].at[0], r.y * 2 + 1 - r.k, r.c)


def line_copy(r, i, src, dst, key, slot, part=0):
    at = part * r.nY
    return rcopy(
        src,
        dst,
        r.sems[key + "_s"].at[at + i],
        r.sems[key + "_r"].at[at + slot],
        lax.rem(r.y + i, r.nY) * 2 + r.k,
        r.c,
    )


def plane_copy(r, i, along_x, src, dst, key, slot):
    at, seq = (0 if along_x else r.nX), r.s
    chan = r.z * r.nX + lax.rem(r.x + i, r.nX) if along_x else lax.rem(r.z + i, r.nY) * r.nX + r.x
    return rcopy(src, dst, r.sems[key + "_s"].at[at + i], r.sems[key + "_r"].at[at + slot], seq, chan)


def greet(r, during):
    barrier = pltpu.get_barrier_semaphore()

    def tell(seq, chan):
        pl.semaphore_signal(barrier, inc=1, device_id=dict(seq=seq, chan=chan), device_id_type=MESH)

    pl.when(r.y != r.z)(lambda: tell(r.z * 2 + r.k, r.y * r.nX + r.x))
    for i in range(1, r.nX):
        tell(r.s, r.z * r.nX + lax.rem(r.x + i, r.nX))
        tell(r.s, lax.rem(r.z + i, r.nY) * r.nX + r.x)
    for i, j, dev in peers(r, b.seq):
        tell(*dev)
    during()
    apart = (r.y - r.z) * (r.y - r.z)
    apart = lax.div(apart + r.nY * r.nY - 1, r.nY * r.nY)
    pl.semaphore_wait(barrier, 2 * (r.nX - 1) + r.nS - 1 + apart)


def load(r):
    for at, (name, ref) in enumerate(r.given.items()):
        if name in (b.w_in, b.hidden):
            continue
        pltpu.make_async_copy(ref, getattr(r, name), r.sems[b.inp].at[at]).start()


def need(r, *names):
    for name in names:
        at = list(r.given).index(name)
        pltpu.make_async_copy(r.given[name], getattr(r, name), r.sems[b.inp].at[at]).wait()


def pack(r, low, small):
    r.pad[:, pl.ds(0, 2 * r.N)] = small
    parts = [low[:, at : at + LANES] for at in range(0, r.R, LANES)] + [r.pad[...]]
    parts = [part.reshape(r.nC, r.RP, LANES) for part in parts]
    parts += [jnp.zeros_like(parts[0])] * (r.PR // r.RP - len(parts))
    return jnp.concatenate(parts, 1).astype(BF16)


def unpack(r, pieces):
    pieces = pieces.astype(F32)
    parts = [pieces[:, at : at + r.RP].reshape(r.T, LANES) for at in range(0, r.PR, r.RP)]
    count = r.R // LANES
    return jnp.concatenate(parts[:count], 1), parts[count]


def weight_rows(r, y2, core, part):
    half, cut = r.nX // 2, r.DH // 2
    return r.wf.at[y2, pl.ds(core * half, half), pl.ds(part * cut, cut)]


def weight_copy(r, i, y2, part):
    rows = weight_rows(r, y2, r.k, part)
    return line_copy(r, i, rows, rows, b.wy, y2, part)


def relay_copy(r, i, y2, core, part):
    rows, at = weight_rows(r, y2, core, part), part * r.nY + i
    return rcopy(rows, rows, r.sems[b.wz_s].at[at], r.sems[b.wz_r].at[at], r.y * 2 + 1 - r.k, r.c)


def weight_send(r, part):
    for i in range(1, r.nY):
        start(r, weight_copy(r, i, r.y, part))


def weight_relay(r, part):
    for i in range(1, r.nY):
        y2 = lax.rem(r.y + i, r.nY)
        weight_copy(r, i, y2, part).wait_recv()
        start(r, relay_copy(r, i, y2, r.k, part))


def take_hidden(r):
    half, cut = r.nX // 2, r.T // 2
    mine = r.wf.at[r.y, pl.ds(r.k * half, half)]
    own_w = pltpu.make_async_copy(r.w_in, mine, r.sems[b.loc].at[0])
    own_h = pltpu.make_async_copy(r.hidden, r.hg.at[r.x, r.y], r.sems[b.loc].at[1])
    turn = rcopy(
        r.hidden, r.hg.at[r.x, r.y], r.sems[b.tu_s].at[0], r.sems[b.tu_r].at[0], r.z * 2 + r.k, r.y * r.nX + r.x
    )
    start(r, turn, r.y != r.z)
    start(r, pair_copy(r, r.w_in, mine, b.wp))
    own_w.start()
    pl.when(r.y == r.z)(own_h.start)
    need(r, b.gate_in, b.out_grad, b.a_log)

    gate = r.gate_in[...].astype(F32)
    sig = jax.nn.sigmoid(gate)
    grad = r.out_grad[...].astype(F32)
    r.g[...] = grad * (gate * sig)
    r.gs[...] = grad * (sig * (1.0 + gate * (1.0 - sig)))
    r.am[...] = -jnp.exp(r.a_log[...])
    r.pad[...] = jnp.zeros_like(r.pad)
    own_w.wait()
    pl.when(r.y == r.z)(own_h.wait)

    @pl.when(r.y != r.z)
    def _():
        rcopy(
            r.hidden, r.hg.at[r.x, r.z], r.sems[b.tu_s].at[0], r.sems[b.tu_r].at[0], r.z * 2 + r.k, r.y * r.nX + r.x
        ).wait_recv()

    low, high = pl.ds(0, cut), pl.ds(cut, r.T - cut)
    for i in range(1, r.nX):
        start(r, plane_copy(r, i, True, r.hg.at[r.x, r.z, low], r.hg.at[r.x, r.z, low], b.g1, r.x))
        start(r, plane_copy(r, i, False, r.hg.at[r.x, r.z, high], r.hg.at[r.x, r.z, high], b.g1, r.z))
    weight_send(r, 0)
    for i in range(1, r.nX):
        x2, z2 = lax.rem(r.x + i, r.nX), lax.rem(r.z + i, r.nY)
        plane_copy(r, i, True, r.hg.at[x2, r.z, low], r.hg.at[x2, r.z, low], b.g1, x2).wait_recv()
        plane_copy(r, i, False, r.hg.at[r.x, z2, high], r.hg.at[r.x, z2, high], b.g1, z2).wait_recv()
    for i in range(1, r.nX):
        start(r, plane_copy(r, i, False, r.hg.at[:, r.z, low], r.hg.at[:, r.z, low], b.g2, r.z))
        start(r, plane_copy(r, i, True, r.hg.at[r.x, :, high], r.hg.at[r.x, :, high], b.g2, r.x))
    pair_copy(r, r.w_in, r.wf.at[r.y, pl.ds((1 - r.k) * half, half)], b.wp).wait_recv()
    for i in range(1, r.nX):
        x2, z2 = lax.rem(r.x + i, r.nX), lax.rem(r.z + i, r.nY)
        plane_copy(r, i, True, r.hg.at[x2, :, high], r.hg.at[x2, :, high], b.g2, x2).wait_recv()
        plane_copy(r, i, False, r.hg.at[:, z2, low], r.hg.at[:, z2, low], b.g2, z2).wait_recv()


def tail_copy(r, i, y2, slot):
    return rcopy(
        r.xs.at[i, pl.ds(r.T - HALO, HALO)],
        r.xt.at[slot],
        r.sems[b.tail_s].at[i],
        r.sems[b.tail_r].at[slot],
        y2 * 2 + r.k + 1,
        r.c,
    )


def project(r):
    for i in range(1, r.nY + 1):
        y2 = lax.rem(r.y + i, r.nY)
        total = None
        for j in range(r.nX):
            term = dot(r.hg[j, y2], r.wf[r.y, j])
            total = term if total is None else total + term
        r.xs[i - 1] = total.astype(BF16)
        if i < r.nY:
            start(r, line_copy(r, i, r.xs.at[i - 1], r.xr.at[r.y], b.xr, r.y))
        start(r, tail_copy(r, i - 1, y2, r.y), y2 * 2 + r.k + 1 < r.nS)
    own = total

    @pl.when(r.s == 0)
    def _():
        r.xpad[pl.ds(0, HALO), :] = jnp.zeros((HALO, r.C), F32)

    @pl.when(r.s > 0)
    def _():
        tail = None
        for y2 in range(r.nY):
            tail_copy(r, 0, r.y, y2).wait_recv()
            term = r.xt[y2].astype(F32)
            tail = term if tail is None else tail + term
        r.xpad[pl.ds(0, HALO), :] = tail.astype(BF16).astype(F32)

    for i in range(1, r.nY):
        y2 = lax.rem(r.y + i, r.nY)
        line_copy(r, i, r.xs.at[i - 1], r.xr.at[y2], b.xr, y2).wait_recv()
        own = own + r.xr[y2].astype(F32)
    r.xpad[pl.ds(HALO, r.T), :] = own.astype(BF16).astype(F32)
    need(r, b.conv_w, b.conv_b, b.w_delta_in, b.w_bc)
    conv = jnp.zeros((r.T, r.C), F32) + r.conv_b[...]
    for k in range(r.KC):
        conv = conv + r.conv_w[k : k + 1, :] * r.xpad[pl.ds(HALO - r.KC + 1 + k, r.T), :]
    sig = jax.nn.sigmoid(conv)
    u = (conv * sig).astype(BF16)
    r.u[...] = u
    r.part[...] = pack(r, contract_last(u, r.w_delta_in[...]), contract_last(u, r.w_bc[...]))
    scatter_start(r, b.chan, r.part, r.part_r, b.p1)
    weight_send(r, 1)
    weight_relay(r, 0)
    r.slope[...] = sig * (1.0 + conv * (1.0 - sig))
    r.part_a[r.c] = scatter_sum(r, b.chan, r.part, r.part_r, b.p1).astype(BF16)
    gather_start(r, b.chan, r.part_a, b.p2)
    recv_wait(r, b.chan, r.part_a, b.p2)
    low, r.bcw[...] = unpack(r, r.part_a[...])
    r.low[...] = low.astype(BF16)


def wide(r, b):
    return jnp.concatenate([b] * (r.C // LANES), axis=1) if r.C > LANES else b


def block_mask(r, rows):
    row = lax.broadcasted_iota(jnp.int32, (rows, CH * r.N), 0)
    col = lax.broadcasted_iota(jnp.int32, (rows, CH * r.N), 1)
    return jnp.where(lax.rem(row, CH) == lax.div(col, r.N), 1.0, 0.0).astype(F32)


def pick(r):
    row = lax.broadcasted_iota(jnp.int32, (r.N, CH * r.N), 0)
    col = lax.broadcasted_iota(jnp.int32, (r.N, CH * r.N), 1)
    return jnp.where(lax.rem(col, r.N) == row, 1.0, 0.0).astype(F32)


def prepare(r):
    need(r, b.w_dt, b.dt_bias, b.skip_d)
    pre = dot(r.low[...], r.w_dt[...]) + r.dt_bias[...]
    r.pre[...] = pre
    delta = softplus(pre)
    r.delta[...] = delta
    r.sd[...] = jnp.sum(delta, 0, keepdims=True)
    for i, j, dev in peers(r, b.seq):
        start(r, rcopy(r.sd, r.sd_r.at[r.s], r.sems[b.sd_s].at[i], r.sems[b.sd_r].at[r.s], *dev))
    u = r.u[...].astype(F32)
    r.du[...] = delta * u
    turned = r.bcw[...].T
    for t in range(r.T):
        r.bx[t] = jnp.broadcast_to(turned[0 : r.N, t : t + 1], (r.N, LANES))


def forward_chunk(r, j, h, kept):
    a_mat = r.am[...]
    base = pl.multiple_of(j * CH, CH)
    d = r.delta[pl.ds(base, CH), :]
    du = r.du[pl.ds(base, CH), :]
    for t in range(CH):
        at = pl.multiple_of((base + t) * r.N, r.N)
        if kept is None:
            a = jnp.exp(d[t : t + 1, :] * a_mat)
            r.aa[pl.ds(at, r.N), :] = a
        else:
            a = r.aa[pl.ds(at, r.N), :]
        h = a * h + du[t : t + 1, :] * wide(r, r.bx[base + t])
        if kept is not None:
            r.hh[pl.ds(at + r.N, r.N), :] = h
            kept[pl.ds(t * r.N, r.N), :] = h.astype(BF16)
    return h


def forward_sums(r, j, kept, mask):
    rows = pl.ds(pl.multiple_of(j * CH, CH), CH)
    states = kept[...]
    r.y_scan[rows, :] = dot(r.cd[rows, :], states)
    r.cm[rows, :] = mask * contract_last(r.g[rows, :].astype(BF16), states)


def forward_free(r):
    return lax.fori_loop(0, r.T // CH, lambda j, h: forward_chunk(r, j, h, None), jnp.zeros((r.N, r.C), F32))


def forward_full(r):
    mask = block_mask(r, CH)
    r.hh[pl.ds(0, r.N), :] = r.h_in[...]
    r.kept1[...] = jnp.zeros_like(r.kept1)

    def two(i, h):
        forward_sums(r, jnp.maximum(2 * i - 1, 0), r.kept1, mask)
        h = forward_chunk(r, 2 * i, h, r.kept0)
        forward_sums(r, 2 * i, r.kept0, mask)
        return forward_chunk(r, 2 * i + 1, h, r.kept1)

    lax.fori_loop(0, r.T // CH // 2, two, r.h_in[...])
    forward_sums(r, r.T // CH - 1, r.kept1, mask)


def backward_chunk(r, j, carry, kept):
    a_mat = r.am[...]
    base = pl.multiple_of(j * CH, CH)
    kap, acc = carry
    d = r.delta[pl.ds(base, CH), :]
    g = r.g[pl.ds(base, CH), :]
    for t in reversed(range(CH)):
        at = pl.multiple_of((base + t) * r.N, r.N)
        lam = kap + wide(r, r.cx[base + t]) * g[t : t + 1, :]
        kap = r.aa[pl.ds(at, r.N), :] * lam
        if kept is not None:
            q = kap * r.hh[pl.ds(at, r.N), :]
            acc = acc + q * d[t : t + 1, :]
            kept[0][pl.ds(t * r.N, r.N), :] = lam.astype(BF16)
            kept[1][pl.ds(t * r.N, r.N), :] = (q * a_mat).astype(BF16)
    return kap, acc


def backward_sums(r, j, kept, mask):
    rows = pl.ds(pl.multiple_of(j * CH, CH), CH)
    lam = kept[0][...]
    r.s1[rows, :] = dot(r.bd[rows, :], lam)
    r.s2[rows, :] = dot(mask.astype(BF16), kept[1][...])
    r.bm[rows, :] = mask * contract_last(r.du[rows, :].astype(BF16), lam)


def backward_free(r):
    zero = jnp.zeros((r.N, r.C), F32)
    last = r.T // CH - 1
    return lax.fori_loop(0, last + 1, lambda i, c: backward_chunk(r, last - i, c, None), (zero, zero))[0]


def backward_full(r):
    mask = block_mask(r, CH)
    last = r.T // CH - 1
    even, odd = (r.kept0, r.kept2), (r.kept1, r.kept3)
    for ref in odd:
        ref[...] = jnp.zeros_like(ref)

    def two(i, carry):
        backward_sums(r, jnp.minimum(last - 2 * i + 1, last), odd, mask)
        carry = backward_chunk(r, last - 2 * i, carry, even)
        backward_sums(r, last - 2 * i, even, mask)
        return backward_chunk(r, last - 2 * i - 1, carry, odd)

    a_adj = lax.fori_loop(0, r.T // CH // 2, two, (r.l_in[...], jnp.zeros((r.N, r.C), F32)))[1]
    backward_sums(r, 0, odd, mask)
    return a_adj


def state_copy(r, which, j, slot):
    return rcopy(r.ef.at[which], r.st_r.at[slot], r.sems[b.st_s].at[j], r.sems[b.st_r].at[slot], j, r.c)


def scan(r):
    zero = jnp.zeros((r.N, r.C), F32)
    r.ef[0] = forward_free(r).astype(BF16)
    for j in range(1, r.nS):
        start(r, state_copy(r, 0, j, r.s), j > r.s)
    turned = r.bcw[...].T
    for t in range(r.T):
        r.cx[t] = jnp.broadcast_to(turned[r.N : 2 * r.N, t : t + 1], (r.N, LANES))
    r.ef[1] = backward_free(r).astype(BF16)
    for j in range(r.nS - 1):
        start(r, state_copy(r, 1, j, r.s), j < r.s)
    picked = pick(r)
    tall = block_mask(r, r.T)
    r.bd[...] = (tall * dot(r.bcw[:, pl.ds(0, r.N)], picked)).astype(BF16)
    r.cd[...] = (tall * dot(r.bcw[:, pl.ds(r.N, r.N)], picked)).astype(BF16)

    def enter(j, into):
        rcopy(r.sd, r.sd_r.at[j], r.sems[b.sd_s].at[0], r.sems[b.sd_r].at[j], j, r.c).wait_recv()
        state_copy(r, 0, j, j).wait_recv()
        into[...] = jnp.exp(r.am[...] * r.sd_r[j]) * into[...] + r.st_r[j].astype(F32)

    r.h_in[...] = zero
    for j in range(r.nS - 1):
        pl.when(j < r.s)(functools.partial(enter, j, r.h_in))
    forward_full(r)
    r.l_in[...] = zero
    for j in range(r.nS - 1, 0, -1):
        pl.when(j > r.s)(functools.partial(enter, j, r.l_in))
    r.ug[r.y] = r.u[...]
    for i in range(1, r.nY):
        start(r, line_copy(r, i, r.ug.at[r.y], r.ug.at[r.y], b.ug, r.y))
    a_adj = backward_full(r)
    s1 = r.s1[...]
    u = r.u[...].astype(F32)
    pre_adj = ((u * s1 + r.s2[...]) * jax.nn.sigmoid(r.pre[...])).astype(BF16)
    exact = lax.Precision.HIGHEST
    nt = (((1,), (1,)), ((), ()))
    b_adj = lax.dot_general(r.bm[...], picked, nt, precision=exact, preferred_element_type=F32)
    c_adj = lax.dot_general(r.cm[...], picked, nt, precision=exact, preferred_element_type=F32)
    r.part2[...] = pack(r, contract_last(pre_adj, r.w_dt[...]), jnp.concatenate([b_adj, c_adj], 1))
    scatter_start(r, b.chan, r.part2, r.part2_r, b.p3)
    weight_relay(r, 1)
    r.dt_p[...] = contract_first(r.low[...], pre_adj).astype(BF16).reshape(2, r.nY, r.R // r.nS, r.C)
    start(r, pair_copy(r, r.dt_p.at[1 - r.k], r.dt_b, b.d1))
    alog = (a_adj * r.am[...]).astype(BF16)
    wide_half = r.C // 2
    for j in range(2):
        r.mi_p[j] = alog[:, j * wide_half : (j + 1) * wide_half]
    start(r, pair_copy(r, r.mi_p.at[1 - r.k], r.mi_b, b.m1))
    skip = r.skip_d[...]
    r.uu[...] = r.delta[...] * s1 + skip * r.g[...]
    r.gate_out[...] = (r.gs[...] * (r.y_scan[...] + skip * u)).astype(BF16)


def grad_copy(r, i, part):
    rows = pl.ds(part * (r.T // 2), r.T // 2)
    c2 = lax.rem(r.c + i, r.nC)
    at = part * r.nC
    return rcopy(
        r.hs.at[i, rows], r.hr.at[r.c, rows], r.sems[b.hg_s].at[at + i], r.sems[b.hg_r].at[at + r.c], r.s, c2
    )


def grad_part(r, part):
    rows = pl.ds(part * (r.T // 2), r.T // 2)
    for i in range(r.nC - 1, -1, -1):
        c2 = lax.rem(r.c + i, r.nC)
        term = contract_last(r.xg[r.y, rows], r.wf[lax.div(c2, r.nX), lax.rem(c2, r.nX)])
        r.hs[i, rows] = term.astype(BF16)
        if i:
            start(r, grad_copy(r, i, part))


def weight_pair(r, part, got, summed, key):
    pair_copy(r, part.at[1 - r.k], got, key[0]).wait_recv()
    summed[...] = (part[r.k].astype(F32) + got[...].astype(F32)).astype(BF16)


def weight_line(r, summed, got, whole, keys):
    total = summed[r.y].astype(F32)
    for i in range(1, r.nY):
        y2 = lax.rem(r.y + i, r.nY)
        line_copy(r, i, summed.at[y2], got.at[y2], keys[0], y2).wait_recv()
        total = total + got[y2].astype(F32)
    whole[r.k, r.y] = total.astype(BF16)
    for i in range(1, r.nY):
        start(r, line_copy(r, i, whole.at[r.k, r.y], whole.at[r.k, r.y], keys[1], r.y))


def weight_back(r, whole, line_key, pair_key):
    for i in range(1, r.nY):
        y2 = lax.rem(r.y + i, r.nY)
        line_copy(r, i, whole.at[r.k, y2], whole.at[r.k, y2], line_key, y2).wait_recv()
    start(r, pair_copy(r, whole.at[r.k], whole.at[r.k], pair_key))


def weight_end(r, whole, pair_key):
    pair_copy(r, whole.at[r.k], whole.at[1 - r.k], pair_key).wait_recv()


def spread(r, summed, got, key):
    for i in range(1, r.nY):
        start(r, line_copy(r, i, summed.at[lax.rem(r.y + i, r.nY)], got.at[r.y], key, r.y))


def gradients(r):
    half = r.nX // 2
    wide_half = r.C // 2
    flush(r)
    r.part2_a[r.c] = scatter_sum(r, b.chan, r.part2, r.part2_r, b.p3).astype(BF16)
    gather_start(r, b.chan, r.part2_a, b.p4)
    weight_pair(r, r.dt_p, r.dt_b, r.dt_c, (b.d1,))
    spread(r, r.dt_c, r.dt_d, b.d2)
    pair_copy(r, r.mi_p.at[1 - r.k], r.mi_b, b.m1).wait_recv()
    r.mi_c[r.y] = (r.mi_p[r.k].astype(F32) + r.mi_b[...].astype(F32)).astype(BF16)
    for i in range(1, r.nY):
        start(r, line_copy(r, i, r.mi_c.at[r.y], r.mi_c.at[r.y], b.m2, r.y))
    recv_wait(r, b.chan, r.part2_a, b.p4)
    full = jnp.concatenate(unpack(r, r.part2_a[...]), 1).astype(BF16)
    r.lg[r.y] = full
    for i in range(1, r.nY):
        start(r, line_copy(r, i, r.lg.at[r.y], r.lg.at[r.y], b.lg, r.y))
    low_adj = full[:, : r.R]
    bc_adj = full[:, r.R : r.R + 2 * r.N]
    u_adj = r.uu[...] + dot(low_adj, r.w_delta_in[...]) + dot(bc_adj, r.w_bc[...])
    conv_adj = u_adj * r.slope[...]
    r.cpad[pl.ds(0, r.T), :] = conv_adj

    def head_copy(to):
        return rcopy(
            r.cpad.at[pl.ds(0, HEAD)],
            r.cpad.at[pl.ds(r.T, HEAD)],
            r.sems[b.head_s].at[0],
            r.sems[b.head_r].at[0],
            to,
            r.c,
        )

    start(r, head_copy(r.s - 1), r.s > 0)

    @pl.when(r.s == r.nS - 1)
    def _():
        r.cpad[pl.ds(r.T, HEAD), :] = jnp.zeros((HEAD, r.C), F32)

    def x_adj(first, count):
        rows = pl.ds(first, count)
        total = jnp.zeros((count, r.C), F32)
        for k in range(r.KC):
            total = total + r.conv_w[k : k + 1, :] * r.cpad[pl.ds(first + r.KC - 1 - k, count), :]
        r.xg[r.y, rows] = total.astype(BF16)

    def x_copy(i, slot, part):
        rows = pl.ds(part * (r.T // 2), r.T // 2)
        return line_copy(r, i, r.xg.at[slot, rows], r.xg.at[slot, rows], b.xg, slot, part)

    x_adj(0, r.T // 2)
    for i in range(1, r.nY):
        start(r, x_copy(i, r.y, 0))
    for part in range(2):
        for i in range(1, r.nY):
            relay_copy(r, i, lax.rem(r.y + i, r.nY), 1 - r.k, part).wait_recv()
    grad_part(r, 0)
    weight_line(r, r.dt_c, r.dt_d, r.dt_e, (b.d2, b.d3))
    pl.when(r.s < r.nS - 1)(lambda: head_copy(r.s + 1).wait_recv())
    x_adj(r.T // 2, r.T // 2)
    for i in range(1, r.nY):
        start(r, x_copy(i, r.y, 1))
    grad_part(r, 1)
    total = None
    for y2 in range(r.nY):
        pl.when(r.y != y2)(
            line_copy(r, 1, r.mi_c.at[y2], r.mi_c.at[y2], b.m2, y2).wait_recv
        )
        term = r.mi_c[y2].astype(F32)
        total = term if total is None else total + term
    r.mi_e[r.k] = total
    start(r, pair_copy(r, r.mi_e.at[r.k], r.mi_e.at[r.k], b.m3))
    weight_back(r, r.dt_e, b.d3, b.d4)
    for i in range(1, r.nY):
        y2 = lax.rem(r.y + i, r.nY)
        line_copy(r, i, r.ug.at[y2], r.ug.at[y2], b.ug, y2).wait_recv()
        line_copy(r, i, r.lg.at[y2], r.lg.at[y2], b.lg, y2).wait_recv()
    tokens = r.nY * r.T
    term = contract_first(r.lg[...].reshape(tokens, r.R + LANES), r.ug[...].reshape(tokens, r.C))
    r.li_p[...] = term[: r.R + 2 * r.N].astype(BF16)
    start(r, pair_copy(r, r.li_p, r.li_b, b.d5))
    for i in range(1, r.nY):
        y2 = lax.rem(r.y + i, r.nY)
        x_copy(i, y2, 0).wait_recv()
        x_copy(i, y2, 1).wait_recv()

    x_all = r.xg[...].reshape(r.nY * r.T, r.C)

    def weight(x2):
        return contract_first(r.hg[x2].reshape(r.nY * r.T, r.DH), x_all)

    for j in range(half):
        r.ws[j] = weight((1 - r.k) * half + j).astype(BF16)
    start(r, pair_copy(r, r.ws, r.wr, b.wg))
    for j in range(half):
        r.wo[j] = weight(r.k * half + j)
    pair_copy(r, r.ws, r.wr, b.wg).wait_recv()
    r.w_out[...] = (r.wo[...] + r.wr[...].astype(F32)).astype(BF16)
    weight_end(r, r.dt_e, b.d4)
    pair_copy(r, r.mi_e.at[r.k], r.mi_e.at[1 - r.k], b.m3).wait_recv()
    total = r.hs[0].astype(F32)
    for i, c2, dev in peers(r, b.chan):
        for part in range(2):
            rows, at = pl.ds(part * (r.T // 2), r.T // 2), part * r.nC + c2
            got = r.hr.at[c2, rows]
            rcopy(got, got, r.sems[b.hg_s].at[i], r.sems[b.hg_r].at[at], *dev).wait_recv()
        total = total + r.hr[c2].astype(F32)
    r.hidden_out[...] = total.astype(BF16)
    pair_copy(r, r.li_p, r.li_b, b.d5).wait_recv()
    r.li_e[...] = (r.li_p[...].astype(F32) + r.li_b[...].astype(F32)).astype(BF16)
    flush(r)


def finish(r):
    scale = 1.0 / math.sqrt(r.T * r.nS)
    wide_half = r.C // 2
    r.hidden_grad[...] = r.hidden_out[...]
    r.gate_grad[...] = r.gate_out[...]
    r.w_in_grad[...] = r.w_out[...].astype(F32) * scale
    r.w_dt_grad[...] = r.dt_e[...].astype(F32).reshape(r.R, r.C) * scale
    r.w_delta_in_grad[...] = r.li_e[pl.ds(0, r.R), :].astype(F32) * scale
    r.w_bc_grad[...] = r.li_e[pl.ds(r.R, 2 * r.N), :].astype(F32) * scale
    for j in range(2):
        cols = pl.ds(j * wide_half, wide_half)
        r.a_log_grad[:, cols] = r.mi_e[j] * scale


def tables(dim):
    d = types.SimpleNamespace(**dim)
    t, c, n, rows, q = d.T, d.C, d.N, d.R, d.R // d.nS
    wide_row = rows + LANES
    buffers = dict(
        hg=((d.nX, d.nY, t, d.DH), BF16),
        wf=((d.nY, d.nX, d.DH, c), BF16),
        xs=((d.nY, t, c), BF16),
        xr=((d.nY, t, c), BF16),
        xt=((d.nY, HALO, c), BF16),
        xpad=((HALO + t, c), F32),
        slope=((t, c), F32),
        gs=((t, c), F32),
        u=((t, c), BF16),
        part=((d.nC, d.PR, LANES), BF16),
        part_r=((d.nC, d.PR, LANES), BF16),
        part_a=((d.nC, d.PR, LANES), BF16),
        pad=((t, LANES), F32),
        low=((t, rows), BF16),
        bcw=((t, LANES), F32),
        pre=((t, c), F32),
        delta=((t, c), F32),
        du=((t, c), F32),
        g=((t, c), F32),
        am=((n, c), F32),
        bx=((t, n, LANES), F32),
        cx=((t, n, LANES), F32),
        sd=((1, c), F32),
        aa=((t * n, c), F32),
        hh=(((t + 1) * n, c), F32),
        ef=((2, n, c), BF16),
        st_r=((d.nS, n, c), BF16),
        sd_r=((d.nS, 1, c), F32),
        kept0=((CH * n, c), BF16),
        kept1=((CH * n, c), BF16),
        kept2=((CH * n, c), BF16),
        kept3=((CH * n, c), BF16),
        h_in=((n, c), F32),
        l_in=((n, c), F32),
        bd=((t, CH * n), BF16),
        cd=((t, CH * n), BF16),
        bm=((t, CH * n), F32),
        cm=((t, CH * n), F32),
        y_scan=((t, c), F32),
        s1=((t, c), F32),
        s2=((t, c), F32),
        uu=((t, c), F32),
        part2=((d.nC, d.PR, LANES), BF16),
        part2_r=((d.nC, d.PR, LANES), BF16),
        part2_a=((d.nC, d.PR, LANES), BF16),
        dt_p=((2, d.nY, q, c), BF16),
        dt_b=((d.nY, q, c), BF16),
        dt_c=((d.nY, q, c), BF16),
        dt_d=((d.nY, q, c), BF16),
        dt_e=((2, d.nY, q, c), BF16),
        ug=((d.nY, t, c), BF16),
        lg=((d.nY, t, wide_row), BF16),
        li_p=((rows + 2 * n, c), BF16),
        li_b=((rows + 2 * n, c), BF16),
        li_e=((rows + 2 * n, c), BF16),
        mi_p=((2, n, c // 2), BF16),
        mi_b=((n, c // 2), BF16),
        mi_c=((d.nY, n, c // 2), BF16),
        mi_e=((2, n, c // 2), F32),
        cpad=((t + HEAD, c), F32),
        xg=((d.nY, t, c), BF16),
        hs=((d.nC, t, d.DH), BF16),
        hr=((d.nC, t, d.DH), BF16),
        ws=((d.nX // 2, d.DH, c), BF16),
        wr=((d.nX // 2, d.DH, c), BF16),
        wo=((d.nX // 2, d.DH, c), F32),
        w_out=((d.nX // 2, d.DH, c), BF16),
        hidden_out=((t, d.DH), BF16),
        gate_out=((t, c), BF16),
        hidden_grad=((t, d.DH), BF16),
        gate_grad=((t, c), BF16),
        w_in_grad=((d.nX // 2, d.DH, c), F32),
        w_delta_in_grad=((rows, c), F32),
        w_bc_grad=((2 * n, c), F32),
        w_dt_grad=((rows, c), F32),
        a_log_grad=((n, c), F32),
    )
    sems = dict(loc=2, inp=12)
    pairs = (b.tu, b.wp, b.head, b.wg, b.d1, b.d4, b.d5, b.m1, b.m3)
    lines = (b.xr, b.tail, b.d2, b.d3, b.m2, b.ug, b.lg)
    for key in pairs:
        sems[key + "_s"] = sems[key + "_r"] = 1
    for key in lines:
        sems[key + "_s"] = sems[key + "_r"] = d.nY
    for key in (b.xg, b.wy, b.wz):
        sems[key + "_s"] = sems[key + "_r"] = 2 * d.nY
    sems[b.hg_s] = sems[b.hg_r] = 2 * d.nC
    for key in (b.g1, b.g2):
        sems[key + "_s"] = sems[key + "_r"] = d.nX + d.nY
    for key in (b.p1, b.p2, b.p3, b.p4):
        sems[key + "_s"] = sems[key + "_r"] = d.nC
    for key in (b.st, b.sd):
        sems[key + "_s"] = sems[key + "_r"] = d.nS
    return buffers, sems


def run(dim, phases, remote, values, ins, outs, scratch, sem_names, cost):
    buffers, sem_sizes = tables(dim)
    held = [name for name in ins if name not in (b.hidden, b.w_in)] if remote else []

    def body(*refs):
        r = types.SimpleNamespace(**dim)
        r.sent = []
        names = ins + outs + scratch
        for name, ref in zip(names, refs):
            setattr(r, name, ref)
        refs = refs[len(names) :]
        r.sems = dict(zip(sem_names, refs))
        if remote:
            r.given = {name: getattr(r, name) for name in ins}
            for name, ref in zip(held, refs[len(sem_names) :]):
                setattr(r, name, ref)
            r.s, r.c = lax.axis_index(b.seq), lax.axis_index(b.chan)
            r.y, r.k = lax.div(r.s, 2), lax.rem(r.s, 2)
            r.z, r.x = lax.div(r.c, r.nX), lax.rem(r.c, r.nX)
            greet(r, functools.partial(load, r))
        for phase in phases:
            phase(r)

    space = pl.BlockSpec(memory_space=pltpu.VMEM)
    extra = dict(collective_id=0, has_side_effects=True) if remote else {}
    results = pl.pallas_call(
        body,
        out_shape=[jax.ShapeDtypeStruct(*buffers[name]) for name in outs],
        in_specs=[pl.BlockSpec(memory_space=pl.ANY) if remote else space] * len(ins),
        out_specs=[space] * len(outs),
        scratch_shapes=[pltpu.VMEM(*buffers[name]) for name in scratch]
        + [pltpu.SemaphoreType.DMA((sem_sizes[name],)) for name in sem_names]
        + [pltpu.VMEM(values[name].shape, values[name].dtype) for name in held],
        compiler_params=pltpu.CompilerParams(vmem_limit_bytes=56 << 20, **extra),
        cost_estimate=pl.CostEstimate(flops=cost, bytes_accessed=4 << 20, transcendentals=0),
        name=phases[-1].__name__,
    )(*[values[name] for name in ins])
    values.update(zip(outs, results))


ORDER = [b.hidden_grad, b.gate_grad, b.w_in_grad, b.w_delta_in_grad, b.w_bc_grad, b.w_dt_grad, b.a_log_grad]


def per_device(
    seq, chan, hidden, gate_in, out_grad, w_in, conv_w, conv_b, w_delta_in, w_bc, w_dt, dt_bias, a_log, skip_d
):
    lines = seq // 2
    dim = dict(
        nS=seq,
        nC=chan,
        nY=lines,
        nX=chan // lines,
        T=hidden.shape[0],
        DH=hidden.shape[1],
        C=w_in.shape[1],
        R=w_delta_in.shape[0],
        N=a_log.shape[0],
        KC=conv_w.shape[0],
        RP=hidden.shape[0] // chan,
        PR=-(-(hidden.shape[0] // chan) * (w_delta_in.shape[0] // LANES + 1) // 16) * 16,
    )
    v = dict(
        hidden=hidden,
        gate_in=gate_in,
        out_grad=out_grad,
        w_in=w_in.reshape(dim[b.nX] // 2, dim[b.DH], dim[b.C]),
        conv_w=conv_w,
        conv_b=conv_b[None],
        w_delta_in=w_delta_in,
        w_bc=w_bc,
        w_dt=w_dt,
        dt_bias=dt_bias[None],
        a_log=a_log,
        skip_d=skip_d[None],
    )
    raw = [b.hidden_out, b.gate_out, b.w_out, b.dt_e, b.li_e, b.mi_e]
    given = list(v)
    buffers, sems = tables(dim)
    scratch = [name for name in buffers if name not in given + raw + ORDER]
    phases = [take_hidden, project, prepare, scan, gradients]
    run(dim, phases, True, v, given, raw, scratch, list(sems), 2_000_000_000)
    run(dim, [finish], False, v, raw, ORDER, [], [], 1_000_000)
    v[b.w_in_grad] = v[b.w_in_grad].reshape(w_in.shape)
    return tuple(v[name] for name in ORDER)


def solution(mesh):
    placed = (
        P(b.seq, b.chan),
        P(b.seq, b.chan),
        P(b.seq, b.chan),
        P(b.seq, b.chan),
        P(None, b.chan),
        P(b.chan),
        P(None, b.chan),
        P(None, b.chan),
        P(None, b.chan),
        P(b.chan),
        P(None, b.chan),
        P(b.chan),
    )
    return jax.shard_map(
        functools.partial(per_device, mesh.shape[b.seq], mesh.shape[b.chan]),
        mesh=mesh,
        in_specs=placed,
        out_specs=(
            P(b.seq, b.chan),
            P(b.seq, b.chan),
            P(b.seq, b.chan),
            P(None, b.chan),
            P(None, b.chan),
            P(None, b.chan),
            P(None, b.chan),
        ),
        check_vma=False,
    )
```

```python
import functools
import math
import types

import jax
import jax.numpy as jnp
from jax import lax
from jax.experimental import pallas as pl
from jax.experimental.pallas import tpu as pltpu
from jax.sharding import PartitionSpec as P

MESH = pl.DeviceIdType.MESH


class Names:
    def __getattr__(self, name):
        return name


b = Names()
F32, BF16 = jnp.float32, jnp.bfloat16
CH = 16
LANES = 128
HALO = 16
HEAD = 8


def contract_last(left, right):
    return lax.dot_general(left, right, (((1,), (1,)), ((), ())), preferred_element_type=F32)


def contract_first(left, right):
    return lax.dot_general(left, right, (((0,), (0,)), ((), ())), preferred_element_type=F32)


def dot(left, right):
    return jnp.dot(left, right, preferred_element_type=F32)


def silu_slope(values):
    sig = jax.nn.sigmoid(values)
    return sig * (1.0 + values * (1.0 - sig))


def softplus(v):
    return jnp.maximum(v, 0.0) + jnp.log1p(jnp.exp(-jnp.abs(v)))


def rcopy(src, dst, send, recv, seq, chan):
    return pltpu.make_async_remote_copy(
        src_ref=src,
        dst_ref=dst,
        send_sem=send,
        recv_sem=recv,
        device_id=dict(seq=seq, chan=chan),
        device_id_type=MESH,
    )


def ring(r, group):
    if group == b.seq:
        return r.s, r.nS, lambda j: (j, r.c)
    return r.c, r.nC, lambda j: (r.s, j)


def peers(r, group):
    me, n, dev = ring(r, group)
    for i in range(1, n):
        j = lax.rem(me + i, n)
        yield i, j, dev(j)


def start(r, copy, when=None):
    r.sent.append((copy, when))
    if when is None:
        copy.start()
    else:
        pl.when(when)(copy.start)


def flush(r):
    for copy, when in r.sent:
        if when is None:
            copy.wait_send()
        else:
            pl.when(when)(copy.wait_send)
    r.sent.clear()


def scatter_start(r, group, src, dst, key):
    me = ring(r, group)[0]
    for i, j, dev in peers(r, group):
        start(r, rcopy(src.at[j], dst.at[me], r.sems[key + "_s"].at[i], r.sems[key + "_r"].at[me], *dev))


def gather_start(r, group, buf, key):
    me = ring(r, group)[0]
    for i, j, dev in peers(r, group):
        start(r, rcopy(buf.at[me], buf.at[me], r.sems[key + "_s"].at[i], r.sems[key + "_r"].at[me], *dev))


def recv_wait(r, group, buf, key):
    for i, j, dev in peers(r, group):
        rcopy(buf.at[j], buf.at[j], r.sems[key + "_s"].at[i], r.sems[key + "_r"].at[j], *dev).wait_recv()


def scatter_sum(r, group, src, dst, key):
    me = ring(r, group)[0]
    total = src[me].astype(F32)
    recv_wait(r, group, dst, key)
    for i, j, dev in peers(r, group):
        total = total + dst[j].astype(F32)
    return total


def pair_copy(r, src, dst, key):
    return rcopy(src, dst, r.sems[key + "_s"].at[0], r.sems[key + "_r"].at[0], r.y * 2 + 1 - r.k, r.c)


def line_copy(r, i, src, dst, key, slot, part=0):
    at = part * r.nY
    return rcopy(
        src,
        dst,
        r.sems[key + "_s"].at[at + i],
        r.sems[key + "_r"].at[at + slot],
        lax.rem(r.y + i, r.nY) * 2 + r.k,
        r.c,
    )


def plane_copy(r, i, along_x, src, dst, key, slot):
    at, seq = (0 if along_x else r.nX), r.s
    chan = r.z * r.nX + lax.rem(r.x + i, r.nX) if along_x else lax.rem(r.z + i, r.nY) * r.nX + r.x
    return rcopy(src, dst, r.sems[key + "_s"].at[at + i], r.sems[key + "_r"].at[at + slot], seq, chan)


def greet(r, during):
    barrier = pltpu.get_barrier_semaphore()

    def tell(seq, chan):
        pl.semaphore_signal(barrier, inc=1, device_id=dict(seq=seq, chan=chan), device_id_type=MESH)

    pl.when(r.y != r.z)(lambda: tell(r.z * 2 + r.k, r.y * r.nX + r.x))
    for i in range(1, r.nX):
        tell(r.s, r.z * r.nX + lax.rem(r.x + i, r.nX))
        tell(r.s, lax.rem(r.z + i, r.nY) * r.nX + r.x)
    for i, j, dev in peers(r, b.seq):
        tell(*dev)
    during()
    apart = (r.y - r.z) * (r.y - r.z)
    apart = lax.div(apart + r.nY * r.nY - 1, r.nY * r.nY)
    pl.semaphore_wait(barrier, 2 * (r.nX - 1) + r.nS - 1 + apart)


def load(r):
    for at, (name, ref) in enumerate(r.given.items()):
        if name in (b.w_in, b.hidden):
            continue
        pltpu.make_async_copy(ref, getattr(r, name), r.sems[b.inp].at[at]).start()


def need(r, *names):
    for name in names:
        at = list(r.given).index(name)
        pltpu.make_async_copy(r.given[name], getattr(r, name), r.sems[b.inp].at[at]).wait()


def pack(r, low, small):
    r.pad[:, pl.ds(0, 2 * r.N)] = small
    parts = [low[:, at : at + LANES] for at in range(0, r.R, LANES)] + [r.pad[...]]
    parts = [part.reshape(r.nC, r.RP, LANES) for part in parts]
    parts += [jnp.zeros_like(parts[0])] * (r.PR // r.RP - len(parts))
    return jnp.concatenate(parts, 1).astype(BF16)


def unpack(r, pieces):
    pieces = pieces.astype(F32)
    parts = [pieces[:, at : at + r.RP].reshape(r.T, LANES) for at in range(0, r.PR, r.RP)]
    count = r.R // LANES
    return jnp.concatenate(parts[:count], 1), parts[count]


def weight_rows(r, y2, core, part):
    half, cut = r.nX // 2, r.DH // 2
    return r.wf.at[y2, pl.ds(core * half, half), pl.ds(part * cut, cut)]


def weight_copy(r, i, y2, part):
    rows = weight_rows(r, y2, r.k, part)
    return line_copy(r, i, rows, rows, b.wy, y2, part)


def relay_copy(r, i, y2, core, part):
    rows, at = weight_rows(r, y2, core, part), part * r.nY + i
    return rcopy(rows, rows, r.sems[b.wz_s].at[at], r.sems[b.wz_r].at[at], r.y * 2 + 1 - r.k, r.c)


def weight_send(r, part):
    for i in range(1, r.nY):
        start(r, weight_copy(r, i, r.y, part))


def weight_relay(r, part):
    for i in range(1, r.nY):
        y2 = lax.rem(r.y + i, r.nY)
        weight_copy(r, i, y2, part).wait_recv()
        start(r, relay_copy(r, i, y2, r.k, part))


def take_hidden(r):
    half, cut = r.nX // 2, r.T // 2
    mine = r.wf.at[r.y, pl.ds(r.k * half, half)]
    own_w = pltpu.make_async_copy(r.w_in, mine, r.sems[b.loc].at[0])
    own_h = pltpu.make_async_copy(r.hidden, r.hg.at[r.x, r.y], r.sems[b.loc].at[1])
    turn = rcopy(
        r.hidden, r.hg.at[r.x, r.y], r.sems[b.tu_s].at[0], r.sems[b.tu_r].at[0], r.z * 2 + r.k, r.y * r.nX + r.x
    )
    start(r, turn, r.y != r.z)
    start(r, pair_copy(r, r.w_in, mine, b.wp))
    own_w.start()
    pl.when(r.y == r.z)(own_h.start)
    need(r, b.gate_in, b.out_grad, b.a_log)

    gate = r.gate_in[...].astype(F32)
    sig = jax.nn.sigmoid(gate)
    grad = r.out_grad[...].astype(F32)
    r.g[...] = grad * (gate * sig)
    r.gs[...] = grad * (sig * (1.0 + gate * (1.0 - sig)))
    r.am[...] = -jnp.exp(r.a_log[...])
    r.pad[...] = jnp.zeros_like(r.pad)
    own_w.wait()
    pl.when(r.y == r.z)(own_h.wait)

    @pl.when(r.y != r.z)
    def _():
        rcopy(
            r.hidden, r.hg.at[r.x, r.z], r.sems[b.tu_s].at[0], r.sems[b.tu_r].at[0], r.z * 2 + r.k, r.y * r.nX + r.x
        ).wait_recv()

    low, high = pl.ds(0, cut), pl.ds(cut, r.T - cut)
    for i in range(1, r.nX):
        start(r, plane_copy(r, i, True, r.hg.at[r.x, r.z, low], r.hg.at[r.x, r.z, low], b.g1, r.x))
        start(r, plane_copy(r, i, False, r.hg.at[r.x, r.z, high], r.hg.at[r.x, r.z, high], b.g1, r.z))
    weight_send(r, 0)
    for i in range(1, r.nX):
        x2, z2 = lax.rem(r.x + i, r.nX), lax.rem(r.z + i, r.nY)
        plane_copy(r, i, True, r.hg.at[x2, r.z, low], r.hg.at[x2, r.z, low], b.g1, x2).wait_recv()
        plane_copy(r, i, False, r.hg.at[r.x, z2, high], r.hg.at[r.x, z2, high], b.g1, z2).wait_recv()
    for i in range(1, r.nX):
        start(r, plane_copy(r, i, False, r.hg.at[:, r.z, low], r.hg.at[:, r.z, low], b.g2, r.z))
        start(r, plane_copy(r, i, True, r.hg.at[r.x, :, high], r.hg.at[r.x, :, high], b.g2, r.x))
    pair_copy(r, r.w_in, r.wf.at[r.y, pl.ds((1 - r.k) * half, half)], b.wp).wait_recv()
    for i in range(1, r.nX):
        x2, z2 = lax.rem(r.x + i, r.nX), lax.rem(r.z + i, r.nY)
        plane_copy(r, i, True, r.hg.at[x2, :, high], r.hg.at[x2, :, high], b.g2, x2).wait_recv()
        plane_copy(r, i, False, r.hg.at[:, z2, low], r.hg.at[:, z2, low], b.g2, z2).wait_recv()


def tail_copy(r, i, y2, slot):
    return rcopy(
        r.xs.at[i, pl.ds(r.T - HALO, HALO)],
        r.xt.at[slot],
        r.sems[b.tail_s].at[i],
        r.sems[b.tail_r].at[slot],
        y2 * 2 + r.k + 1,
        r.c,
    )


def project(r):
    for i in range(1, r.nY + 1):
        y2 = lax.rem(r.y + i, r.nY)
        total = None
        for j in range(r.nX):
            term = dot(r.hg[j, y2], r.wf[r.y, j])
            total = term if total is None else total + term
        r.xs[i - 1] = total.astype(BF16)
        if i < r.nY:
            start(r, line_copy(r, i, r.xs.at[i - 1], r.xr.at[r.y], b.xr, r.y))
        start(r, tail_copy(r, i - 1, y2, r.y), y2 * 2 + r.k + 1 < r.nS)
    own = total

    @pl.when(r.s == 0)
    def _():
        r.xpad[pl.ds(0, HALO), :] = jnp.zeros((HALO, r.C), F32)

    @pl.when(r.s > 0)
    def _():
        tail = None
        for y2 in range(r.nY):
            tail_copy(r, 0, r.y, y2).wait_recv()
            term = r.xt[y2].astype(F32)
            tail = term if tail is None else tail + term
        r.xpad[pl.ds(0, HALO), :] = tail.astype(BF16).astype(F32)

    for i in range(1, r.nY):
        y2 = lax.rem(r.y + i, r.nY)
        line_copy(r, i, r.xs.at[i - 1], r.xr.at[y2], b.xr, y2).wait_recv()
        own = own + r.xr[y2].astype(F32)
    r.xpad[pl.ds(HALO, r.T), :] = own.astype(BF16).astype(F32)
    need(r, b.conv_w, b.conv_b, b.w_delta_in, b.w_bc)
    conv = jnp.zeros((r.T, r.C), F32) + r.conv_b[...]
    for k in range(r.KC):
        conv = conv + r.conv_w[k : k + 1, :] * r.xpad[pl.ds(HALO - r.KC + 1 + k, r.T), :]
    sig = jax.nn.sigmoid(conv)
    u = (conv * sig).astype(BF16)
    r.u[...] = u
    r.part[...] = pack(r, contract_last(u, r.w_delta_in[...]), contract_last(u, r.w_bc[...]))
    scatter_start(r, b.chan, r.part, r.part_r, b.p1)
    weight_send(r, 1)
    weight_relay(r, 0)
    r.slope[...] = sig * (1.0 + conv * (1.0 - sig))
    r.part_a[r.c] = scatter_sum(r, b.chan, r.part, r.part_r, b.p1).astype(BF16)
    gather_start(r, b.chan, r.part_a, b.p2)
    recv_wait(r, b.chan, r.part_a, b.p2)
    low, r.bcw[...] = unpack(r, r.part_a[...])
    r.low[...] = low.astype(BF16)


def wide(r, b):
    return jnp.concatenate([b] * (r.C // LANES), axis=1) if r.C > LANES else b


def block_mask(r, rows):
    row = lax.broadcasted_iota(jnp.int32, (rows, CH * r.N), 0)
    col = lax.broadcasted_iota(jnp.int32, (rows, CH * r.N), 1)
    return jnp.where(lax.rem(row, CH) == lax.div(col, r.N), 1.0, 0.0).astype(F32)


def pick(r):
    row = lax.broadcasted_iota(jnp.int32, (r.N, CH * r.N), 0)
    col = lax.broadcasted_iota(jnp.int32, (r.N, CH * r.N), 1)
    return jnp.where(lax.rem(col, r.N) == row, 1.0, 0.0).astype(F32)


def prepare(r):
    need(r, b.w_dt, b.dt_bias, b.skip_d)
    pre = dot(r.low[...], r.w_dt[...]) + r.dt_bias[...]
    r.pre[...] = pre
    delta = softplus(pre)
    r.delta[...] = delta
    r.sd[...] = jnp.sum(delta, 0, keepdims=True)
    for i, j, dev in peers(r, b.seq):
        start(r, rcopy(r.sd, r.sd_r.at[r.s], r.sems[b.sd_s].at[i], r.sems[b.sd_r].at[r.s], *dev))
    u = r.u[...].astype(F32)
    r.du[...] = delta * u
    turned = r.bcw[...].T
    for t in range(r.T):
        r.bx[t] = jnp.broadcast_to(turned[0 : r.N, t : t + 1], (r.N, LANES))


def forward_chunk(r, j, h, kept):
    a_mat = r.am[...]
    base = pl.multiple_of(j * CH, CH)
    d = r.delta[pl.ds(base, CH), :]
    du = r.du[pl.ds(base, CH), :]
    for t in range(CH):
        at = pl.multiple_of((base + t) * r.N, r.N)
        if kept is None:
            a = jnp.exp(d[t : t + 1, :] * a_mat)
            r.aa[pl.ds(at, r.N), :] = a
        else:
            a = r.aa[pl.ds(at, r.N), :]
        h = a * h + du[t : t + 1, :] * wide(r, r.bx[base + t])
        if kept is not None:
            r.hh[pl.ds(at + r.N, r.N), :] = h
            kept[pl.ds(t * r.N, r.N), :] = h.astype(BF16)
            r.hb[pl.ds(at, r.N), :] = h.astype(BF16)
    return h


def forward_sums(r, j, kept, mask):
    rows = pl.ds(pl.multiple_of(j * CH, CH), CH)
    states = kept[...]
    r.cm[rows, :] = mask * contract_last(r.g[rows, :].astype(BF16), states)


def outputs(r):
    def one(j, carry):
        rows = pl.ds(pl.multiple_of(j * CH, CH), CH)
        states = r.hb[pl.ds(pl.multiple_of(j * CH * r.N, CH * r.N), CH * r.N), :]
        r.y_scan[rows, :] = dot(r.cd[rows, :], states)
        return carry

    lax.fori_loop(0, r.T // CH, one, 0)


def forward_free(r):
    return lax.fori_loop(0, r.T // CH, lambda j, h: forward_chunk(r, j, h, None), jnp.zeros((r.N, r.C), F32))


def forward_full(r):
    mask = block_mask(r, CH)
    r.hh[pl.ds(0, r.N), :] = r.h_in[...]
    r.kept1[...] = jnp.zeros_like(r.kept1)

    def two(i, h):
        forward_sums(r, jnp.maximum(2 * i - 1, 0), r.kept1, mask)
        h = forward_chunk(r, 2 * i, h, r.kept0)
        forward_sums(r, 2 * i, r.kept0, mask)
        return forward_chunk(r, 2 * i + 1, h, r.kept1)

    lax.fori_loop(0, r.T // CH // 2, two, r.h_in[...])
    forward_sums(r, r.T // CH - 1, r.kept1, mask)


def backward_chunk(r, j, carry, kept):
    a_mat = r.am[...]
    base = pl.multiple_of(j * CH, CH)
    kap, acc = carry
    d = r.delta[pl.ds(base, CH), :]
    g = r.g[pl.ds(base, CH), :]
    for t in reversed(range(CH)):
        at = pl.multiple_of((base + t) * r.N, r.N)
        lam = kap + wide(r, r.cx[base + t]) * g[t : t + 1, :]
        kap = r.aa[pl.ds(at, r.N), :] * lam
        if kept is not None:
            q = kap * r.hh[pl.ds(at, r.N), :]
            acc = acc + q * d[t : t + 1, :]
            kept[0][pl.ds(t * r.N, r.N), :] = lam.astype(BF16)
            kept[1][pl.ds(t * r.N, r.N), :] = (q * a_mat).astype(BF16)
    return kap, acc


def backward_sums(r, j, kept, mask):
    rows = pl.ds(pl.multiple_of(j * CH, CH), CH)
    lam = kept[0][...]
    r.s1[rows, :] = dot(r.bd[rows, :], lam)
    r.s2[rows, :] = dot(mask.astype(BF16), kept[1][...])
    r.bm[rows, :] = mask * contract_last(r.du[rows, :].astype(BF16), lam)


def backward_free(r):
    zero = jnp.zeros((r.N, r.C), F32)
    last = r.T // CH - 1
    return lax.fori_loop(0, last + 1, lambda i, c: backward_chunk(r, last - i, c, None), (zero, zero))[0]


def backward_full(r):
    mask = block_mask(r, CH)
    last = r.T // CH - 1
    even, odd = (r.kept0, r.kept2), (r.kept1, r.kept3)
    for ref in odd:
        ref[...] = jnp.zeros_like(ref)

    def two(i, carry):
        backward_sums(r, jnp.minimum(last - 2 * i + 1, last), odd, mask)
        carry = backward_chunk(r, last - 2 * i, carry, even)
        backward_sums(r, last - 2 * i, even, mask)
        return backward_chunk(r, last - 2 * i - 1, carry, odd)

    a_adj = lax.fori_loop(0, r.T // CH // 2, two, (r.l_in[...], jnp.zeros((r.N, r.C), F32)))[1]
    backward_sums(r, 0, odd, mask)
    return a_adj


def state_copy(r, which, j, slot):
    return rcopy(r.ef.at[which], r.st_r.at[slot], r.sems[b.st_s].at[j], r.sems[b.st_r].at[slot], j, r.c)


def scan(r):
    zero = jnp.zeros((r.N, r.C), F32)
    r.ef[0] = forward_free(r).astype(BF16)
    for j in range(1, r.nS):
        start(r, state_copy(r, 0, j, r.s), j > r.s)
    turned = r.bcw[...].T
    for t in range(r.T):
        r.cx[t] = jnp.broadcast_to(turned[r.N : 2 * r.N, t : t + 1], (r.N, LANES))
    r.ef[1] = backward_free(r).astype(BF16)
    for j in range(r.nS - 1):
        start(r, state_copy(r, 1, j, r.s), j < r.s)
    picked = pick(r)
    tall = block_mask(r, r.T)
    r.bd[...] = (tall * dot(r.bcw[:, pl.ds(0, r.N)], picked)).astype(BF16)
    r.cd[...] = (tall * dot(r.bcw[:, pl.ds(r.N, r.N)], picked)).astype(BF16)

    r.sp[...] = jax.nn.sigmoid(r.pre[...])

    def enter(j, into):
        rcopy(r.sd, r.sd_r.at[j], r.sems[b.sd_s].at[0], r.sems[b.sd_r].at[j], j, r.c).wait_recv()
        state_copy(r, 0, j, j).wait_recv()
        into[...] = jnp.exp(r.am[...] * r.sd_r[j]) * into[...] + r.st_r[j].astype(F32)

    r.h_in[...] = zero
    for j in range(r.nS - 1):
        pl.when(j < r.s)(functools.partial(enter, j, r.h_in))
    forward_full(r)
    r.l_in[...] = zero
    for j in range(r.nS - 1, 0, -1):
        pl.when(j > r.s)(functools.partial(enter, j, r.l_in))
    r.ug[r.y] = r.u[...]
    for i in range(1, r.nY):
        start(r, line_copy(r, i, r.ug.at[r.y], r.ug.at[r.y], b.ug, r.y))
    a_adj = backward_full(r)
    s1 = r.s1[...]
    u = r.u[...].astype(F32)
    pre_adj = ((u * s1 + r.s2[...]) * r.sp[...]).astype(BF16)
    exact = lax.Precision.HIGHEST
    nt = (((1,), (1,)), ((), ()))
    b_adj = lax.dot_general(r.bm[...], picked, nt, precision=exact, preferred_element_type=F32)
    c_adj = lax.dot_general(r.cm[...], picked, nt, precision=exact, preferred_element_type=F32)
    r.part2[...] = pack(r, contract_last(pre_adj, r.w_dt[...]), jnp.concatenate([b_adj, c_adj], 1))
    scatter_start(r, b.chan, r.part2, r.part2_r, b.p3)
    weight_relay(r, 1)
    r.dt_p[...] = contract_first(r.low[...], pre_adj).astype(BF16).reshape(2, r.nY, r.R // r.nS, r.C)
    start(r, pair_copy(r, r.dt_p.at[1 - r.k], r.dt_b, b.d1))
    alog = (a_adj * r.am[...]).astype(BF16)
    wide_half = r.C // 2
    for j in range(2):
        r.mi_p[j] = alog[:, j * wide_half : (j + 1) * wide_half]
    start(r, pair_copy(r, r.mi_p.at[1 - r.k], r.mi_b, b.m1))
    skip = r.skip_d[...]
    r.uu[...] = r.delta[...] * s1 + skip * r.g[...]
    outputs(r)
    r.gate_out[...] = (r.gs[...] * (r.y_scan[...] + skip * u)).astype(BF16)


def grad_copy(r, i, part):
    rows = pl.ds(part * (r.T // 2), r.T // 2)
    c2 = lax.rem(r.c + i, r.nC)
    at = part * r.nC
    return rcopy(
        r.hs.at[i, rows], r.hr.at[r.c, rows], r.sems[b.hg_s].at[at + i], r.sems[b.hg_r].at[at + r.c], r.s, c2
    )


def grad_part(r, part):
    rows = pl.ds(part * (r.T // 2), r.T // 2)
    for i in range(r.nC - 1, -1, -1):
        c2 = lax.rem(r.c + i, r.nC)
        term = contract_last(r.xg[r.y, rows], r.wf[lax.div(c2, r.nX), lax.rem(c2, r.nX)])
        r.hs[i, rows] = term.astype(BF16)
        if i:
            start(r, grad_copy(r, i, part))


def weight_pair(r, part, got, summed, key):
    pair_copy(r, part.at[1 - r.k], got, key[0]).wait_recv()
    summed[...] = (part[r.k].astype(F32) + got[...].astype(F32)).astype(BF16)


def weight_line(r, summed, got, whole, keys):
    total = summed[r.y].astype(F32)
    for i in range(1, r.nY):
        y2 = lax.rem(r.y + i, r.nY)
        line_copy(r, i, summed.at[y2], got.at[y2], keys[0], y2).wait_recv()
        total = total + got[y2].astype(F32)
    whole[r.k, r.y] = total.astype(BF16)
    for i in range(1, r.nY):
        start(r, line_copy(r, i, whole.at[r.k, r.y], whole.at[r.k, r.y], keys[1], r.y))


def weight_back(r, whole, line_key, pair_key):
    for i in range(1, r.nY):
        y2 = lax.rem(r.y + i, r.nY)
        line_copy(r, i, whole.at[r.k, y2], whole.at[r.k, y2], line_key, y2).wait_recv()
    start(r, pair_copy(r, whole.at[r.k], whole.at[r.k], pair_key))


def weight_end(r, whole, pair_key):
    pair_copy(r, whole.at[r.k], whole.at[1 - r.k], pair_key).wait_recv()


def spread(r, summed, got, key):
    for i in range(1, r.nY):
        start(r, line_copy(r, i, summed.at[lax.rem(r.y + i, r.nY)], got.at[r.y], key, r.y))


def gradients(r):
    half = r.nX // 2
    wide_half = r.C // 2
    flush(r)
    r.part2_a[r.c] = scatter_sum(r, b.chan, r.part2, r.part2_r, b.p3).astype(BF16)
    gather_start(r, b.chan, r.part2_a, b.p4)
    weight_pair(r, r.dt_p, r.dt_b, r.dt_c, (b.d1,))
    spread(r, r.dt_c, r.dt_d, b.d2)
    pair_copy(r, r.mi_p.at[1 - r.k], r.mi_b, b.m1).wait_recv()
    r.mi_c[r.y] = (r.mi_p[r.k].astype(F32) + r.mi_b[...].astype(F32)).astype(BF16)
    for i in range(1, r.nY):
        start(r, line_copy(r, i, r.mi_c.at[r.y], r.mi_c.at[r.y], b.m2, r.y))
    recv_wait(r, b.chan, r.part2_a, b.p4)
    low_adj, bc_adj = unpack(r, r.part2_a[...])
    low_adj = low_adj.astype(BF16)
    r.lg[r.y] = low_adj
    r.bt[r.y] = bc_adj.T[: 2 * r.N].astype(BF16)
    for i in range(1, r.nY):
        start(r, line_copy(r, i, r.lg.at[r.y], r.lg.at[r.y], b.lg, r.y))
        start(r, line_copy(r, i, r.bt.at[r.y], r.bt.at[r.y], b.bt, r.y))
    bc_adj = bc_adj[:, : 2 * r.N].astype(BF16)
    u_adj = r.uu[...] + dot(low_adj, r.w_delta_in[...]) + dot(bc_adj, r.w_bc[...])
    conv_adj = u_adj * r.slope[...]
    r.cpad[pl.ds(0, r.T), :] = conv_adj

    def head_copy(to):
        return rcopy(
            r.cpad.at[pl.ds(0, HEAD)],
            r.cpad.at[pl.ds(r.T, HEAD)],
            r.sems[b.head_s].at[0],
            r.sems[b.head_r].at[0],
            to,
            r.c,
        )

    start(r, head_copy(r.s - 1), r.s > 0)

    @pl.when(r.s == r.nS - 1)
    def _():
        r.cpad[pl.ds(r.T, HEAD), :] = jnp.zeros((HEAD, r.C), F32)

    def x_adj(first, count):
        rows = pl.ds(first, count)
        total = jnp.zeros((count, r.C), F32)
        for k in range(r.KC):
            total = total + r.conv_w[k : k + 1, :] * r.cpad[pl.ds(first + r.KC - 1 - k, count), :]
        r.xg[r.y, rows] = total.astype(BF16)

    def x_copy(i, slot, part):
        rows = pl.ds(part * (r.T // 2), r.T // 2)
        return line_copy(r, i, r.xg.at[slot, rows], r.xg.at[slot, rows], b.xg, slot, part)

    x_adj(0, r.T // 2)
    for i in range(1, r.nY):
        start(r, x_copy(i, r.y, 0))
    for part in range(2):
        for i in range(1, r.nY):
            relay_copy(r, i, lax.rem(r.y + i, r.nY), 1 - r.k, part).wait_recv()
    grad_part(r, 0)
    weight_line(r, r.dt_c, r.dt_d, r.dt_e, (b.d2, b.d3))
    pl.when(r.s < r.nS - 1)(lambda: head_copy(r.s + 1).wait_recv())
    x_adj(r.T // 2, r.T // 2)
    for i in range(1, r.nY):
        start(r, x_copy(i, r.y, 1))
    grad_part(r, 1)
    total = None
    for y2 in range(r.nY):
        pl.when(r.y != y2)(
            line_copy(r, 1, r.mi_c.at[y2], r.mi_c.at[y2], b.m2, y2).wait_recv
        )
        term = r.mi_c[y2].astype(F32)
        total = term if total is None else total + term
    r.mi_e[r.k] = total
    start(r, pair_copy(r, r.mi_e.at[r.k], r.mi_e.at[r.k], b.m3))
    weight_back(r, r.dt_e, b.d3, b.d4)
    for i in range(1, r.nY):
        y2 = lax.rem(r.y + i, r.nY)
        line_copy(r, i, r.ug.at[y2], r.ug.at[y2], b.ug, y2).wait_recv()
        line_copy(r, i, r.lg.at[y2], r.lg.at[y2], b.lg, y2).wait_recv()
        line_copy(r, i, r.bt.at[y2], r.bt.at[y2], b.bt, y2).wait_recv()
    tokens = r.nY * r.T
    term = contract_first(r.lg[...].reshape(tokens, r.R), r.ug[...].reshape(tokens, r.C))
    r.li_p[pl.ds(0, r.R), :] = term.astype(BF16)
    term = dot(r.bt[0], r.ug[0])
    for y2 in range(1, r.nY):
        term = term + dot(r.bt[y2], r.ug[y2])
    r.li_p[pl.ds(r.R, 2 * r.N), :] = term.astype(BF16)
    start(r, pair_copy(r, r.li_p, r.li_b, b.d5))
    def weight(x2, part):
        rows, count = pl.ds(part * (r.T // 2), r.T // 2), r.nY * r.T // 2
        left = r.hg[x2, :, rows].reshape(count, r.DH)
        return contract_first(left, r.xg[:, rows].reshape(count, r.C))

    def arrive(part):
        for i in range(1, r.nY):
            x_copy(i, lax.rem(r.y + i, r.nY), part).wait_recv()

    arrive(0)
    for j in range(r.nX):
        r.wl[j] = weight(j, 0)
    arrive(1)
    for j in range(half):
        x2 = (1 - r.k) * half + j
        r.ws[j] = (r.wl[x2] + weight(x2, 1)).astype(BF16)
    start(r, pair_copy(r, r.ws, r.wr, b.wg))
    for j in range(half):
        x2 = r.k * half + j
        r.wo[j] = r.wl[x2] + weight(x2, 1)
    pair_copy(r, r.ws, r.wr, b.wg).wait_recv()
    r.w_out[...] = (r.wo[...] + r.wr[...].astype(F32)).astype(BF16)
    weight_end(r, r.dt_e, b.d4)
    pair_copy(r, r.mi_e.at[r.k], r.mi_e.at[1 - r.k], b.m3).wait_recv()
    total = r.hs[0].astype(F32)
    for i, c2, dev in peers(r, b.chan):
        for part in range(2):
            rows, at = pl.ds(part * (r.T // 2), r.T // 2), part * r.nC + c2
            got = r.hr.at[c2, rows]
            rcopy(got, got, r.sems[b.hg_s].at[i], r.sems[b.hg_r].at[at], *dev).wait_recv()
        total = total + r.hr[c2].astype(F32)
    r.hidden_out[...] = total.astype(BF16)
    pair_copy(r, r.li_p, r.li_b, b.d5).wait_recv()
    r.li_e[...] = (r.li_p[...].astype(F32) + r.li_b[...].astype(F32)).astype(BF16)
    flush(r)


def finish(r):
    scale = 1.0 / math.sqrt(r.T * r.nS)
    wide_half = r.C // 2
    r.hidden_grad[...] = r.hidden_out[...]
    r.gate_grad[...] = r.gate_out[...]
    r.w_in_grad[...] = r.w_out[...].astype(F32) * scale
    r.w_dt_grad[...] = r.dt_e[...].astype(F32).reshape(r.R, r.C) * scale
    r.w_delta_in_grad[...] = r.li_e[pl.ds(0, r.R), :].astype(F32) * scale
    r.w_bc_grad[...] = r.li_e[pl.ds(r.R, 2 * r.N), :].astype(F32) * scale
    for j in range(2):
        cols = pl.ds(j * wide_half, wide_half)
        r.a_log_grad[:, cols] = r.mi_e[j] * scale


def tables(dim):
    d = types.SimpleNamespace(**dim)
    t, c, n, rows, q = d.T, d.C, d.N, d.R, d.R // d.nS
    buffers = dict(
        hg=((d.nX, d.nY, t, d.DH), BF16),
        wf=((d.nY, d.nX, d.DH, c), BF16),
        xs=((d.nY, t, c), BF16),
        xr=((d.nY, t, c), BF16),
        xt=((d.nY, HALO, c), BF16),
        xpad=((HALO + t, c), F32),
        slope=((t, c), F32),
        gs=((t, c), F32),
        u=((t, c), BF16),
        part=((d.nC, d.PR, LANES), BF16),
        part_r=((d.nC, d.PR, LANES), BF16),
        part_a=((d.nC, d.PR, LANES), BF16),
        pad=((t, LANES), F32),
        low=((t, rows), BF16),
        bcw=((t, LANES), F32),
        pre=((t, c), F32),
        delta=((t, c), F32),
        du=((t, c), F32),
        g=((t, c), F32),
        am=((n, c), F32),
        bx=((t, n, LANES), F32),
        cx=((t, n, LANES), F32),
        sd=((1, c), F32),
        aa=((t * n, c), F32),
        hh=(((t + 1) * n, c), F32),
        hb=((t * n, c), BF16),
        sp=((t, c), F32),
        ef=((2, n, c), BF16),
        st_r=((d.nS, n, c), BF16),
        sd_r=((d.nS, 1, c), F32),
        kept0=((CH * n, c), BF16),
        kept1=((CH * n, c), BF16),
        kept2=((CH * n, c), BF16),
        kept3=((CH * n, c), BF16),
        h_in=((n, c), F32),
        l_in=((n, c), F32),
        bd=((t, CH * n), BF16),
        cd=((t, CH * n), BF16),
        bm=((t, CH * n), F32),
        cm=((t, CH * n), F32),
        y_scan=((t, c), F32),
        s1=((t, c), F32),
        s2=((t, c), F32),
        uu=((t, c), F32),
        part2=((d.nC, d.PR, LANES), BF16),
        part2_r=((d.nC, d.PR, LANES), BF16),
        part2_a=((d.nC, d.PR, LANES), BF16),
        dt_p=((2, d.nY, q, c), BF16),
        dt_b=((d.nY, q, c), BF16),
        dt_c=((d.nY, q, c), BF16),
        dt_d=((d.nY, q, c), BF16),
        dt_e=((2, d.nY, q, c), BF16),
        ug=((d.nY, t, c), BF16),
        lg=((d.nY, t, rows), BF16),
        bt=((d.nY, 2 * n, t), BF16),
        li_p=((rows + 2 * n, c), BF16),
        li_b=((rows + 2 * n, c), BF16),
        li_e=((rows + 2 * n, c), BF16),
        mi_p=((2, n, c // 2), BF16),
        mi_b=((n, c // 2), BF16),
        mi_c=((d.nY, n, c // 2), BF16),
        mi_e=((2, n, c // 2), F32),
        cpad=((t + HEAD, c), F32),
        xg=((d.nY, t, c), BF16),
        hs=((d.nC, t, d.DH), BF16),
        hr=((d.nC, t, d.DH), BF16),
        ws=((d.nX // 2, d.DH, c), BF16),
        wr=((d.nX // 2, d.DH, c), BF16),
        wo=((d.nX // 2, d.DH, c), F32),
        wl=((d.nX, d.DH, c), F32),
        w_out=((d.nX // 2, d.DH, c), BF16),
        hidden_out=((t, d.DH), BF16),
        gate_out=((t, c), BF16),
        hidden_grad=((t, d.DH), BF16),
        gate_grad=((t, c), BF16),
        w_in_grad=((d.nX // 2, d.DH, c), F32),
        w_delta_in_grad=((rows, c), F32),
        w_bc_grad=((2 * n, c), F32),
        w_dt_grad=((rows, c), F32),
        a_log_grad=((n, c), F32),
    )
    sems = dict(loc=2, inp=12)
    pairs = (b.tu, b.wp, b.head, b.wg, b.d1, b.d4, b.d5, b.m1, b.m3)
    lines = (b.xr, b.tail, b.d2, b.d3, b.m2, b.ug, b.lg, b.bt)
    for key in pairs:
        sems[key + "_s"] = sems[key + "_r"] = 1
    for key in lines:
        sems[key + "_s"] = sems[key + "_r"] = d.nY
    for key in (b.xg, b.wy, b.wz):
        sems[key + "_s"] = sems[key + "_r"] = 2 * d.nY
    sems[b.hg_s] = sems[b.hg_r] = 2 * d.nC
    for key in (b.g1, b.g2):
        sems[key + "_s"] = sems[key + "_r"] = d.nX + d.nY
    for key in (b.p1, b.p2, b.p3, b.p4):
        sems[key + "_s"] = sems[key + "_r"] = d.nC
    for key in (b.st, b.sd):
        sems[key + "_s"] = sems[key + "_r"] = d.nS
    return buffers, sems


def run(dim, phases, remote, values, ins, outs, scratch, sem_names, cost):
    buffers, sem_sizes = tables(dim)
    held = [name for name in ins if name not in (b.hidden, b.w_in)] if remote else []

    def body(*refs):
        r = types.SimpleNamespace(**dim)
        r.sent = []
        names = ins + outs + scratch
        for name, ref in zip(names, refs):
            setattr(r, name, ref)
        refs = refs[len(names) :]
        r.sems = dict(zip(sem_names, refs))
        if remote:
            r.given = {name: getattr(r, name) for name in ins}
            for name, ref in zip(held, refs[len(sem_names) :]):
                setattr(r, name, ref)
            r.s, r.c = lax.axis_index(b.seq), lax.axis_index(b.chan)
            r.y, r.k = lax.div(r.s, 2), lax.rem(r.s, 2)
            r.z, r.x = lax.div(r.c, r.nX), lax.rem(r.c, r.nX)
            greet(r, functools.partial(load, r))
        for phase in phases:
            phase(r)

    space = pl.BlockSpec(memory_space=pltpu.VMEM)
    extra = dict(collective_id=0, has_side_effects=True) if remote else {}
    results = pl.pallas_call(
        body,
        out_shape=[jax.ShapeDtypeStruct(*buffers[name]) for name in outs],
        in_specs=[pl.BlockSpec(memory_space=pl.ANY) if remote else space] * len(ins),
        out_specs=[space] * len(outs),
        scratch_shapes=[pltpu.VMEM(*buffers[name]) for name in scratch]
        + [pltpu.SemaphoreType.DMA((sem_sizes[name],)) for name in sem_names]
        + [pltpu.VMEM(values[name].shape, values[name].dtype) for name in held],
        compiler_params=pltpu.CompilerParams(vmem_limit_bytes=56 << 20, **extra),
        cost_estimate=pl.CostEstimate(flops=cost, bytes_accessed=4 << 20, transcendentals=0),
        name=phases[-1].__name__,
    )(*[values[name] for name in ins])
    values.update(zip(outs, results))


ORDER = [b.hidden_grad, b.gate_grad, b.w_in_grad, b.w_delta_in_grad, b.w_bc_grad, b.w_dt_grad, b.a_log_grad]


def per_device(
    seq, chan, hidden, gate_in, out_grad, w_in, conv_w, conv_b, w_delta_in, w_bc, w_dt, dt_bias, a_log, skip_d
):
    lines = seq // 2
    dim = dict(
        nS=seq,
        nC=chan,
        nY=lines,
        nX=chan // lines,
        T=hidden.shape[0],
        DH=hidden.shape[1],
        C=w_in.shape[1],
        R=w_delta_in.shape[0],
        N=a_log.shape[0],
        KC=conv_w.shape[0],
        RP=hidden.shape[0] // chan,
        PR=-(-(hidden.shape[0] // chan) * (w_delta_in.shape[0] // LANES + 1) // 16) * 16,
    )
    v = dict(
        hidden=hidden,
        gate_in=gate_in,
        out_grad=out_grad,
        w_in=w_in.reshape(dim[b.nX] // 2, dim[b.DH], dim[b.C]),
        conv_w=conv_w,
        conv_b=conv_b[None],
        w_delta_in=w_delta_in,
        w_bc=w_bc,
        w_dt=w_dt,
        dt_bias=dt_bias[None],
        a_log=a_log,
        skip_d=skip_d[None],
    )
    raw = [b.hidden_out, b.gate_out, b.w_out, b.dt_e, b.li_e, b.mi_e]
    given = list(v)
    buffers, sems = tables(dim)
    scratch = [name for name in buffers if name not in given + raw + ORDER]
    phases = [take_hidden, project, prepare, scan, gradients]
    run(dim, phases, True, v, given, raw, scratch, list(sems), 2_000_000_000)
    run(dim, [finish], False, v, raw, ORDER, [], [], 1_000_000)
    v[b.w_in_grad] = v[b.w_in_grad].reshape(w_in.shape)
    return tuple(v[name] for name in ORDER)


def solution(mesh):
    placed = (
        P(b.seq, b.chan),
        P(b.seq, b.chan),
        P(b.seq, b.chan),
        P(b.seq, b.chan),
        P(None, b.chan),
        P(b.chan),
        P(None, b.chan),
        P(None, b.chan),
        P(None, b.chan),
        P(b.chan),
        P(None, b.chan),
        P(b.chan),
    )
    return jax.shard_map(
        functools.partial(per_device, mesh.shape[b.seq], mesh.shape[b.chan]),
        mesh=mesh,
        in_specs=placed,
        out_specs=(
            P(b.seq, b.chan),
            P(b.seq, b.chan),
            P(b.seq, b.chan),
            P(None, b.chan),
            P(None, b.chan),
            P(None, b.chan),
            P(None, b.chan),
        ),
        check_vma=False,
    )
```

```python
import functools
import math
import types

import jax
import jax.numpy as jnp
from jax import lax
from jax.experimental import pallas as pl
from jax.experimental.pallas import tpu as pltpu
from jax.sharding import PartitionSpec as P

MESH = pl.DeviceIdType.MESH


class Names:
    def __getattr__(self, name):
        return name


b = Names()
F32, BF16 = jnp.float32, jnp.bfloat16
CH = 16
LANES = 128
HALO = 16
HEAD = 8


def contract_last(left, right):
    return lax.dot_general(left, right, (((1,), (1,)), ((), ())), preferred_element_type=F32)


def contract_first(left, right):
    return lax.dot_general(left, right, (((0,), (0,)), ((), ())), preferred_element_type=F32)


def dot(left, right):
    return jnp.dot(left, right, preferred_element_type=F32)


def silu_slope(values):
    sig = jax.nn.sigmoid(values)
    return sig * (1.0 + values * (1.0 - sig))


def softplus(v):
    return jnp.maximum(v, 0.0) + jnp.log1p(jnp.exp(-jnp.abs(v)))


def rcopy(src, dst, send, recv, seq, chan):
    return pltpu.make_async_remote_copy(
        src_ref=src,
        dst_ref=dst,
        send_sem=send,
        recv_sem=recv,
        device_id=dict(seq=seq, chan=chan),
        device_id_type=MESH,
    )


def ring(r, group):
    if group == b.seq:
        return r.s, r.nS, lambda j: (j, r.c)
    return r.c, r.nC, lambda j: (r.s, j)


def plane_at(r, i):
    shifts = [(dz, dx) for dz in range(r.nY) for dx in range(r.nX)]
    shifts.sort(key=lambda s: min(s[0], r.nY - s[0]) + min(s[1], r.nX - s[1]))
    dz, dx = shifts[i]
    return lax.rem(r.z + dz, r.nY) * r.nX + lax.rem(r.x + dx, r.nX)


def peers(r, group):
    me, n, dev = ring(r, group)
    for i in range(n - 1, 0, -1):
        j = plane_at(r, i) if group == b.chan else lax.rem(me + i, n)
        yield i, j, dev(j)


def start(r, copy, when=None):
    r.sent.append((copy, when))
    if when is None:
        copy.start()
    else:
        pl.when(when)(copy.start)


def flush(r):
    for copy, when in r.sent:
        if when is None:
            copy.wait_send()
        else:
            pl.when(when)(copy.wait_send)
    r.sent.clear()


def scatter_start(r, group, src, dst, key):
    me = ring(r, group)[0]
    for i, j, dev in peers(r, group):
        start(r, rcopy(src.at[j], dst.at[me], r.sems[key + "_s"].at[i], r.sems[key + "_r"].at[me], *dev))


def gather_start(r, group, buf, key):
    me = ring(r, group)[0]
    for i, j, dev in peers(r, group):
        start(r, rcopy(buf.at[me], buf.at[me], r.sems[key + "_s"].at[i], r.sems[key + "_r"].at[me], *dev))


def recv_wait(r, group, buf, key):
    for i, j, dev in peers(r, group):
        rcopy(buf.at[j], buf.at[j], r.sems[key + "_s"].at[i], r.sems[key + "_r"].at[j], *dev).wait_recv()


def scatter_sum(r, group, src, dst, key):
    me = ring(r, group)[0]
    total = src[me].astype(F32)
    recv_wait(r, group, dst, key)
    for i, j, dev in peers(r, group):
        total = total + dst[j].astype(F32)
    return total


def pair_copy(r, src, dst, key):
    return rcopy(src, dst, r.sems[key + "_s"].at[0], r.sems[key + "_r"].at[0], r.y * 2 + 1 - r.k, r.c)


def line_copy(r, i, src, dst, key, slot, part=0):
    at = part * r.nY
    return rcopy(
        src,
        dst,
        r.sems[key + "_s"].at[at + i],
        r.sems[key + "_r"].at[at + slot],
        lax.rem(r.y + i, r.nY) * 2 + r.k,
        r.c,
    )


def plane_copy(r, i, along_x, src, dst, key, slot):
    at, seq = (0 if along_x else r.nX), r.s
    chan = r.z * r.nX + lax.rem(r.x + i, r.nX) if along_x else lax.rem(r.z + i, r.nY) * r.nX + r.x
    return rcopy(src, dst, r.sems[key + "_s"].at[at + i], r.sems[key + "_r"].at[at + slot], seq, chan)


def greet(r, during):
    barrier = pltpu.get_barrier_semaphore()

    def tell(seq, chan):
        pl.semaphore_signal(barrier, inc=1, device_id=dict(seq=seq, chan=chan), device_id_type=MESH)

    pl.when(r.y != r.z)(lambda: tell(r.z * 2 + r.k, r.y * r.nX + r.x))
    for i in range(1, r.nX):
        tell(r.s, r.z * r.nX + lax.rem(r.x + i, r.nX))
        tell(r.s, lax.rem(r.z + i, r.nY) * r.nX + r.x)
    for i, j, dev in peers(r, b.seq):
        tell(*dev)
    during()
    apart = (r.y - r.z) * (r.y - r.z)
    apart = lax.div(apart + r.nY * r.nY - 1, r.nY * r.nY)
    pl.semaphore_wait(barrier, 2 * (r.nX - 1) + r.nS - 1 + apart)


def load(r):
    for at, (name, ref) in enumerate(r.given.items()):
        if name in (b.w_in, b.hidden):
            continue
        pltpu.make_async_copy(ref, getattr(r, name), r.sems[b.inp].at[at]).start()


def need(r, *names):
    for name in names:
        at = list(r.given).index(name)
        pltpu.make_async_copy(r.given[name], getattr(r, name), r.sems[b.inp].at[at]).wait()


def pack(r, low, small):
    r.pad[:, pl.ds(0, 2 * r.N)] = small
    parts = [low[:, at : at + LANES] for at in range(0, r.R, LANES)] + [r.pad[...]]
    parts = [part.reshape(r.nC, r.RP, LANES) for part in parts]
    parts += [jnp.zeros_like(parts[0])] * (r.PR // r.RP - len(parts))
    return jnp.concatenate(parts, 1).astype(BF16)


def unpack(r, pieces):
    pieces = pieces.astype(F32)
    parts = [pieces[:, at : at + r.RP].reshape(r.T, LANES) for at in range(0, r.PR, r.RP)]
    count = r.R // LANES
    return jnp.concatenate(parts[:count], 1), parts[count]


def weight_rows(r, y2, core, part):
    half, cut = r.nX // 2, r.DH // 2
    return r.wf.at[y2, pl.ds(core * half, half), pl.ds(part * cut, cut)]


def weight_copy(r, i, y2, part):
    rows = weight_rows(r, y2, r.k, part)
    return line_copy(r, i, rows, rows, b.wy, y2, part)


def relay_copy(r, i, y2, core, part):
    rows, at = weight_rows(r, y2, core, part), part * r.nY + i
    return rcopy(rows, rows, r.sems[b.wz_s].at[at], r.sems[b.wz_r].at[at], r.y * 2 + 1 - r.k, r.c)


def weight_send(r, part):
    for i in range(1, r.nY):
        start(r, weight_copy(r, i, r.y, part))


def weight_relay(r, part):
    for i in range(1, r.nY):
        y2 = lax.rem(r.y + i, r.nY)
        weight_copy(r, i, y2, part).wait_recv()
        start(r, relay_copy(r, i, y2, r.k, part))


def take_hidden(r):
    half, cut = r.nX // 2, r.T // 2
    mine = r.wf.at[r.y, pl.ds(r.k * half, half)]
    own_w = pltpu.make_async_copy(r.w_in, mine, r.sems[b.loc].at[0])
    own_h = pltpu.make_async_copy(r.hidden, r.hg.at[r.x, r.y], r.sems[b.loc].at[1])
    turn = rcopy(
        r.hidden, r.hg.at[r.x, r.y], r.sems[b.tu_s].at[0], r.sems[b.tu_r].at[0], r.z * 2 + r.k, r.y * r.nX + r.x
    )
    start(r, turn, r.y != r.z)
    start(r, pair_copy(r, r.w_in, mine, b.wp))
    own_w.start()
    pl.when(r.y == r.z)(own_h.start)
    need(r, b.gate_in, b.out_grad, b.a_log)

    gate = r.gate_in[...].astype(F32)
    sig = jax.nn.sigmoid(gate)
    grad = r.out_grad[...].astype(F32)
    r.g[...] = grad * (gate * sig)
    r.gs[...] = grad * (sig * (1.0 + gate * (1.0 - sig)))
    r.am[...] = -jnp.exp(r.a_log[...])
    r.pad[...] = jnp.zeros_like(r.pad)
    own_w.wait()
    pl.when(r.y == r.z)(own_h.wait)

    @pl.when(r.y != r.z)
    def _():
        rcopy(
            r.hidden, r.hg.at[r.x, r.z], r.sems[b.tu_s].at[0], r.sems[b.tu_r].at[0], r.z * 2 + r.k, r.y * r.nX + r.x
        ).wait_recv()

    low, high = pl.ds(0, cut), pl.ds(cut, r.T - cut)
    for i in range(1, r.nX):
        start(r, plane_copy(r, i, True, r.hg.at[r.x, r.z, low], r.hg.at[r.x, r.z, low], b.g1, r.x))
        start(r, plane_copy(r, i, False, r.hg.at[r.x, r.z, high], r.hg.at[r.x, r.z, high], b.g1, r.z))
    weight_send(r, 0)
    for i in range(1, r.nX):
        x2, z2 = lax.rem(r.x + i, r.nX), lax.rem(r.z + i, r.nY)
        plane_copy(r, i, True, r.hg.at[x2, r.z, low], r.hg.at[x2, r.z, low], b.g1, x2).wait_recv()
        plane_copy(r, i, False, r.hg.at[r.x, z2, high], r.hg.at[r.x, z2, high], b.g1, z2).wait_recv()
    for i in range(1, r.nX):
        start(r, plane_copy(r, i, False, r.hg.at[:, r.z, low], r.hg.at[:, r.z, low], b.g2, r.z))
        start(r, plane_copy(r, i, True, r.hg.at[r.x, :, high], r.hg.at[r.x, :, high], b.g2, r.x))
    pair_copy(r, r.w_in, r.wf.at[r.y, pl.ds((1 - r.k) * half, half)], b.wp).wait_recv()
    for i in range(1, r.nX):
        x2, z2 = lax.rem(r.x + i, r.nX), lax.rem(r.z + i, r.nY)
        plane_copy(r, i, True, r.hg.at[x2, :, high], r.hg.at[x2, :, high], b.g2, x2).wait_recv()
        plane_copy(r, i, False, r.hg.at[:, z2, low], r.hg.at[:, z2, low], b.g2, z2).wait_recv()


def tail_copy(r, i, y2, slot):
    return rcopy(
        r.xs.at[i, pl.ds(r.T - HALO, HALO)],
        r.xt.at[slot],
        r.sems[b.tail_s].at[i],
        r.sems[b.tail_r].at[slot],
        y2 * 2 + r.k + 1,
        r.c,
    )


def project(r):
    for i in range(1, r.nY + 1):
        y2 = lax.rem(r.y + i, r.nY)
        total = None
        for j in range(r.nX):
            term = dot(r.hg[j, y2], r.wf[r.y, j])
            total = term if total is None else total + term
        r.xs[i - 1] = total.astype(BF16)
        if i < r.nY:
            start(r, line_copy(r, i, r.xs.at[i - 1], r.xr.at[r.y], b.xr, r.y))
        start(r, tail_copy(r, i - 1, y2, r.y), y2 * 2 + r.k + 1 < r.nS)
    own = total

    @pl.when(r.s == 0)
    def _():
        r.xpad[pl.ds(0, HALO), :] = jnp.zeros((HALO, r.C), F32)

    @pl.when(r.s > 0)
    def _():
        tail = None
        for y2 in range(r.nY):
            tail_copy(r, 0, r.y, y2).wait_recv()
            term = r.xt[y2].astype(F32)
            tail = term if tail is None else tail + term
        r.xpad[pl.ds(0, HALO), :] = tail.astype(BF16).astype(F32)

    for i in range(1, r.nY):
        y2 = lax.rem(r.y + i, r.nY)
        line_copy(r, i, r.xs.at[i - 1], r.xr.at[y2], b.xr, y2).wait_recv()
        own = own + r.xr[y2].astype(F32)
    r.xpad[pl.ds(HALO, r.T), :] = own.astype(BF16).astype(F32)
    need(r, b.conv_w, b.conv_b, b.w_delta_in, b.w_bc)
    conv = jnp.zeros((r.T, r.C), F32) + r.conv_b[...]
    for k in range(r.KC):
        conv = conv + r.conv_w[k : k + 1, :] * r.xpad[pl.ds(HALO - r.KC + 1 + k, r.T), :]
    sig = jax.nn.sigmoid(conv)
    u = (conv * sig).astype(BF16)
    r.u[...] = u
    r.part[...] = pack(r, contract_last(u, r.w_delta_in[...]), contract_last(u, r.w_bc[...]))
    scatter_start(r, b.chan, r.part, r.part_r, b.p1)
    weight_send(r, 1)
    weight_relay(r, 0)
    r.slope[...] = sig * (1.0 + conv * (1.0 - sig))
    r.part_a[r.c] = scatter_sum(r, b.chan, r.part, r.part_r, b.p1).astype(BF16)
    gather_start(r, b.chan, r.part_a, b.p2)
    recv_wait(r, b.chan, r.part_a, b.p2)
    low, r.bcw[...] = unpack(r, r.part_a[...])
    r.low[...] = low.astype(BF16)


def wide(r, b):
    return jnp.concatenate([b] * (r.C // LANES), axis=1) if r.C > LANES else b


def block_mask(r, rows):
    row = lax.broadcasted_iota(jnp.int32, (rows, CH * r.N), 0)
    col = lax.broadcasted_iota(jnp.int32, (rows, CH * r.N), 1)
    return jnp.where(lax.rem(row, CH) == lax.div(col, r.N), 1.0, 0.0).astype(F32)


def pick(r):
    row = lax.broadcasted_iota(jnp.int32, (r.N, CH * r.N), 0)
    col = lax.broadcasted_iota(jnp.int32, (r.N, CH * r.N), 1)
    return jnp.where(lax.rem(col, r.N) == row, 1.0, 0.0).astype(F32)


def prepare(r):
    need(r, b.w_dt, b.dt_bias, b.skip_d)
    pre = dot(r.low[...], r.w_dt[...]) + r.dt_bias[...]
    r.pre[...] = pre
    delta = softplus(pre)
    r.delta[...] = delta
    r.sd[...] = jnp.sum(delta, 0, keepdims=True)
    for i, j, dev in peers(r, b.seq):
        start(r, rcopy(r.sd, r.sd_r.at[r.s], r.sems[b.sd_s].at[i], r.sems[b.sd_r].at[r.s], *dev))
    u = r.u[...].astype(F32)
    r.du[...] = delta * u
    turned = r.bcw[...].T
    for t in range(r.T):
        r.bx[t] = jnp.broadcast_to(turned[0 : r.N, t : t + 1], (r.N, LANES))


def forward_chunk(r, j, h, kept):
    a_mat = r.am[...]
    base = pl.multiple_of(j * CH, CH)
    d = r.delta[pl.ds(base, CH), :]
    du = r.du[pl.ds(base, CH), :]
    for t in range(CH):
        at = pl.multiple_of((base + t) * r.N, r.N)
        if kept is None:
            a = jnp.exp(d[t : t + 1, :] * a_mat)
            r.aa[pl.ds(at, r.N), :] = a
        else:
            a = r.aa[pl.ds(at, r.N), :]
        h = a * h + du[t : t + 1, :] * wide(r, r.bx[base + t])
        if kept is not None:
            r.hh[pl.ds(at + r.N, r.N), :] = h
            kept[pl.ds(t * r.N, r.N), :] = h.astype(BF16)
            r.hb[pl.ds(at, r.N), :] = h.astype(BF16)
    return h


def forward_sums(r, j, kept, mask):
    rows = pl.ds(pl.multiple_of(j * CH, CH), CH)
    states = kept[...]
    r.cm[rows, :] = mask * contract_last(r.g[rows, :].astype(BF16), states)


def outputs(r):
    def one(j, carry):
        rows = pl.ds(pl.multiple_of(j * CH, CH), CH)
        states = r.hb[pl.ds(pl.multiple_of(j * CH * r.N, CH * r.N), CH * r.N), :]
        r.y_scan[rows, :] = dot(r.cd[rows, :], states)
        return carry

    lax.fori_loop(0, r.T // CH, one, 0)


def forward_free(r):
    return lax.fori_loop(0, r.T // CH, lambda j, h: forward_chunk(r, j, h, None), jnp.zeros((r.N, r.C), F32))


def forward_full(r):
    mask = block_mask(r, CH)
    r.hh[pl.ds(0, r.N), :] = r.h_in[...]
    r.kept1[...] = jnp.zeros_like(r.kept1)

    def two(i, h):
        forward_sums(r, jnp.maximum(2 * i - 1, 0), r.kept1, mask)
        h = forward_chunk(r, 2 * i, h, r.kept0)
        forward_sums(r, 2 * i, r.kept0, mask)
        return forward_chunk(r, 2 * i + 1, h, r.kept1)

    lax.fori_loop(0, r.T // CH // 2, two, r.h_in[...])
    forward_sums(r, r.T // CH - 1, r.kept1, mask)


def backward_chunk(r, j, carry, kept):
    a_mat = r.am[...]
    base = pl.multiple_of(j * CH, CH)
    kap, acc = carry
    d = r.delta[pl.ds(base, CH), :]
    g = r.g[pl.ds(base, CH), :]
    for t in reversed(range(CH)):
        at = pl.multiple_of((base + t) * r.N, r.N)
        lam = kap + wide(r, r.cx[base + t]) * g[t : t + 1, :]
        kap = r.aa[pl.ds(at, r.N), :] * lam
        if kept is not None:
            q = kap * r.hh[pl.ds(at, r.N), :]
            acc = acc + q * d[t : t + 1, :]
            kept[0][pl.ds(t * r.N, r.N), :] = lam.astype(BF16)
            kept[1][pl.ds(t * r.N, r.N), :] = (q * a_mat).astype(BF16)
    return kap, acc


def backward_sums(r, j, kept, mask):
    rows = pl.ds(pl.multiple_of(j * CH, CH), CH)
    lam = kept[0][...]
    r.s1[rows, :] = dot(r.bd[rows, :], lam)
    r.s2[rows, :] = dot(mask.astype(BF16), kept[1][...])
    r.bm[rows, :] = mask * contract_last(r.du[rows, :].astype(BF16), lam)


def backward_free(r):
    zero = jnp.zeros((r.N, r.C), F32)
    last = r.T // CH - 1
    return lax.fori_loop(0, last + 1, lambda i, c: backward_chunk(r, last - i, c, None), (zero, zero))[0]


def backward_full(r):
    mask = block_mask(r, CH)
    last = r.T // CH - 1
    even, odd = (r.kept0, r.kept2), (r.kept1, r.kept3)
    for ref in odd:
        ref[...] = jnp.zeros_like(ref)

    def two(i, carry):
        backward_sums(r, jnp.minimum(last - 2 * i + 1, last), odd, mask)
        carry = backward_chunk(r, last - 2 * i, carry, even)
        backward_sums(r, last - 2 * i, even, mask)
        return backward_chunk(r, last - 2 * i - 1, carry, odd)

    a_adj = lax.fori_loop(0, r.T // CH // 2, two, (r.l_in[...], jnp.zeros((r.N, r.C), F32)))[1]
    backward_sums(r, 0, odd, mask)
    return a_adj


def state_copy(r, which, j, slot):
    return rcopy(r.ef.at[which], r.st_r.at[slot], r.sems[b.st_s].at[j], r.sems[b.st_r].at[slot], j, r.c)


def scan(r):
    zero = jnp.zeros((r.N, r.C), F32)
    r.ef[0] = forward_free(r).astype(BF16)
    for j in range(1, r.nS):
        start(r, state_copy(r, 0, j, r.s), j > r.s)
    turned = r.bcw[...].T
    for t in range(r.T):
        r.cx[t] = jnp.broadcast_to(turned[r.N : 2 * r.N, t : t + 1], (r.N, LANES))
    r.ef[1] = backward_free(r).astype(BF16)
    for j in range(r.nS - 1):
        start(r, state_copy(r, 1, j, r.s), j < r.s)
    picked = pick(r)
    tall = block_mask(r, r.T)
    r.bd[...] = (tall * dot(r.bcw[:, pl.ds(0, r.N)], picked)).astype(BF16)
    r.cd[...] = (tall * dot(r.bcw[:, pl.ds(r.N, r.N)], picked)).astype(BF16)

    r.sp[...] = jax.nn.sigmoid(r.pre[...])

    def enter(j, into):
        rcopy(r.sd, r.sd_r.at[j], r.sems[b.sd_s].at[0], r.sems[b.sd_r].at[j], j, r.c).wait_recv()
        state_copy(r, 0, j, j).wait_recv()
        into[...] = jnp.exp(r.am[...] * r.sd_r[j]) * into[...] + r.st_r[j].astype(F32)

    r.h_in[...] = zero
    for j in range(r.nS - 1):
        pl.when(j < r.s)(functools.partial(enter, j, r.h_in))
    forward_full(r)
    r.l_in[...] = zero
    for j in range(r.nS - 1, 0, -1):
        pl.when(j > r.s)(functools.partial(enter, j, r.l_in))
    r.ug[r.y] = r.u[...]
    for i in range(1, r.nY):
        start(r, line_copy(r, i, r.ug.at[r.y], r.ug.at[r.y], b.ug, r.y))
    a_adj = backward_full(r)
    s1 = r.s1[...]
    u = r.u[...].astype(F32)
    pre_adj = ((u * s1 + r.s2[...]) * r.sp[...]).astype(BF16)
    exact = lax.Precision.HIGHEST
    nt = (((1,), (1,)), ((), ()))
    b_adj = lax.dot_general(r.bm[...], picked, nt, precision=exact, preferred_element_type=F32)
    c_adj = lax.dot_general(r.cm[...], picked, nt, precision=exact, preferred_element_type=F32)
    r.part2[...] = pack(r, contract_last(pre_adj, r.w_dt[...]), jnp.concatenate([b_adj, c_adj], 1))
    scatter_start(r, b.chan, r.part2, r.part2_r, b.p3)
    weight_relay(r, 1)
    r.dt_p[...] = contract_first(r.low[...], pre_adj).astype(BF16).reshape(2, r.nY, r.R // r.nS, r.C)
    start(r, pair_copy(r, r.dt_p.at[1 - r.k], r.dt_b, b.d1))
    alog = (a_adj * r.am[...]).astype(BF16)
    wide_half = r.C // 2
    for j in range(2):
        r.mi_p[j] = alog[:, j * wide_half : (j + 1) * wide_half]
    start(r, pair_copy(r, r.mi_p.at[1 - r.k], r.mi_b, b.m1))
    skip = r.skip_d[...]
    r.uu[...] = r.delta[...] * s1 + skip * r.g[...]
    outputs(r)
    r.gate_out[...] = (r.gs[...] * (r.y_scan[...] + skip * u)).astype(BF16)


def grad_copy(r, i, part):
    rows = pl.ds(part * (r.T // 2), r.T // 2)
    c2 = plane_at(r, i)
    at = part * r.nC
    return rcopy(
        r.hs.at[i, rows], r.hr.at[r.c, rows], r.sems[b.hg_s].at[at + i], r.sems[b.hg_r].at[at + r.c], r.s, c2
    )


def grad_part(r, part):
    rows = pl.ds(part * (r.T // 2), r.T // 2)
    for i in range(r.nC - 1, -1, -1):
        c2 = plane_at(r, i)
        term = contract_last(r.xg[r.y, rows], r.wf[lax.div(c2, r.nX), lax.rem(c2, r.nX)])
        r.hs[i, rows] = term.astype(BF16)
        if i:
            start(r, grad_copy(r, i, part))


def weight_pair(r, part, got, summed, key):
    pair_copy(r, part.at[1 - r.k], got, key[0]).wait_recv()
    summed[...] = (part[r.k].astype(F32) + got[...].astype(F32)).astype(BF16)


def weight_line(r, summed, got, whole, keys):
    total = summed[r.y].astype(F32)
    for i in range(1, r.nY):
        y2 = lax.rem(r.y + i, r.nY)
        line_copy(r, i, summed.at[y2], got.at[y2], keys[0], y2).wait_recv()
        total = total + got[y2].astype(F32)
    whole[r.k, r.y] = total.astype(BF16)
    for i in range(1, r.nY):
        start(r, line_copy(r, i, whole.at[r.k, r.y], whole.at[r.k, r.y], keys[1], r.y))


def weight_back(r, whole, line_key, pair_key):
    for i in range(1, r.nY):
        y2 = lax.rem(r.y + i, r.nY)
        line_copy(r, i, whole.at[r.k, y2], whole.at[r.k, y2], line_key, y2).wait_recv()
    start(r, pair_copy(r, whole.at[r.k], whole.at[r.k], pair_key))


def weight_end(r, whole, pair_key):
    pair_copy(r, whole.at[r.k], whole.at[1 - r.k], pair_key).wait_recv()


def spread(r, summed, got, key):
    for i in range(1, r.nY):
        start(r, line_copy(r, i, summed.at[lax.rem(r.y + i, r.nY)], got.at[r.y], key, r.y))


def gradients(r):
    half = r.nX // 2
    wide_half = r.C // 2
    flush(r)
    r.part2_a[r.c] = scatter_sum(r, b.chan, r.part2, r.part2_r, b.p3).astype(BF16)
    gather_start(r, b.chan, r.part2_a, b.p4)
    weight_pair(r, r.dt_p, r.dt_b, r.dt_c, (b.d1,))
    spread(r, r.dt_c, r.dt_d, b.d2)
    pair_copy(r, r.mi_p.at[1 - r.k], r.mi_b, b.m1).wait_recv()
    r.mi_c[r.y] = (r.mi_p[r.k].astype(F32) + r.mi_b[...].astype(F32)).astype(BF16)
    for i in range(1, r.nY):
        start(r, line_copy(r, i, r.mi_c.at[r.y], r.mi_c.at[r.y], b.m2, r.y))
    recv_wait(r, b.chan, r.part2_a, b.p4)
    low_adj, bc_adj = unpack(r, r.part2_a[...])
    low_adj = low_adj.astype(BF16)
    r.lg[r.y] = low_adj
    r.bt[r.y] = bc_adj.T[: 2 * r.N].astype(BF16)
    for i in range(1, r.nY):
        start(r, line_copy(r, i, r.lg.at[r.y], r.lg.at[r.y], b.lg, r.y))
        start(r, line_copy(r, i, r.bt.at[r.y], r.bt.at[r.y], b.bt, r.y))
    bc_adj = bc_adj[:, : 2 * r.N].astype(BF16)
    u_adj = r.uu[...] + dot(low_adj, r.w_delta_in[...]) + dot(bc_adj, r.w_bc[...])
    conv_adj = u_adj * r.slope[...]
    r.cpad[pl.ds(0, r.T), :] = conv_adj

    def head_copy(to):
        return rcopy(
            r.cpad.at[pl.ds(0, HEAD)],
            r.cpad.at[pl.ds(r.T, HEAD)],
            r.sems[b.head_s].at[0],
            r.sems[b.head_r].at[0],
            to,
            r.c,
        )

    start(r, head_copy(r.s - 1), r.s > 0)

    @pl.when(r.s == r.nS - 1)
    def _():
        r.cpad[pl.ds(r.T, HEAD), :] = jnp.zeros((HEAD, r.C), F32)

    def x_adj(first, count):
        rows = pl.ds(first, count)
        total = jnp.zeros((count, r.C), F32)
        for k in range(r.KC):
            total = total + r.conv_w[k : k + 1, :] * r.cpad[pl.ds(first + r.KC - 1 - k, count), :]
        r.xg[r.y, rows] = total.astype(BF16)

    def x_copy(i, slot, part):
        rows = pl.ds(part * (r.T // 2), r.T // 2)
        return line_copy(r, i, r.xg.at[slot, rows], r.xg.at[slot, rows], b.xg, slot, part)

    x_adj(0, r.T // 2)
    for i in range(1, r.nY):
        start(r, x_copy(i, r.y, 0))
    for part in range(2):
        for i in range(1, r.nY):
            relay_copy(r, i, lax.rem(r.y + i, r.nY), 1 - r.k, part).wait_recv()
    grad_part(r, 0)
    weight_line(r, r.dt_c, r.dt_d, r.dt_e, (b.d2, b.d3))
    pl.when(r.s < r.nS - 1)(lambda: head_copy(r.s + 1).wait_recv())
    x_adj(r.T // 2, r.T // 2)
    for i in range(1, r.nY):
        start(r, x_copy(i, r.y, 1))
    grad_part(r, 1)
    total = None
    for y2 in range(r.nY):
        pl.when(r.y != y2)(
            line_copy(r, 1, r.mi_c.at[y2], r.mi_c.at[y2], b.m2, y2).wait_recv
        )
        term = r.mi_c[y2].astype(F32)
        total = term if total is None else total + term
    r.mi_e[r.k] = total
    start(r, pair_copy(r, r.mi_e.at[r.k], r.mi_e.at[r.k], b.m3))
    weight_back(r, r.dt_e, b.d3, b.d4)
    for i in range(1, r.nY):
        y2 = lax.rem(r.y + i, r.nY)
        line_copy(r, i, r.ug.at[y2], r.ug.at[y2], b.ug, y2).wait_recv()
        line_copy(r, i, r.lg.at[y2], r.lg.at[y2], b.lg, y2).wait_recv()
        line_copy(r, i, r.bt.at[y2], r.bt.at[y2], b.bt, y2).wait_recv()
    tokens = r.nY * r.T
    term = contract_first(r.lg[...].reshape(tokens, r.R), r.ug[...].reshape(tokens, r.C))
    r.li_p[pl.ds(0, r.R), :] = term.astype(BF16)
    term = dot(r.bt[0], r.ug[0])
    for y2 in range(1, r.nY):
        term = term + dot(r.bt[y2], r.ug[y2])
    r.li_p[pl.ds(r.R, 2 * r.N), :] = term.astype(BF16)
    start(r, pair_copy(r, r.li_p, r.li_b, b.d5))
    def weight(x2, part):
        rows, count = pl.ds(part * (r.T // 2), r.T // 2), r.nY * r.T // 2
        left = r.hg[x2, :, rows].reshape(count, r.DH)
        return contract_first(left, r.xg[:, rows].reshape(count, r.C))

    def arrive(part):
        for i in range(1, r.nY):
            x_copy(i, lax.rem(r.y + i, r.nY), part).wait_recv()

    arrive(0)
    for j in range(r.nX):
        r.wl[j] = weight(j, 0)
    arrive(1)
    for j in range(half):
        x2 = (1 - r.k) * half + j
        r.ws[j] = (r.wl[x2] + weight(x2, 1)).astype(BF16)
    start(r, pair_copy(r, r.ws, r.wr, b.wg))
    for j in range(half):
        x2 = r.k * half + j
        r.wo[j] = r.wl[x2] + weight(x2, 1)
    pair_copy(r, r.ws, r.wr, b.wg).wait_recv()
    r.w_out[...] = (r.wo[...] + r.wr[...].astype(F32)).astype(BF16)
    flush(r)
    weight_end(r, r.dt_e, b.d4)
    pair_copy(r, r.mi_e.at[r.k], r.mi_e.at[1 - r.k], b.m3).wait_recv()
    total = r.hs[0].astype(F32)
    for i, c2, dev in peers(r, b.chan):
        for part in range(2):
            rows, at = pl.ds(part * (r.T // 2), r.T // 2), part * r.nC + c2
            got = r.hr.at[c2, rows]
            rcopy(got, got, r.sems[b.hg_s].at[i], r.sems[b.hg_r].at[at], *dev).wait_recv()
        total = total + r.hr[c2].astype(F32)
    r.hidden_out[...] = total.astype(BF16)
    pair_copy(r, r.li_p, r.li_b, b.d5).wait_recv()
    r.li_e[...] = (r.li_p[...].astype(F32) + r.li_b[...].astype(F32)).astype(BF16)
    flush(r)


def finish(r):
    scale = 1.0 / math.sqrt(r.T * r.nS)
    wide_half = r.C // 2
    r.hidden_grad[...] = r.hidden_out[...]
    r.gate_grad[...] = r.gate_out[...]
    r.w_in_grad[...] = r.w_out[...].astype(F32) * scale
    r.w_dt_grad[...] = r.dt_e[...].astype(F32).reshape(r.R, r.C) * scale
    r.w_delta_in_grad[...] = r.li_e[pl.ds(0, r.R), :].astype(F32) * scale
    r.w_bc_grad[...] = r.li_e[pl.ds(r.R, 2 * r.N), :].astype(F32) * scale
    for j in range(2):
        cols = pl.ds(j * wide_half, wide_half)
        r.a_log_grad[:, cols] = r.mi_e[j] * scale


def tables(dim):
    d = types.SimpleNamespace(**dim)
    t, c, n, rows, q = d.T, d.C, d.N, d.R, d.R // d.nS
    buffers = dict(
        hg=((d.nX, d.nY, t, d.DH), BF16),
        wf=((d.nY, d.nX, d.DH, c), BF16),
        xs=((d.nY, t, c), BF16),
        xr=((d.nY, t, c), BF16),
        xt=((d.nY, HALO, c), BF16),
        xpad=((HALO + t, c), F32),
        slope=((t, c), F32),
        gs=((t, c), F32),
        u=((t, c), BF16),
        part=((d.nC, d.PR, LANES), BF16),
        part_r=((d.nC, d.PR, LANES), BF16),
        part_a=((d.nC, d.PR, LANES), BF16),
        pad=((t, LANES), F32),
        low=((t, rows), BF16),
        bcw=((t, LANES), F32),
        pre=((t, c), F32),
        delta=((t, c), F32),
        du=((t, c), F32),
        g=((t, c), F32),
        am=((n, c), F32),
        bx=((t, n, LANES), F32),
        cx=((t, n, LANES), F32),
        sd=((1, c), F32),
        aa=((t * n, c), F32),
        hh=(((t + 1) * n, c), F32),
        hb=((t * n, c), BF16),
        sp=((t, c), F32),
        ef=((2, n, c), BF16),
        st_r=((d.nS, n, c), BF16),
        sd_r=((d.nS, 1, c), F32),
        kept0=((CH * n, c), BF16),
        kept1=((CH * n, c), BF16),
        kept2=((CH * n, c), BF16),
        kept3=((CH * n, c), BF16),
        h_in=((n, c), F32),
        l_in=((n, c), F32),
        bd=((t, CH * n), BF16),
        cd=((t, CH * n), BF16),
        bm=((t, CH * n), F32),
        cm=((t, CH * n), F32),
        y_scan=((t, c), F32),
        s1=((t, c), F32),
        s2=((t, c), F32),
        uu=((t, c), F32),
        part2=((d.nC, d.PR, LANES), BF16),
        part2_r=((d.nC, d.PR, LANES), BF16),
        part2_a=((d.nC, d.PR, LANES), BF16),
        dt_p=((2, d.nY, q, c), BF16),
        dt_b=((d.nY, q, c), BF16),
        dt_c=((d.nY, q, c), BF16),
        dt_d=((d.nY, q, c), BF16),
        dt_e=((2, d.nY, q, c), BF16),
        ug=((d.nY, t, c), BF16),
        lg=((d.nY, t, rows), BF16),
        bt=((d.nY, 2 * n, t), BF16),
        li_p=((rows + 2 * n, c), BF16),
        li_b=((rows + 2 * n, c), BF16),
        li_e=((rows + 2 * n, c), BF16),
        mi_p=((2, n, c // 2), BF16),
        mi_b=((n, c // 2), BF16),
        mi_c=((d.nY, n, c // 2), BF16),
        mi_e=((2, n, c // 2), F32),
        cpad=((t + HEAD, c), F32),
        xg=((d.nY, t, c), BF16),
        hs=((d.nC, t, d.DH), BF16),
        hr=((d.nC, t, d.DH), BF16),
        ws=((d.nX // 2, d.DH, c), BF16),
        wr=((d.nX // 2, d.DH, c), BF16),
        wo=((d.nX // 2, d.DH, c), F32),
        wl=((d.nX, d.DH, c), F32),
        w_out=((d.nX // 2, d.DH, c), BF16),
        hidden_out=((t, d.DH), BF16),
        gate_out=((t, c), BF16),
        hidden_grad=((t, d.DH), BF16),
        gate_grad=((t, c), BF16),
        w_in_grad=((d.nX // 2, d.DH, c), F32),
        w_delta_in_grad=((rows, c), F32),
        w_bc_grad=((2 * n, c), F32),
        w_dt_grad=((rows, c), F32),
        a_log_grad=((n, c), F32),
    )
    sems = dict(loc=2, inp=12)
    pairs = (b.tu, b.wp, b.head, b.wg, b.d1, b.d4, b.d5, b.m1, b.m3)
    lines = (b.xr, b.tail, b.d2, b.d3, b.m2, b.ug, b.lg, b.bt)
    for key in pairs:
        sems[key + "_s"] = sems[key + "_r"] = 1
    for key in lines:
        sems[key + "_s"] = sems[key + "_r"] = d.nY
    for key in (b.xg, b.wy, b.wz):
        sems[key + "_s"] = sems[key + "_r"] = 2 * d.nY
    sems[b.hg_s] = sems[b.hg_r] = 2 * d.nC
    for key in (b.g1, b.g2):
        sems[key + "_s"] = sems[key + "_r"] = d.nX + d.nY
    for key in (b.p1, b.p2, b.p3, b.p4):
        sems[key + "_s"] = sems[key + "_r"] = d.nC
    for key in (b.st, b.sd):
        sems[key + "_s"] = sems[key + "_r"] = d.nS
    return buffers, sems


def run(dim, phases, remote, values, ins, outs, scratch, sem_names, cost):
    buffers, sem_sizes = tables(dim)
    held = [name for name in ins if name not in (b.hidden, b.w_in)] if remote else []

    def body(*refs):
        r = types.SimpleNamespace(**dim)
        r.sent = []
        names = ins + outs + scratch
        for name, ref in zip(names, refs):
            setattr(r, name, ref)
        refs = refs[len(names) :]
        r.sems = dict(zip(sem_names, refs))
        if remote:
            r.given = {name: getattr(r, name) for name in ins}
            for name, ref in zip(held, refs[len(sem_names) :]):
                setattr(r, name, ref)
            r.s, r.c = lax.axis_index(b.seq), lax.axis_index(b.chan)
            r.y, r.k = lax.div(r.s, 2), lax.rem(r.s, 2)
            r.z, r.x = lax.div(r.c, r.nX), lax.rem(r.c, r.nX)
            greet(r, functools.partial(load, r))
        for phase in phases:
            phase(r)

    space = pl.BlockSpec(memory_space=pltpu.VMEM)
    extra = dict(collective_id=0, has_side_effects=True) if remote else {}
    results = pl.pallas_call(
        body,
        out_shape=[jax.ShapeDtypeStruct(*buffers[name]) for name in outs],
        in_specs=[pl.BlockSpec(memory_space=pl.ANY) if remote else space] * len(ins),
        out_specs=[space] * len(outs),
        scratch_shapes=[pltpu.VMEM(*buffers[name]) for name in scratch]
        + [pltpu.SemaphoreType.DMA((sem_sizes[name],)) for name in sem_names]
        + [pltpu.VMEM(values[name].shape, values[name].dtype) for name in held],
        compiler_params=pltpu.CompilerParams(vmem_limit_bytes=56 << 20, **extra),
        cost_estimate=pl.CostEstimate(flops=cost, bytes_accessed=4 << 20, transcendentals=0),
        name=phases[-1].__name__,
    )(*[values[name] for name in ins])
    values.update(zip(outs, results))


ORDER = [b.hidden_grad, b.gate_grad, b.w_in_grad, b.w_delta_in_grad, b.w_bc_grad, b.w_dt_grad, b.a_log_grad]


def per_device(
    seq, chan, hidden, gate_in, out_grad, w_in, conv_w, conv_b, w_delta_in, w_bc, w_dt, dt_bias, a_log, skip_d
):
    lines = seq // 2
    dim = dict(
        nS=seq,
        nC=chan,
        nY=lines,
        nX=chan // lines,
        T=hidden.shape[0],
        DH=hidden.shape[1],
        C=w_in.shape[1],
        R=w_delta_in.shape[0],
        N=a_log.shape[0],
        KC=conv_w.shape[0],
        RP=hidden.shape[0] // chan,
        PR=-(-(hidden.shape[0] // chan) * (w_delta_in.shape[0] // LANES + 1) // 16) * 16,
    )
    v = dict(
        hidden=hidden,
        gate_in=gate_in,
        out_grad=out_grad,
        w_in=w_in.reshape(dim[b.nX] // 2, dim[b.DH], dim[b.C]),
        conv_w=conv_w,
        conv_b=conv_b[None],
        w_delta_in=w_delta_in,
        w_bc=w_bc,
        w_dt=w_dt,
        dt_bias=dt_bias[None],
        a_log=a_log,
        skip_d=skip_d[None],
    )
    raw = [b.hidden_out, b.gate_out, b.w_out, b.dt_e, b.li_e, b.mi_e]
    given = list(v)
    buffers, sems = tables(dim)
    scratch = [name for name in buffers if name not in given + raw + ORDER]
    phases = [take_hidden, project, prepare, scan, gradients]
    run(dim, phases, True, v, given, raw, scratch, list(sems), 2_000_000_000)
    run(dim, [finish], False, v, raw, ORDER, [], [], 1_000_000)
    v[b.w_in_grad] = v[b.w_in_grad].reshape(w_in.shape)
    return tuple(v[name] for name in ORDER)


def solution(mesh):
    placed = (
        P(b.seq, b.chan),
        P(b.seq, b.chan),
        P(b.seq, b.chan),
        P(b.seq, b.chan),
        P(None, b.chan),
        P(b.chan),
        P(None, b.chan),
        P(None, b.chan),
        P(None, b.chan),
        P(b.chan),
        P(None, b.chan),
        P(b.chan),
    )
    return jax.shard_map(
        functools.partial(per_device, mesh.shape[b.seq], mesh.shape[b.chan]),
        mesh=mesh,
        in_specs=placed,
        out_specs=(
            P(b.seq, b.chan),
            P(b.seq, b.chan),
            P(b.seq, b.chan),
            P(None, b.chan),
            P(None, b.chan),
            P(None, b.chan),
            P(None, b.chan),
        ),
        check_vma=False,
    )
```

```python
import functools
import math
import types

import jax
import jax.numpy as jnp
from jax import lax
from jax.experimental import pallas as pl
from jax.experimental.pallas import tpu as pltpu
from jax.sharding import PartitionSpec as P

MESH = pl.DeviceIdType.MESH


class Names:
    def __getattr__(self, name):
        return name


b = Names()
F32, BF16 = jnp.float32, jnp.bfloat16
CH = 16
LANES = 128
HALO = 16
HEAD = 8


def contract_last(left, right):
    return lax.dot_general(left, right, (((1,), (1,)), ((), ())), preferred_element_type=F32)


def contract_first(left, right):
    return lax.dot_general(left, right, (((0,), (0,)), ((), ())), preferred_element_type=F32)


def dot(left, right):
    return jnp.dot(left, right, preferred_element_type=F32)


def silu_slope(values):
    sig = jax.nn.sigmoid(values)
    return sig * (1.0 + values * (1.0 - sig))


def softplus(v):
    return jnp.maximum(v, 0.0) + jnp.log1p(jnp.exp(-jnp.abs(v)))


def rcopy(src, dst, send, recv, seq, chan):
    return pltpu.make_async_remote_copy(
        src_ref=src,
        dst_ref=dst,
        send_sem=send,
        recv_sem=recv,
        device_id=dict(seq=seq, chan=chan),
        device_id_type=MESH,
    )


def ring(r, group):
    if group == b.seq:
        return r.s, r.nS, lambda j: (j, r.c)
    return r.c, r.nC, lambda j: (r.s, j)


def plane_at(r, i):
    shifts = [(dz, dx) for dz in range(r.nY) for dx in range(r.nX)]
    shifts.sort(key=lambda s: min(s[0], r.nY - s[0]) + min(s[1], r.nX - s[1]))
    dz, dx = shifts[i]
    return lax.rem(r.z + dz, r.nY) * r.nX + lax.rem(r.x + dx, r.nX)


def peers(r, group):
    me, n, dev = ring(r, group)
    for i in range(n - 1, 0, -1):
        j = plane_at(r, i) if group == b.chan else lax.rem(me + i, n)
        yield i, j, dev(j)


def start(r, copy, when=None):
    r.sent.append((copy, when))
    if when is None:
        copy.start()
    else:
        pl.when(when)(copy.start)


def flush(r):
    for copy, when in r.sent:
        if when is None:
            copy.wait_send()
        else:
            pl.when(when)(copy.wait_send)
    r.sent.clear()


def scatter_start(r, group, src, dst, key):
    me = ring(r, group)[0]
    for i, j, dev in peers(r, group):
        start(r, rcopy(src.at[j], dst.at[me], r.sems[key + "_s"].at[i], r.sems[key + "_r"].at[me], *dev))


def gather_start(r, group, buf, key):
    me = ring(r, group)[0]
    for i, j, dev in peers(r, group):
        start(r, rcopy(buf.at[me], buf.at[me], r.sems[key + "_s"].at[i], r.sems[key + "_r"].at[me], *dev))


def recv_wait(r, group, buf, key):
    for i, j, dev in peers(r, group):
        rcopy(buf.at[j], buf.at[j], r.sems[key + "_s"].at[i], r.sems[key + "_r"].at[j], *dev).wait_recv()


def scatter_sum(r, group, src, dst, key):
    me = ring(r, group)[0]
    total = src[me].astype(F32)
    recv_wait(r, group, dst, key)
    for i, j, dev in peers(r, group):
        total = total + dst[j].astype(F32)
    return total


def pair_copy(r, src, dst, key):
    return rcopy(src, dst, r.sems[key + "_s"].at[0], r.sems[key + "_r"].at[0], r.y * 2 + 1 - r.k, r.c)


def line_copy(r, i, src, dst, key, slot, part=0):
    at = part * r.nY
    return rcopy(
        src,
        dst,
        r.sems[key + "_s"].at[at + i],
        r.sems[key + "_r"].at[at + slot],
        lax.rem(r.y + i, r.nY) * 2 + r.k,
        r.c,
    )


def far_first(n):
    return sorted(range(1, n), key=lambda i: -min(i, n - i))


def plane_copy(r, i, along_x, src, dst, key, slot):
    at, seq = (0 if along_x else r.nX), r.s
    chan = r.z * r.nX + lax.rem(r.x + i, r.nX) if along_x else lax.rem(r.z + i, r.nY) * r.nX + r.x
    return rcopy(src, dst, r.sems[key + "_s"].at[at + i], r.sems[key + "_r"].at[at + slot], seq, chan)


def greet(r, during):
    barrier = pltpu.get_barrier_semaphore()

    def tell(seq, chan):
        pl.semaphore_signal(barrier, inc=1, device_id=dict(seq=seq, chan=chan), device_id_type=MESH)

    pl.when(r.y != r.z)(lambda: tell(r.z * 2 + r.k, r.y * r.nX + r.x))
    for i in range(1, r.nX):
        tell(r.s, r.z * r.nX + lax.rem(r.x + i, r.nX))
        tell(r.s, lax.rem(r.z + i, r.nY) * r.nX + r.x)
    for i, j, dev in peers(r, b.seq):
        tell(*dev)
    during()
    apart = (r.y - r.z) * (r.y - r.z)
    apart = lax.div(apart + r.nY * r.nY - 1, r.nY * r.nY)
    pl.semaphore_wait(barrier, 2 * (r.nX - 1) + r.nS - 1 + apart)


def load(r):
    for at, (name, ref) in enumerate(r.given.items()):
        if name in (b.w_in, b.hidden):
            continue
        pltpu.make_async_copy(ref, getattr(r, name), r.sems[b.inp].at[at]).start()


def need(r, *names):
    for name in names:
        at = list(r.given).index(name)
        pltpu.make_async_copy(r.given[name], getattr(r, name), r.sems[b.inp].at[at]).wait()


def pack(r, low, small):
    r.pad[:, pl.ds(0, 2 * r.N)] = small
    parts = [low[:, at : at + LANES] for at in range(0, r.R, LANES)] + [r.pad[...]]
    parts = [part.reshape(r.nC, r.RP, LANES) for part in parts]
    parts += [jnp.zeros_like(parts[0])] * (r.PR // r.RP - len(parts))
    return jnp.concatenate(parts, 1).astype(BF16)


def unpack(r, pieces):
    pieces = pieces.astype(F32)
    parts = [pieces[:, at : at + r.RP].reshape(r.T, LANES) for at in range(0, r.PR, r.RP)]
    count = r.R // LANES
    return jnp.concatenate(parts[:count], 1), parts[count]


def weight_rows(r, y2, core, part):
    half, cut = r.nX // 2, r.DH // 2
    return r.wf.at[y2, pl.ds(core * half, half), pl.ds(part * cut, cut)]


def weight_copy(r, i, y2, part):
    rows = weight_rows(r, y2, r.k, part)
    return line_copy(r, i, rows, rows, b.wy, y2, part)


def relay_copy(r, i, y2, core, part):
    rows, at = weight_rows(r, y2, core, part), part * r.nY + i
    return rcopy(rows, rows, r.sems[b.wz_s].at[at], r.sems[b.wz_r].at[at], r.y * 2 + 1 - r.k, r.c)


def weight_send(r, part):
    for i in range(1, r.nY):
        start(r, weight_copy(r, i, r.y, part))


def weight_relay(r, part):
    for i in range(1, r.nY):
        y2 = lax.rem(r.y + i, r.nY)
        weight_copy(r, i, y2, part).wait_recv()
        start(r, relay_copy(r, i, y2, r.k, part))


def take_hidden(r):
    half, cut = r.nX // 2, r.T // 2
    mine = r.wf.at[r.y, pl.ds(r.k * half, half)]
    own_w = pltpu.make_async_copy(r.w_in, mine, r.sems[b.loc].at[0])
    own_h = pltpu.make_async_copy(r.hidden, r.hg.at[r.x, r.y], r.sems[b.loc].at[1])
    turn = rcopy(
        r.hidden, r.hg.at[r.x, r.y], r.sems[b.tu_s].at[0], r.sems[b.tu_r].at[0], r.z * 2 + r.k, r.y * r.nX + r.x
    )
    start(r, turn, r.y != r.z)
    start(r, pair_copy(r, r.w_in, mine, b.wp))
    own_w.start()
    pl.when(r.y == r.z)(own_h.start)
    need(r, b.gate_in, b.out_grad, b.a_log)

    gate = r.gate_in[...].astype(F32)
    sig = jax.nn.sigmoid(gate)
    grad = r.out_grad[...].astype(F32)
    r.g[...] = grad * (gate * sig)
    r.gs[...] = grad * (sig * (1.0 + gate * (1.0 - sig)))
    r.am[...] = -jnp.exp(r.a_log[...])
    r.pad[...] = jnp.zeros_like(r.pad)
    own_w.wait()
    pl.when(r.y == r.z)(own_h.wait)

    @pl.when(r.y != r.z)
    def _():
        rcopy(
            r.hidden, r.hg.at[r.x, r.z], r.sems[b.tu_s].at[0], r.sems[b.tu_r].at[0], r.z * 2 + r.k, r.y * r.nX + r.x
        ).wait_recv()

    low, high = pl.ds(0, cut), pl.ds(cut, r.T - cut)
    for i in far_first(r.nX):
        start(r, plane_copy(r, i, True, r.hg.at[r.x, r.z, low], r.hg.at[r.x, r.z, low], b.g1, r.x))
        start(r, plane_copy(r, i, False, r.hg.at[r.x, r.z, high], r.hg.at[r.x, r.z, high], b.g1, r.z))
    weight_send(r, 0)
    for i in range(1, r.nX):
        x2, z2 = lax.rem(r.x + i, r.nX), lax.rem(r.z + i, r.nY)
        plane_copy(r, i, True, r.hg.at[x2, r.z, low], r.hg.at[x2, r.z, low], b.g1, x2).wait_recv()
        plane_copy(r, i, False, r.hg.at[r.x, z2, high], r.hg.at[r.x, z2, high], b.g1, z2).wait_recv()
    for i in far_first(r.nX):
        start(r, plane_copy(r, i, False, r.hg.at[:, r.z, low], r.hg.at[:, r.z, low], b.g2, r.z))
        start(r, plane_copy(r, i, True, r.hg.at[r.x, :, high], r.hg.at[r.x, :, high], b.g2, r.x))
    pair_copy(r, r.w_in, r.wf.at[r.y, pl.ds((1 - r.k) * half, half)], b.wp).wait_recv()
    for i in range(1, r.nX):
        x2, z2 = lax.rem(r.x + i, r.nX), lax.rem(r.z + i, r.nY)
        plane_copy(r, i, True, r.hg.at[x2, :, high], r.hg.at[x2, :, high], b.g2, x2).wait_recv()
        plane_copy(r, i, False, r.hg.at[:, z2, low], r.hg.at[:, z2, low], b.g2, z2).wait_recv()


def tail_copy(r, i, y2, slot):
    return rcopy(
        r.xs.at[i, pl.ds(r.T - HALO, HALO)],
        r.xt.at[slot],
        r.sems[b.tail_s].at[i],
        r.sems[b.tail_r].at[slot],
        y2 * 2 + r.k + 1,
        r.c,
    )


def project(r):
    for i in range(1, r.nY + 1):
        y2 = lax.rem(r.y + i, r.nY)
        total = None
        for j in range(r.nX):
            term = dot(r.hg[j, y2], r.wf[r.y, j])
            total = term if total is None else total + term
        r.xs[i - 1] = total.astype(BF16)
        if i < r.nY:
            start(r, line_copy(r, i, r.xs.at[i - 1], r.xr.at[r.y], b.xr, r.y))
        start(r, tail_copy(r, i - 1, y2, r.y), y2 * 2 + r.k + 1 < r.nS)
    own = total

    @pl.when(r.s == 0)
    def _():
        r.xpad[pl.ds(0, HALO), :] = jnp.zeros((HALO, r.C), F32)

    @pl.when(r.s > 0)
    def _():
        tail = None
        for y2 in range(r.nY):
            tail_copy(r, 0, r.y, y2).wait_recv()
            term = r.xt[y2].astype(F32)
            tail = term if tail is None else tail + term
        r.xpad[pl.ds(0, HALO), :] = tail.astype(BF16).astype(F32)

    for i in range(1, r.nY):
        y2 = lax.rem(r.y + i, r.nY)
        line_copy(r, i, r.xs.at[i - 1], r.xr.at[y2], b.xr, y2).wait_recv()
        own = own + r.xr[y2].astype(F32)
    r.xpad[pl.ds(HALO, r.T), :] = own.astype(BF16).astype(F32)
    need(r, b.conv_w, b.conv_b, b.w_delta_in, b.w_bc)
    conv = jnp.zeros((r.T, r.C), F32) + r.conv_b[...]
    for k in range(r.KC):
        conv = conv + r.conv_w[k : k + 1, :] * r.xpad[pl.ds(HALO - r.KC + 1 + k, r.T), :]
    sig = jax.nn.sigmoid(conv)
    u = (conv * sig).astype(BF16)
    r.u[...] = u
    r.part[...] = pack(r, contract_last(u, r.w_delta_in[...]), contract_last(u, r.w_bc[...]))
    scatter_start(r, b.chan, r.part, r.part_r, b.p1)
    weight_send(r, 1)
    weight_relay(r, 0)
    r.slope[...] = sig * (1.0 + conv * (1.0 - sig))
    r.part_a[r.c] = scatter_sum(r, b.chan, r.part, r.part_r, b.p1).astype(BF16)
    gather_start(r, b.chan, r.part_a, b.p2)
    recv_wait(r, b.chan, r.part_a, b.p2)
    low, r.bcw[...] = unpack(r, r.part_a[...])
    r.low[...] = low.astype(BF16)


def wide(r, b):
    return jnp.concatenate([b] * (r.C // LANES), axis=1) if r.C > LANES else b


def block_mask(r, rows):
    row = lax.broadcasted_iota(jnp.int32, (rows, CH * r.N), 0)
    col = lax.broadcasted_iota(jnp.int32, (rows, CH * r.N), 1)
    return jnp.where(lax.rem(row, CH) == lax.div(col, r.N), 1.0, 0.0).astype(F32)


def pick(r):
    row = lax.broadcasted_iota(jnp.int32, (r.N, CH * r.N), 0)
    col = lax.broadcasted_iota(jnp.int32, (r.N, CH * r.N), 1)
    return jnp.where(lax.rem(col, r.N) == row, 1.0, 0.0).astype(F32)


def prepare(r):
    need(r, b.w_dt, b.dt_bias, b.skip_d)
    pre = dot(r.low[...], r.w_dt[...]) + r.dt_bias[...]
    r.pre[...] = pre
    delta = softplus(pre)
    r.delta[...] = delta
    r.sd[...] = jnp.sum(delta, 0, keepdims=True)
    for i, j, dev in peers(r, b.seq):
        start(r, rcopy(r.sd, r.sd_r.at[r.s], r.sems[b.sd_s].at[i], r.sems[b.sd_r].at[r.s], *dev))
    u = r.u[...].astype(F32)
    r.du[...] = delta * u
    turned = r.bcw[...].T
    for t in range(r.T):
        r.bx[t] = jnp.broadcast_to(turned[0 : r.N, t : t + 1], (r.N, LANES))


def forward_chunk(r, j, h, kept):
    a_mat = r.am[...]
    base = pl.multiple_of(j * CH, CH)
    d = r.delta[pl.ds(base, CH), :]
    du = r.du[pl.ds(base, CH), :]
    for t in range(CH):
        at = pl.multiple_of((base + t) * r.N, r.N)
        if kept is None:
            a = jnp.exp(d[t : t + 1, :] * a_mat)
            r.aa[pl.ds(at, r.N), :] = a
        else:
            a = r.aa[pl.ds(at, r.N), :]
        h = a * h + du[t : t + 1, :] * wide(r, r.bx[base + t])
        if kept is not None:
            r.hh[pl.ds(at + r.N, r.N), :] = h
            kept[pl.ds(t * r.N, r.N), :] = h.astype(BF16)
            r.hb[pl.ds(at, r.N), :] = h.astype(BF16)
    return h


def forward_sums(r, j, kept, mask):
    rows = pl.ds(pl.multiple_of(j * CH, CH), CH)
    states = kept[...]
    r.cm[rows, :] = mask * contract_last(r.g[rows, :].astype(BF16), states)


def outputs(r):
    def one(j, carry):
        rows = pl.ds(pl.multiple_of(j * CH, CH), CH)
        states = r.hb[pl.ds(pl.multiple_of(j * CH * r.N, CH * r.N), CH * r.N), :]
        r.y_scan[rows, :] = dot(r.cd[rows, :], states)
        return carry

    lax.fori_loop(0, r.T // CH, one, 0)


def forward_free(r):
    return lax.fori_loop(0, r.T // CH, lambda j, h: forward_chunk(r, j, h, None), jnp.zeros((r.N, r.C), F32))


def forward_full(r):
    mask = block_mask(r, CH)
    r.hh[pl.ds(0, r.N), :] = r.h_in[...]
    r.kept1[...] = jnp.zeros_like(r.kept1)

    def two(i, h):
        forward_sums(r, jnp.maximum(2 * i - 1, 0), r.kept1, mask)
        h = forward_chunk(r, 2 * i, h, r.kept0)
        forward_sums(r, 2 * i, r.kept0, mask)
        return forward_chunk(r, 2 * i + 1, h, r.kept1)

    lax.fori_loop(0, r.T // CH // 2, two, r.h_in[...])
    forward_sums(r, r.T // CH - 1, r.kept1, mask)


def backward_chunk(r, j, carry, kept):
    a_mat = r.am[...]
    base = pl.multiple_of(j * CH, CH)
    kap, acc = carry
    d = r.delta[pl.ds(base, CH), :]
    g = r.g[pl.ds(base, CH), :]
    for t in reversed(range(CH)):
        at = pl.multiple_of((base + t) * r.N, r.N)
        lam = kap + wide(r, r.cx[base + t]) * g[t : t + 1, :]
        kap = r.aa[pl.ds(at, r.N), :] * lam
        if kept is not None:
            q = kap * r.hh[pl.ds(at, r.N), :]
            acc = acc + q * d[t : t + 1, :]
            kept[0][pl.ds(t * r.N, r.N), :] = lam.astype(BF16)
            kept[1][pl.ds(t * r.N, r.N), :] = (q * a_mat).astype(BF16)
    return kap, acc


def backward_sums(r, j, kept, mask):
    rows = pl.ds(pl.multiple_of(j * CH, CH), CH)
    lam = kept[0][...]
    r.s1[rows, :] = dot(r.bd[rows, :], lam)
    r.s2[rows, :] = dot(mask.astype(BF16), kept[1][...])
    r.bm[rows, :] = mask * contract_last(r.du[rows, :].astype(BF16), lam)


def backward_free(r):
    zero = jnp.zeros((r.N, r.C), F32)
    last = r.T // CH - 1
    return lax.fori_loop(0, last + 1, lambda i, c: backward_chunk(r, last - i, c, None), (zero, zero))[0]


def backward_full(r):
    mask = block_mask(r, CH)
    last = r.T // CH - 1
    even, odd = (r.kept0, r.kept2), (r.kept1, r.kept3)
    for ref in odd:
        ref[...] = jnp.zeros_like(ref)

    def two(i, carry):
        backward_sums(r, jnp.minimum(last - 2 * i + 1, last), odd, mask)
        carry = backward_chunk(r, last - 2 * i, carry, even)
        backward_sums(r, last - 2 * i, even, mask)
        return backward_chunk(r, last - 2 * i - 1, carry, odd)

    a_adj = lax.fori_loop(0, r.T // CH // 2, two, (r.l_in[...], jnp.zeros((r.N, r.C), F32)))[1]
    backward_sums(r, 0, odd, mask)
    return a_adj


def state_copy(r, which, j, slot):
    return rcopy(r.ef.at[which], r.st_r.at[slot], r.sems[b.st_s].at[j], r.sems[b.st_r].at[slot], j, r.c)


def scan(r):
    zero = jnp.zeros((r.N, r.C), F32)
    r.ef[0] = forward_free(r).astype(BF16)
    for j in range(1, r.nS):
        start(r, state_copy(r, 0, j, r.s), j > r.s)
    turned = r.bcw[...].T
    for t in range(r.T):
        r.cx[t] = jnp.broadcast_to(turned[r.N : 2 * r.N, t : t + 1], (r.N, LANES))
    r.ef[1] = backward_free(r).astype(BF16)
    for j in range(r.nS - 1):
        start(r, state_copy(r, 1, j, r.s), j < r.s)
    picked = pick(r)
    tall = block_mask(r, r.T)
    r.bd[...] = (tall * dot(r.bcw[:, pl.ds(0, r.N)], picked)).astype(BF16)
    r.cd[...] = (tall * dot(r.bcw[:, pl.ds(r.N, r.N)], picked)).astype(BF16)

    r.sp[...] = jax.nn.sigmoid(r.pre[...])

    def enter(j, into):
        rcopy(r.sd, r.sd_r.at[j], r.sems[b.sd_s].at[0], r.sems[b.sd_r].at[j], j, r.c).wait_recv()
        state_copy(r, 0, j, j).wait_recv()
        into[...] = jnp.exp(r.am[...] * r.sd_r[j]) * into[...] + r.st_r[j].astype(F32)

    r.h_in[...] = zero
    for j in range(r.nS - 1):
        pl.when(j < r.s)(functools.partial(enter, j, r.h_in))
    forward_full(r)
    r.l_in[...] = zero
    for j in range(r.nS - 1, 0, -1):
        pl.when(j > r.s)(functools.partial(enter, j, r.l_in))
    r.ug[r.y] = r.u[...]
    for i in range(1, r.nY):
        start(r, line_copy(r, i, r.ug.at[r.y], r.ug.at[r.y], b.ug, r.y))
    a_adj = backward_full(r)
    s1 = r.s1[...]
    u = r.u[...].astype(F32)
    pre_adj = ((u * s1 + r.s2[...]) * r.sp[...]).astype(BF16)
    exact = lax.Precision.HIGHEST
    nt = (((1,), (1,)), ((), ()))
    b_adj = lax.dot_general(r.bm[...], picked, nt, precision=exact, preferred_element_type=F32)
    c_adj = lax.dot_general(r.cm[...], picked, nt, precision=exact, preferred_element_type=F32)
    r.part2[...] = pack(r, contract_last(pre_adj, r.w_dt[...]), jnp.concatenate([b_adj, c_adj], 1))
    scatter_start(r, b.chan, r.part2, r.part2_r, b.p3)
    weight_relay(r, 1)
    r.dt_p[...] = contract_first(r.low[...], pre_adj).astype(BF16).reshape(2, r.nY, r.R // r.nS, r.C)
    start(r, pair_copy(r, r.dt_p.at[1 - r.k], r.dt_b, b.d1))
    alog = (a_adj * r.am[...]).astype(BF16)
    wide_half = r.C // 2
    for j in range(2):
        r.mi_p[j] = alog[:, j * wide_half : (j + 1) * wide_half]
    start(r, pair_copy(r, r.mi_p.at[1 - r.k], r.mi_b, b.m1))
    skip = r.skip_d[...]
    r.uu[...] = r.delta[...] * s1 + skip * r.g[...]
    outputs(r)
    r.gate_out[...] = (r.gs[...] * (r.y_scan[...] + skip * u)).astype(BF16)


def grad_copy(r, i, part):
    rows = pl.ds(part * (r.T // 2), r.T // 2)
    c2 = plane_at(r, i)
    at = part * r.nC
    return rcopy(
        r.hs.at[i, rows], r.hr.at[r.c, rows], r.sems[b.hg_s].at[at + i], r.sems[b.hg_r].at[at + r.c], r.s, c2
    )


def grad_part(r, part):
    rows = pl.ds(part * (r.T // 2), r.T // 2)
    for i in range(r.nC - 1, -1, -1):
        c2 = plane_at(r, i)
        term = contract_last(r.xg[r.y, rows], r.wf[lax.div(c2, r.nX), lax.rem(c2, r.nX)])
        r.hs[i, rows] = term.astype(BF16)
        if i:
            start(r, grad_copy(r, i, part))


def weight_pair(r, part, got, summed, key):
    pair_copy(r, part.at[1 - r.k], got, key[0]).wait_recv()
    summed[...] = (part[r.k].astype(F32) + got[...].astype(F32)).astype(BF16)


def weight_line(r, summed, got, whole, keys):
    total = summed[r.y].astype(F32)
    for i in range(1, r.nY):
        y2 = lax.rem(r.y + i, r.nY)
        line_copy(r, i, summed.at[y2], got.at[y2], keys[0], y2).wait_recv()
        total = total + got[y2].astype(F32)
    whole[r.k, r.y] = total.astype(BF16)
    for i in range(1, r.nY):
        start(r, line_copy(r, i, whole.at[r.k, r.y], whole.at[r.k, r.y], keys[1], r.y))


def weight_back(r, whole, line_key, pair_key):
    for i in range(1, r.nY):
        y2 = lax.rem(r.y + i, r.nY)
        line_copy(r, i, whole.at[r.k, y2], whole.at[r.k, y2], line_key, y2).wait_recv()
    start(r, pair_copy(r, whole.at[r.k], whole.at[r.k], pair_key))


def weight_end(r, whole, pair_key):
    pair_copy(r, whole.at[r.k], whole.at[1 - r.k], pair_key).wait_recv()


def spread(r, summed, got, key):
    for i in range(1, r.nY):
        start(r, line_copy(r, i, summed.at[lax.rem(r.y + i, r.nY)], got.at[r.y], key, r.y))


def gradients(r):
    half = r.nX // 2
    wide_half = r.C // 2
    flush(r)
    r.part2_a[r.c] = scatter_sum(r, b.chan, r.part2, r.part2_r, b.p3).astype(BF16)
    gather_start(r, b.chan, r.part2_a, b.p4)
    weight_pair(r, r.dt_p, r.dt_b, r.dt_c, (b.d1,))
    spread(r, r.dt_c, r.dt_d, b.d2)
    pair_copy(r, r.mi_p.at[1 - r.k], r.mi_b, b.m1).wait_recv()
    r.mi_c[r.y] = (r.mi_p[r.k].astype(F32) + r.mi_b[...].astype(F32)).astype(BF16)
    for i in range(1, r.nY):
        start(r, line_copy(r, i, r.mi_c.at[r.y], r.mi_c.at[r.y], b.m2, r.y))
    recv_wait(r, b.chan, r.part2_a, b.p4)
    low_adj, bc_adj = unpack(r, r.part2_a[...])
    low_adj = low_adj.astype(BF16)
    r.lg[r.y] = low_adj
    r.bt[r.y] = bc_adj.T[: 2 * r.N].astype(BF16)
    for i in far_first(r.nY):
        start(r, line_copy(r, i, r.lg.at[r.y], r.lg.at[r.y], b.lg, r.y))
        start(r, line_copy(r, i, r.bt.at[r.y], r.bt.at[r.y], b.bt, r.y))
    bc_adj = bc_adj[:, : 2 * r.N].astype(BF16)
    u_adj = r.uu[...] + dot(low_adj, r.w_delta_in[...]) + dot(bc_adj, r.w_bc[...])
    conv_adj = u_adj * r.slope[...]
    r.cpad[pl.ds(0, r.T), :] = conv_adj

    def head_copy(to):
        return rcopy(
            r.cpad.at[pl.ds(0, HEAD)],
            r.cpad.at[pl.ds(r.T, HEAD)],
            r.sems[b.head_s].at[0],
            r.sems[b.head_r].at[0],
            to,
            r.c,
        )

    start(r, head_copy(r.s - 1), r.s > 0)

    @pl.when(r.s == r.nS - 1)
    def _():
        r.cpad[pl.ds(r.T, HEAD), :] = jnp.zeros((HEAD, r.C), F32)

    def x_adj(first, count):
        rows = pl.ds(first, count)
        total = jnp.zeros((count, r.C), F32)
        for k in range(r.KC):
            total = total + r.conv_w[k : k + 1, :] * r.cpad[pl.ds(first + r.KC - 1 - k, count), :]
        r.xg[r.y, rows] = total.astype(BF16)

    def x_copy(i, slot, part):
        rows = pl.ds(part * (r.T // 2), r.T // 2)
        return line_copy(r, i, r.xg.at[slot, rows], r.xg.at[slot, rows], b.xg, slot, part)

    x_adj(0, r.T // 2)
    for i in far_first(r.nY):
        start(r, x_copy(i, r.y, 0))
    for part in range(2):
        for i in range(1, r.nY):
            relay_copy(r, i, lax.rem(r.y + i, r.nY), 1 - r.k, part).wait_recv()
    grad_part(r, 0)
    weight_line(r, r.dt_c, r.dt_d, r.dt_e, (b.d2, b.d3))
    pl.when(r.s < r.nS - 1)(lambda: head_copy(r.s + 1).wait_recv())
    x_adj(r.T // 2, r.T // 2)
    for i in far_first(r.nY):
        start(r, x_copy(i, r.y, 1))
    grad_part(r, 1)
    total = None
    for y2 in range(r.nY):
        pl.when(r.y != y2)(
            line_copy(r, 1, r.mi_c.at[y2], r.mi_c.at[y2], b.m2, y2).wait_recv
        )
        term = r.mi_c[y2].astype(F32)
        total = term if total is None else total + term
    r.mi_e[r.k] = total
    start(r, pair_copy(r, r.mi_e.at[r.k], r.mi_e.at[r.k], b.m3))
    weight_back(r, r.dt_e, b.d3, b.d4)
    for i in range(1, r.nY):
        y2 = lax.rem(r.y + i, r.nY)
        line_copy(r, i, r.ug.at[y2], r.ug.at[y2], b.ug, y2).wait_recv()
        line_copy(r, i, r.lg.at[y2], r.lg.at[y2], b.lg, y2).wait_recv()
        line_copy(r, i, r.bt.at[y2], r.bt.at[y2], b.bt, y2).wait_recv()
    tokens = r.nY * r.T
    term = contract_first(r.lg[...].reshape(tokens, r.R), r.ug[...].reshape(tokens, r.C))
    r.li_p[pl.ds(0, r.R), :] = term.astype(BF16)
    term = dot(r.bt[0], r.ug[0])
    for y2 in range(1, r.nY):
        term = term + dot(r.bt[y2], r.ug[y2])
    r.li_p[pl.ds(r.R, 2 * r.N), :] = term.astype(BF16)
    start(r, pair_copy(r, r.li_p, r.li_b, b.d5))
    def weight(x2, part):
        rows, count = pl.ds(part * (r.T // 2), r.T // 2), r.nY * r.T // 2
        left = r.hg[x2, :, rows].reshape(count, r.DH)
        return contract_first(left, r.xg[:, rows].reshape(count, r.C))

    def arrive(part):
        for i in range(1, r.nY):
            x_copy(i, lax.rem(r.y + i, r.nY), part).wait_recv()

    arrive(0)
    for j in range(r.nX):
        r.wl[j] = weight(j, 0)
    arrive(1)
    for j in range(half):
        x2 = (1 - r.k) * half + j
        r.ws[j] = (r.wl[x2] + weight(x2, 1)).astype(BF16)
    start(r, pair_copy(r, r.ws, r.wr, b.wg))
    for j in range(half):
        x2 = r.k * half + j
        r.wo[j] = r.wl[x2] + weight(x2, 1)
    pair_copy(r, r.ws, r.wr, b.wg).wait_recv()
    r.w_out[...] = (r.wo[...] + r.wr[...].astype(F32)).astype(BF16)
    flush(r)
    weight_end(r, r.dt_e, b.d4)
    pair_copy(r, r.mi_e.at[r.k], r.mi_e.at[1 - r.k], b.m3).wait_recv()
    total = r.hs[0].astype(F32)
    for i, c2, dev in peers(r, b.chan):
        for part in range(2):
            rows, at = pl.ds(part * (r.T // 2), r.T // 2), part * r.nC + c2
            got = r.hr.at[c2, rows]
            rcopy(got, got, r.sems[b.hg_s].at[i], r.sems[b.hg_r].at[at], *dev).wait_recv()
        total = total + r.hr[c2].astype(F32)
    r.hidden_out[...] = total.astype(BF16)
    pair_copy(r, r.li_p, r.li_b, b.d5).wait_recv()
    r.li_e[...] = (r.li_p[...].astype(F32) + r.li_b[...].astype(F32)).astype(BF16)
    flush(r)


def finish(r):
    scale = 1.0 / math.sqrt(r.T * r.nS)
    wide_half = r.C // 2
    r.hidden_grad[...] = r.hidden_out[...]
    r.gate_grad[...] = r.gate_out[...]
    r.w_in_grad[...] = r.w_out[...].astype(F32) * scale
    r.w_dt_grad[...] = r.dt_e[...].astype(F32).reshape(r.R, r.C) * scale
    r.w_delta_in_grad[...] = r.li_e[pl.ds(0, r.R), :].astype(F32) * scale
    r.w_bc_grad[...] = r.li_e[pl.ds(r.R, 2 * r.N), :].astype(F32) * scale
    for j in range(2):
        cols = pl.ds(j * wide_half, wide_half)
        r.a_log_grad[:, cols] = r.mi_e[j] * scale


def tables(dim):
    d = types.SimpleNamespace(**dim)
    t, c, n, rows, q = d.T, d.C, d.N, d.R, d.R // d.nS
    buffers = dict(
        hg=((d.nX, d.nY, t, d.DH), BF16),
        wf=((d.nY, d.nX, d.DH, c), BF16),
        xs=((d.nY, t, c), BF16),
        xr=((d.nY, t, c), BF16),
        xt=((d.nY, HALO, c), BF16),
        xpad=((HALO + t, c), F32),
        slope=((t, c), F32),
        gs=((t, c), F32),
        u=((t, c), BF16),
        part=((d.nC, d.PR, LANES), BF16),
        part_r=((d.nC, d.PR, LANES), BF16),
        part_a=((d.nC, d.PR, LANES), BF16),
        pad=((t, LANES), F32),
        low=((t, rows), BF16),
        bcw=((t, LANES), F32),
        pre=((t, c), F32),
        delta=((t, c), F32),
        du=((t, c), F32),
        g=((t, c), F32),
        am=((n, c), F32),
        bx=((t, n, LANES), F32),
        cx=((t, n, LANES), F32),
        sd=((1, c), F32),
        aa=((t * n, c), F32),
        hh=(((t + 1) * n, c), F32),
        hb=((t * n, c), BF16),
        sp=((t, c), F32),
        ef=((2, n, c), BF16),
        st_r=((d.nS, n, c), BF16),
        sd_r=((d.nS, 1, c), F32),
        kept0=((CH * n, c), BF16),
        kept1=((CH * n, c), BF16),
        kept2=((CH * n, c), BF16),
        kept3=((CH * n, c), BF16),
        h_in=((n, c), F32),
        l_in=((n, c), F32),
        bd=((t, CH * n), BF16),
        cd=((t, CH * n), BF16),
        bm=((t, CH * n), F32),
        cm=((t, CH * n), F32),
        y_scan=((t, c), F32),
        s1=((t, c), F32),
        s2=((t, c), F32),
        uu=((t, c), F32),
        part2=((d.nC, d.PR, LANES), BF16),
        part2_r=((d.nC, d.PR, LANES), BF16),
        part2_a=((d.nC, d.PR, LANES), BF16),
        dt_p=((2, d.nY, q, c), BF16),
        dt_b=((d.nY, q, c), BF16),
        dt_c=((d.nY, q, c), BF16),
        dt_d=((d.nY, q, c), BF16),
        dt_e=((2, d.nY, q, c), BF16),
        ug=((d.nY, t, c), BF16),
        lg=((d.nY, t, rows), BF16),
        bt=((d.nY, 2 * n, t), BF16),
        li_p=((rows + 2 * n, c), BF16),
        li_b=((rows + 2 * n, c), BF16),
        li_e=((rows + 2 * n, c), BF16),
        mi_p=((2, n, c // 2), BF16),
        mi_b=((n, c // 2), BF16),
        mi_c=((d.nY, n, c // 2), BF16),
        mi_e=((2, n, c // 2), F32),
        cpad=((t + HEAD, c), F32),
        xg=((d.nY, t, c), BF16),
        hs=((d.nC, t, d.DH), BF16),
        hr=((d.nC, t, d.DH), BF16),
        ws=((d.nX // 2, d.DH, c), BF16),
        wr=((d.nX // 2, d.DH, c), BF16),
        wo=((d.nX // 2, d.DH, c), F32),
        wl=((d.nX, d.DH, c), F32),
        w_out=((d.nX // 2, d.DH, c), BF16),
        hidden_out=((t, d.DH), BF16),
        gate_out=((t, c), BF16),
        hidden_grad=((t, d.DH), BF16),
        gate_grad=((t, c), BF16),
        w_in_grad=((d.nX // 2, d.DH, c), F32),
        w_delta_in_grad=((rows, c), F32),
        w_bc_grad=((2 * n, c), F32),
        w_dt_grad=((rows, c), F32),
        a_log_grad=((n, c), F32),
    )
    sems = dict(loc=2, inp=12)
    pairs = (b.tu, b.wp, b.head, b.wg, b.d1, b.d4, b.d5, b.m1, b.m3)
    lines = (b.xr, b.tail, b.d2, b.d3, b.m2, b.ug, b.lg, b.bt)
    for key in pairs:
        sems[key + "_s"] = sems[key + "_r"] = 1
    for key in lines:
        sems[key + "_s"] = sems[key + "_r"] = d.nY
    for key in (b.xg, b.wy, b.wz):
        sems[key + "_s"] = sems[key + "_r"] = 2 * d.nY
    sems[b.hg_s] = sems[b.hg_r] = 2 * d.nC
    for key in (b.g1, b.g2):
        sems[key + "_s"] = sems[key + "_r"] = d.nX + d.nY
    for key in (b.p1, b.p2, b.p3, b.p4):
        sems[key + "_s"] = sems[key + "_r"] = d.nC
    for key in (b.st, b.sd):
        sems[key + "_s"] = sems[key + "_r"] = d.nS
    return buffers, sems


def run(dim, phases, remote, values, ins, outs, scratch, sem_names, cost):
    buffers, sem_sizes = tables(dim)
    held = [name for name in ins if name not in (b.hidden, b.w_in)] if remote else []

    def body(*refs):
        r = types.SimpleNamespace(**dim)
        r.sent = []
        names = ins + outs + scratch
        for name, ref in zip(names, refs):
            setattr(r, name, ref)
        refs = refs[len(names) :]
        r.sems = dict(zip(sem_names, refs))
        if remote:
            r.given = {name: getattr(r, name) for name in ins}
            for name, ref in zip(held, refs[len(sem_names) :]):
                setattr(r, name, ref)
            r.s, r.c = lax.axis_index(b.seq), lax.axis_index(b.chan)
            r.y, r.k = lax.div(r.s, 2), lax.rem(r.s, 2)
            r.z, r.x = lax.div(r.c, r.nX), lax.rem(r.c, r.nX)
            greet(r, functools.partial(load, r))
        for phase in phases:
            phase(r)

    space = pl.BlockSpec(memory_space=pltpu.VMEM)
    extra = dict(collective_id=0, has_side_effects=True) if remote else {}
    results = pl.pallas_call(
        body,
        out_shape=[jax.ShapeDtypeStruct(*buffers[name]) for name in outs],
        in_specs=[pl.BlockSpec(memory_space=pl.ANY) if remote else space] * len(ins),
        out_specs=[space] * len(outs),
        scratch_shapes=[pltpu.VMEM(*buffers[name]) for name in scratch]
        + [pltpu.SemaphoreType.DMA((sem_sizes[name],)) for name in sem_names]
        + [pltpu.VMEM(values[name].shape, values[name].dtype) for name in held],
        compiler_params=pltpu.CompilerParams(vmem_limit_bytes=56 << 20, **extra),
        cost_estimate=pl.CostEstimate(flops=cost, bytes_accessed=4 << 20, transcendentals=0),
        name=phases[-1].__name__,
    )(*[values[name] for name in ins])
    values.update(zip(outs, results))


ORDER = [b.hidden_grad, b.gate_grad, b.w_in_grad, b.w_delta_in_grad, b.w_bc_grad, b.w_dt_grad, b.a_log_grad]


def per_device(
    seq, chan, hidden, gate_in, out_grad, w_in, conv_w, conv_b, w_delta_in, w_bc, w_dt, dt_bias, a_log, skip_d
):
    lines = seq // 2
    dim = dict(
        nS=seq,
        nC=chan,
        nY=lines,
        nX=chan // lines,
        T=hidden.shape[0],
        DH=hidden.shape[1],
        C=w_in.shape[1],
        R=w_delta_in.shape[0],
        N=a_log.shape[0],
        KC=conv_w.shape[0],
        RP=hidden.shape[0] // chan,
        PR=-(-(hidden.shape[0] // chan) * (w_delta_in.shape[0] // LANES + 1) // 16) * 16,
    )
    v = dict(
        hidden=hidden,
        gate_in=gate_in,
        out_grad=out_grad,
        w_in=w_in.reshape(dim[b.nX] // 2, dim[b.DH], dim[b.C]),
        conv_w=conv_w,
        conv_b=conv_b[None],
        w_delta_in=w_delta_in,
        w_bc=w_bc,
        w_dt=w_dt,
        dt_bias=dt_bias[None],
        a_log=a_log,
        skip_d=skip_d[None],
    )
    raw = [b.hidden_out, b.gate_out, b.w_out, b.dt_e, b.li_e, b.mi_e]
    given = list(v)
    buffers, sems = tables(dim)
    scratch = [name for name in buffers if name not in given + raw + ORDER]
    phases = [take_hidden, project, prepare, scan, gradients]
    run(dim, phases, True, v, given, raw, scratch, list(sems), 2_000_000_000)
    run(dim, [finish], False, v, raw, ORDER, [], [], 1_000_000)
    v[b.w_in_grad] = v[b.w_in_grad].reshape(w_in.shape)
    return tuple(v[name] for name in ORDER)


def solution(mesh):
    placed = (
        P(b.seq, b.chan),
        P(b.seq, b.chan),
        P(b.seq, b.chan),
        P(b.seq, b.chan),
        P(None, b.chan),
        P(b.chan),
        P(None, b.chan),
        P(None, b.chan),
        P(None, b.chan),
        P(b.chan),
        P(None, b.chan),
        P(b.chan),
    )
    return jax.shard_map(
        functools.partial(per_device, mesh.shape[b.seq], mesh.shape[b.chan]),
        mesh=mesh,
        in_specs=placed,
        out_specs=(
            P(b.seq, b.chan),
            P(b.seq, b.chan),
            P(b.seq, b.chan),
            P(None, b.chan),
            P(None, b.chan),
            P(None, b.chan),
            P(None, b.chan),
        ),
        check_vma=False,
    )
```
